32 devices in a mesh: tab: 8 (over z, y), row: 4 (over x, core).
Axes of the slice: x: 2, y: 2, z: 4, core: 2. Of those that a mesh axis runs over, the one named last changes fastest.
Arguments:
- table_cells: bfloat16 [8, 1024, 12, 512], P('tab', 'row'), may hold values from -6 to 6
- cotangent: bfloat16 [8, 1024, 12, 512], P('tab', 'row'), may hold values from -6 to 6
- row_counts: int32 [8], P('tab'), may hold values from 769 to 1024, as said below
- context_counts: int32 [8], P('tab'), may hold values from 128 to 1024, as said below
- feat_gain: float32 [512], replicated, may hold values from 0.5 to 1.5
- feat_shift: float32 [512], replicated, may hold values from -1.5 to 1.5
- feat_query: bfloat16 [512, 512], replicated, may hold values from -0.25 to 0.25
- feat_key: bfloat16 [512, 512], replicated, may hold values from -0.25 to 0.25
- feat_value: bfloat16 [512, 512], replicated, may hold values from -0.25 to 0.25
- feat_out: bfloat16 [512, 512], replicated, may hold values from -0.375 to 0.375
- feat_bias: float32 [512], replicated, may hold values from -1.5 to 1.5
- row_gain: float32 [512], replicated, may hold values from 0.5 to 1.5
- row_shift: float32 [512], replicated, may hold values from -1.5 to 1.5
- row_query: bfloat16 [512, 512], replicated, may hold values from -0.25 to 0.25
- row_key: bfloat16 [512, 512], replicated, may hold values from -0.25 to 0.25
- row_value: bfloat16 [512, 512], replicated, may hold values from -0.25 to 0.25
- row_out: bfloat16 [512, 512], replicated, may hold values from -4 to 4
- row_bias: float32 [512], replicated, may hold values from -1.5 to 1.5
- mlp_gain: float32 [512], replicated, may hold values from 0.5 to 1.5
- mlp_shift: float32 [512], replicated, may hold values from -1.5 to 1.5
- up_weight: bfloat16 [512, 2048], replicated, may hold values from -0.25 to 0.25
- up_bias: float32 [2048], replicated, may hold values from -1.5 to 1.5
- down_weight: bfloat16 [2048, 512], replicated, may hold values from -0.125 to 0.125
- down_bias: float32 [512], replicated, may hold values from -1.5 to 1.5
Outputs:
- layer_out: bfloat16 [8, 1024, 12, 512], P('tab', 'row')
- cells_grad: bfloat16 [8, 1024, 12, 512], P('tab', 'row')
- feat_gain_grad: float32 [512], P('row')
- feat_shift_grad: float32 [512], P('row')
- feat_query_grad: float32 [512, 512], P('row')
- feat_key_grad: float32 [512, 512], P('row')
- feat_value_grad: float32 [512, 512], P('row')
- feat_out_grad: float32 [512, 512], P('row')
- feat_bias_grad: float32 [512], P('row')
- row_gain_grad: float32 [512], P('row')
- row_shift_grad: float32 [512], P('row')
- row_query_grad: float32 [512, 512], P('row')
- row_key_grad: float32 [512, 512], P('row')
- row_value_grad: float32 [512, 512], P('row')
- row_out_grad: float32 [512, 512], P('row')
- row_bias_grad: float32 [512], P('row')
- mlp_gain_grad: float32 [512], P('row')
- mlp_shift_grad: float32 [512], P('row')
- up_weight_grad: float32 [512, 2048], P('row')
- up_bias_grad: float32 [2048], P('row')
- down_weight_grad: float32 [2048, 512], P('row')
- down_bias_grad: float32 [512], P('row')
The draws below stay inside these ranges and needn't reach their ends.
Inputs may be any that keep to these rules, and one draw needn't show every extreme that they name: Rows 0 to row_counts[t] - 1 of table t hold data, the rest is padding; some table fills all 1024 rows. Rows 0 to context_counts[t] - 1 of table t are its context; context_counts[t] <= row_counts[t]; some table's context is all 1024 rows.
All inputs are finite; a program needn't handle non-finite values.
Results may differ from the reference program's by a relative error of at most 0.024.
Values may be sent and summed in bfloat16 or wider, within the bound.
No kernel may reach another device: no remote copies, remote signals or barrier semaphores. Data moves between devices by JAX's collectives and lax.ppermute only.
A program may use at most 512 MiB of HBM per device.

```python
import math
import jax
import jax.numpy as jnp
from jax import lax

D = 512
HEADS = 4
FF = 2048
FEAT = 12
ROWS = 1024
TABLES = 8
N_ROW = 4


def table_counts(key):
    order_key, rows_key, share_key = jax.random.split(key, 3)
    order = jax.random.permutation(order_key, TABLES)
    least = ROWS - ROWS // N_ROW + 1
    lowest = ROWS // 8
    row_part = jax.random.randint(rows_key, (TABLES,), least, ROWS + 1)
    row_part = row_part.at[order[0]].set(ROWS).at[order[1]].set(least)
    share = jax.random.randint(share_key, (TABLES,), 0, 1 << 20)
    context_part = lowest + share % (row_part - lowest + 1)
    context_part = context_part.at[order[0]].set(ROWS).at[order[1]].set(lowest)
    return (row_part.astype(jnp.int32), context_part.astype(jnp.int32))


def draw_row_counts(key, part):
    shared = table_counts(key)
    return shared[0]


def draw_context_counts(key, part):
    shared = table_counts(key)
    return shared[1]


def block_scale(key, shape, shards, low, high):
    loudness, own = 1.0, jax.random.fold_in(key, 6)
    for dim, shards_of in shards:
        heights = jnp.exp(jax.random.uniform(jax.random.fold_in(own, dim), (shards_of,), jnp.float32, low / len(shards), high / len(shards)))
        loudness = loudness * jnp.repeat(heights, shape[dim] // shards_of).reshape([-1 if axis == dim else 1 for axis in range(len(shape))])
    return loudness


def noise(rng, extent, scale, most, cuts=(), held_as=jnp.bfloat16):
    drawn = scale * jax.random.normal(rng, extent, jnp.float32)
    if cuts:
        drawn = drawn * block_scale(rng, extent, cuts, -0.22, 0.18)
    return jnp.clip(drawn, -most, most).astype(held_as)


def setup_inputs(seed: int = 0) -> dict:
    key_of = jax.random.split(jax.random.key(seed), 25)
    return {
        "table_cells": noise(key_of[0], (TABLES, ROWS, FEAT, D), 1.0, 6.0, ((0, 8), (1, 4))),
        "cotangent": noise(key_of[1], (TABLES, ROWS, FEAT, D), 1.0, 6.0, ((0, 8), (1, 4))),
        "row_counts": draw_row_counts(jax.random.fold_in(key_of[24], 71), 0),
        "context_counts": draw_context_counts(jax.random.fold_in(key_of[24], 71), 0),
        "feat_gain": jnp.clip(1.0 + 0.1 * jax.random.normal(key_of[4], (D,), jnp.float32), 0.5, 1.5),
        "feat_shift": noise(key_of[5], (D,), 0.3, 1.5, (), jnp.float32),
        "feat_query": noise(key_of[6], (D, D), D ** -0.5, 0.25),
        "feat_key": noise(key_of[7], (D, D), D ** -0.5, 0.25),
        "feat_value": noise(key_of[8], (D, D), D ** -0.5, 0.25),
        "feat_out": noise(key_of[9], (D, D), (D // 2) ** -0.5, 0.375),
        "feat_bias": noise(key_of[10], (D,), 0.3, 1.5, (), jnp.float32),
        "row_gain": jnp.clip(1.0 + 0.1 * jax.random.normal(key_of[11], (D,), jnp.float32), 0.5, 1.5),
        "row_shift": noise(key_of[12], (D,), 0.3, 1.5, (), jnp.float32),
        "row_query": noise(key_of[13], (D, D), D ** -0.5, 0.25),
        "row_key": noise(key_of[14], (D, D), D ** -0.5, 0.25),
        "row_value": noise(key_of[15], (D, D), D ** -0.5, 0.25),
        "row_out": noise(key_of[16], (D, D), (max(1, 4 * D // ROWS)) ** -0.5, 4.0),
        "row_bias": noise(key_of[17], (D,), 0.3, 1.5, (), jnp.float32),
        "mlp_gain": jnp.clip(1.0 + 0.1 * jax.random.normal(key_of[18], (D,), jnp.float32), 0.5, 1.5),
        "mlp_shift": noise(key_of[19], (D,), 0.3, 1.5, (), jnp.float32),
        "up_weight": noise(key_of[20], (D, FF), D ** -0.5, 0.25),
        "up_bias": noise(key_of[21], (FF,), 0.3, 1.5, (), jnp.float32),
        "down_weight": noise(key_of[22], (FF, D), FF ** -0.5, 0.125),
        "down_bias": noise(key_of[23], (D,), 0.3, 1.5, (), jnp.float32),
    }


HIGHEST = lax.Precision.HIGHEST
EPSILON = 1e-05
NEGATIVE = -1e+30

@jax.custom_vjp
def low(v):
    return lax.optimization_barrier(v.astype(jnp.bfloat16)).astype(jnp.float32)

@jax.custom_vjp
def low_back(v):
    return v

def low_keep(v):
    return (low(v), None)

def low_pass(kept, grad):
    return (grad,)

def back_keep(v):
    return (v, None)

def back_low(kept, grad):
    return (low(grad),)
low.defvjp(low_keep, low_pass)
low_back.defvjp(back_keep, back_low)

def rounded(values):
    return low_back(low(values))

def normalize(values, gain_vec, shift_vec):
    row_mean = lax.optimization_barrier(jnp.mean(values, -1, keepdims=True))
    centred = values - row_mean
    spread_sq = lax.optimization_barrier(jnp.mean(centred * centred, -1, keepdims=True))
    return centred * lax.rsqrt(spread_sq + EPSILON) * gain_vec + shift_vec

def matmul_high(left_side, right_side):
    return jnp.matmul(left_side, right_side, precision=HIGHEST)

def table_layer(table_cells, row_count, context_count, params):
    feat_gain, feat_shift, feat_query, feat_key, feat_value, feat_out, feat_bias, row_gain, row_shift, row_query, row_key, row_value, row_out, row_bias, mlp_gain, mlp_shift, up_weight, up_bias, down_weight, down_bias = params
    row_total, feat_count, model_width = table_cells.shape
    head_size = model_width // HEADS
    score_scale = 1.0 / math.sqrt(head_size)
    split_shape = (row_total, feat_count, HEADS, head_size)
    normed_a = low(normalize(table_cells, feat_gain, feat_shift))
    query_a = rounded(matmul_high(normed_a, feat_query)).reshape(split_shape)
    key_a = rounded(matmul_high(normed_a, feat_key)).reshape(split_shape)
    value_a = rounded(matmul_high(normed_a, feat_value)).reshape(split_shape)
    scores_a = low_back(jnp.einsum('rfhd,rghd->rhfg', query_a, key_a, precision=HIGHEST) * score_scale)
    probs_a = low(jax.nn.softmax(scores_a, -1))
    mixed_a = rounded(jnp.einsum('rhfg,rghd->rfhd', probs_a, value_a, precision=HIGHEST))
    mixed_a = mixed_a.reshape(row_total, feat_count, model_width)
    after_a = table_cells + low_back(matmul_high(mixed_a, feat_out)) + feat_bias
    normed_b = low(normalize(after_a, row_gain, row_shift))
    query_b = rounded(matmul_high(normed_b, row_query)).reshape(split_shape).transpose(1, 0, 2, 3)
    key_b = rounded(matmul_high(normed_b, row_key)).reshape(split_shape).transpose(1, 0, 2, 3)
    value_b = rounded(matmul_high(normed_b, row_value)).reshape(split_shape).transpose(1, 0, 2, 3)
    context_mask = jnp.arange(row_total) < context_count

    @jax.checkpoint
    def one_feature(operands):
        query_rows, key_rows, value_rows = operands
        raw_scores = low_back(jnp.einsum('ihd,jhd->hij', query_rows, key_rows, precision=HIGHEST) * score_scale)
        raw_scores = jnp.where(context_mask, raw_scores, NEGATIVE)
        weights = low(jax.nn.softmax(raw_scores, -1))
        return rounded(jnp.einsum('hij,jhd->ihd', weights, value_rows, precision=HIGHEST))
    mixed_b = lax.map(one_feature, (query_b, key_b, value_b)).transpose(1, 0, 2, 3)
    mixed_b = mixed_b.reshape(row_total, feat_count, model_width)
    after_b = after_a + low_back(matmul_high(mixed_b, row_out)) + row_bias
    normed_c = low(normalize(after_b, mlp_gain, mlp_shift))
    hidden = low_back(matmul_high(normed_c, up_weight) + up_bias)
    active = low(jax.nn.gelu(hidden))
    after_c = after_b + low_back(matmul_high(active, down_weight)) + down_bias
    row_mask = (jnp.arange(row_total) < row_count).astype(after_c.dtype)[:, None, None]
    return after_c * row_mask

def reference(table_cells, cotangent, row_counts, context_counts, feat_gain, feat_shift, feat_query, feat_key, feat_value, feat_out, feat_bias, row_gain, row_shift, row_query, row_key, row_value, row_out, row_bias, mlp_gain, mlp_shift, up_weight, up_bias, down_weight, down_bias):
    params = tuple((weight.astype(jnp.float32) for weight in (feat_gain, feat_shift, feat_query, feat_key, feat_value, feat_out, feat_bias, row_gain, row_shift, row_query, row_key, row_value, row_out, row_bias, mlp_gain, mlp_shift, up_weight, up_bias, down_weight, down_bias)))

    def one_table(running, table_item):
        cells_now, upstream, row_count, context_count = table_item

        def forward(cells_in, param_set):
            return table_layer(cells_in, row_count, context_count, param_set)
        result, pullback = jax.vjp(forward, cells_now.astype(jnp.float32), params)
        cell_grad, param_grads = pullback(upstream.astype(jnp.float32))
        running = jax.tree.map(jnp.add, running, param_grads)
        return (running, (result.astype(jnp.bfloat16), cell_grad.astype(jnp.bfloat16)))
    zero_grads = tuple((jnp.zeros_like(weight) for weight in params))
    totals, outputs = lax.scan(one_table, zero_grads, (table_cells, cotangent, row_counts, context_counts))
    layer_out, cells_grad = outputs
    return (layer_out, cells_grad, totals[0], totals[1], totals[2], totals[3], totals[4], totals[5], totals[6], totals[7], totals[8], totals[9], totals[10], totals[11], totals[12], totals[13], totals[14], totals[15], totals[16], totals[17], totals[18], totals[19])
```

```python
import functools
import math

import jax
import jax.numpy as jnp
from jax import lax
from jax.experimental import pallas as pl
from jax.experimental.pallas import tpu as pltpu
from jax.sharding import PartitionSpec as P

HEADS = 4


EPSILON = 1e-05
NEGATIVE = -1e30


def normalize(values, gain_vec, shift_vec):
    row_mean = jnp.mean(values, -1, keepdims=True)
    centred = values - row_mean
    inverse = lax.rsqrt(jnp.mean(centred * centred, -1, keepdims=True) + EPSILON)
    unit_part = centred * inverse
    return (unit_part * gain_vec + shift_vec, unit_part, inverse)


def normalize_back(upstream, unit_part, inverse, gain_vec):
    scaled = upstream * gain_vec
    inner_part = (
        scaled
        - jnp.mean(scaled, -1, keepdims=True)
        - unit_part * jnp.mean(scaled * unit_part, -1, keepdims=True)
    )
    return (
        inverse * inner_part,
        jnp.sum(upstream * unit_part, axis=(0, 1)),
        jnp.sum(upstream, axis=(0, 1)),
    )


def project(left_side, weight):
    return jnp.einsum("rfd,de->rfe", left_side, weight, preferred_element_type=jnp.float32)


def project_back(upstream, weight):
    return jnp.einsum("rfe,de->rfd", upstream, weight, preferred_element_type=jnp.float32)


def outer_sum(left_side, upstream):
    return jnp.einsum("rfd,rfe->de", left_side, upstream, preferred_element_type=jnp.float32)


def split_heads(values):
    return values.reshape(values.shape[0], values.shape[1], HEADS, values.shape[2] // HEADS)


def join_heads(values):
    return values.reshape(values.shape[0], values.shape[1], values.shape[2] * values.shape[3])


def shards(
    table_cells,
    cotangent,
    row_counts,
    context_counts,
    feat_gain,
    feat_shift,
    feat_query,
    feat_key,
    feat_value,
    feat_out,
    feat_bias,
    row_gain,
    row_shift,
    row_query,
    row_key,
    row_value,
    row_out,
    row_bias,
    mlp_gain,
    mlp_shift,
    up_weight,
    up_bias,
    down_weight,
    down_bias,
):
    source = table_cells[0].astype(jnp.float32)
    local_rows, feat_count, model_width = source.shape
    score_scale = 1.0 / math.sqrt(model_width // HEADS)
    total_rows = local_rows * lax.axis_size("row")
    row_ids = lax.axis_index("row") * local_rows + jnp.arange(local_rows, dtype=jnp.int32)
    row_mask = (row_ids < row_counts[0]).astype(jnp.float32)[:, None, None]
    context_mask = jnp.arange(total_rows, dtype=jnp.int32) < context_counts[0]
    normed_a, unit_a, inverse_a = normalize(source, feat_gain, feat_shift)
    normed_a = normed_a.astype(jnp.bfloat16)
    query_a = split_heads(project(normed_a, feat_query).astype(jnp.bfloat16))
    key_a = split_heads(project(normed_a, feat_key).astype(jnp.bfloat16))
    value_a = split_heads(project(normed_a, feat_value).astype(jnp.bfloat16))
    scores_a = (
        jnp.einsum("rfhd,rghd->rhfg", query_a, key_a, preferred_element_type=jnp.float32)
        * score_scale
    )
    probs_a = jax.nn.softmax(scores_a, -1)
    probs_a_low = probs_a.astype(jnp.bfloat16)
    mixed_a = join_heads(
        jnp.einsum(
            "rhfg,rghd->rfhd", probs_a_low, value_a, preferred_element_type=jnp.float32
        ).astype(jnp.bfloat16)
    )
    after_a = source + project(mixed_a, feat_out) + feat_bias
    normed_b, unit_b, inverse_b = normalize(after_a, row_gain, row_shift)
    normed_b = normed_b.astype(jnp.bfloat16)
    query_b = split_heads(project(normed_b, row_query).astype(jnp.bfloat16))
    key_b = project(normed_b, row_key).astype(jnp.bfloat16)
    value_b = project(normed_b, row_value).astype(jnp.bfloat16)
    key_all, value_all = (
        lax.all_gather(key_b, "row", axis=0, tiled=True),
        lax.all_gather(value_b, "row", axis=0, tiled=True),
    )

    def row_scores(key_whole):
        raw_scores = (
            jnp.einsum(
                "ifhd,jfhd->fhij",
                query_b,
                split_heads(key_whole),
                preferred_element_type=jnp.float32,
            )
            * score_scale
        )
        return jnp.where(context_mask, raw_scores, NEGATIVE)

    scores_b = row_scores(key_all)
    highest = jnp.max(scores_b, -1, keepdims=True)
    log_total = highest + jnp.log(jnp.sum(jnp.exp(scores_b - highest), -1, keepdims=True))
    probs_b_low = jnp.exp(scores_b - log_total).astype(jnp.bfloat16)
    mixed_b = join_heads(
        jnp.einsum(
            "fhij,jfhd->ifhd",
            probs_b_low,
            split_heads(value_all),
            preferred_element_type=jnp.float32,
        ).astype(jnp.bfloat16)
    )
    after_b = after_a + project(mixed_b, row_out) + row_bias
    normed_c, unit_c, inverse_c = normalize(after_b, mlp_gain, mlp_shift)
    normed_c = normed_c.astype(jnp.bfloat16)
    hidden = project(normed_c, up_weight) + up_bias
    active, gelu_pull = jax.vjp(jax.nn.gelu, hidden)
    active = active.astype(jnp.bfloat16)
    after_c = after_b + project(active, down_weight) + down_bias
    layer_out = (after_c * row_mask).astype(jnp.bfloat16)
    grad_c = cotangent[0].astype(jnp.float32) * row_mask
    grad_c_low = grad_c.astype(jnp.bfloat16)
    down_bias_grad = jnp.sum(grad_c, axis=(0, 1))
    down_weight_grad = outer_sum(active, grad_c_low)
    active_grad = project_back(grad_c_low, down_weight)
    hidden_grad = gelu_pull(active_grad)[0].astype(jnp.bfloat16)
    up_bias_grad = jnp.sum(hidden_grad.astype(jnp.float32), axis=(0, 1))
    up_weight_grad = outer_sum(normed_c, hidden_grad)
    back_c, mlp_gain_grad, mlp_shift_grad = normalize_back(
        project_back(hidden_grad, up_weight), unit_c, inverse_c, mlp_gain
    )
    grad_b = grad_c + back_c
    grad_b_low = grad_b.astype(jnp.bfloat16)
    row_bias_grad = jnp.sum(grad_b, axis=(0, 1))
    row_out_grad = outer_sum(mixed_b, grad_b_low)
    mixed_b_grad = split_heads(project_back(grad_b_low, row_out).astype(jnp.bfloat16))
    key_back, value_back = (
        lax.all_gather(key_b, "row", axis=0, tiled=True),
        lax.all_gather(value_b, "row", axis=0, tiled=True),
    )
    probs_full = jnp.exp(row_scores(key_back) - log_total)
    probs_grad = jnp.einsum(
        "ifhd,jfhd->fhij", mixed_b_grad, split_heads(value_back), preferred_element_type=jnp.float32
    )
    row_dot = jnp.sum(probs_full * probs_grad, -1, keepdims=True)
    score_b_grad = (probs_full * (probs_grad - row_dot)).astype(jnp.bfloat16)
    query_b_grad = join_heads(
        (
            jnp.einsum(
                "fhij,jfhd->ifhd",
                score_b_grad,
                split_heads(key_back),
                preferred_element_type=jnp.float32,
            )
            * score_scale
        ).astype(jnp.bfloat16)
    )
    flat_rows = feat_count * HEADS
    log_all, dot_all = (
        lax.all_gather(log_total.reshape(flat_rows, local_rows), "row", axis=1, tiled=True),
        lax.all_gather(row_dot.reshape(flat_rows, local_rows), "row", axis=1, tiled=True),
    )
    own_mask = row_ids < context_counts[0]
    key_own = split_heads(key_b)
    value_own = split_heads(value_b)
    query_piece = lax.all_gather(query_b, "row", axis=0, tiled=True)
    grad_piece = lax.all_gather(mixed_b_grad, "row", axis=0, tiled=True)
    count = query_piece.shape[0]
    log_piece = log_all.reshape(feat_count, HEADS, count, 1)
    dot_piece = dot_all.reshape(feat_count, HEADS, count, 1)
    piece_scores = (
        jnp.einsum("ifhd,jfhd->fhij", query_piece, key_own, preferred_element_type=jnp.float32)
        * score_scale
    )
    piece_scores = jnp.where(own_mask, piece_scores, NEGATIVE)
    piece_probs = jnp.exp(piece_scores - log_piece)
    piece_inner = jnp.einsum(
        "ifhd,jfhd->fhij", grad_piece, value_own, preferred_element_type=jnp.float32
    )
    piece_grad = (piece_probs * (piece_inner - dot_piece)).astype(jnp.bfloat16)
    key_total = (
        jnp.einsum("fhij,ifhd->jfhd", piece_grad, query_piece, preferred_element_type=jnp.float32)
        * score_scale
    )
    value_total = jnp.einsum(
        "fhij,ifhd->jfhd",
        piece_probs.astype(jnp.bfloat16),
        grad_piece,
        preferred_element_type=jnp.float32,
    )
    key_total, value_total = (key_total, value_total)
    key_b_grad = join_heads(key_total).astype(jnp.bfloat16)
    value_b_grad = join_heads(value_total).astype(jnp.bfloat16)
    row_query_grad = outer_sum(normed_b, query_b_grad)
    row_key_grad = outer_sum(normed_b, key_b_grad)
    row_value_grad = outer_sum(normed_b, value_b_grad)
    normed_b_grad = (
        project_back(query_b_grad, row_query)
        + project_back(key_b_grad, row_key)
        + project_back(value_b_grad, row_value)
    )
    back_b, row_gain_grad, row_shift_grad = normalize_back(
        normed_b_grad, unit_b, inverse_b, row_gain
    )
    grad_a = grad_b + back_b
    grad_a_low = grad_a.astype(jnp.bfloat16)
    feat_bias_grad = jnp.sum(grad_a, axis=(0, 1))
    feat_out_grad = outer_sum(mixed_a, grad_a_low)
    mixed_a_grad = split_heads(project_back(grad_a_low, feat_out).astype(jnp.bfloat16))
    probs_a_grad = jnp.einsum(
        "rfhd,rghd->rhfg", mixed_a_grad, value_a, preferred_element_type=jnp.float32
    )
    score_a_grad = (
        probs_a * (probs_a_grad - jnp.sum(probs_a * probs_a_grad, -1, keepdims=True))
    ).astype(jnp.bfloat16)
    query_a_grad = join_heads(
        (
            jnp.einsum("rhfg,rghd->rfhd", score_a_grad, key_a, preferred_element_type=jnp.float32)
            * score_scale
        ).astype(jnp.bfloat16)
    )
    key_a_grad = join_heads(
        (
            jnp.einsum("rhfg,rfhd->rghd", score_a_grad, query_a, preferred_element_type=jnp.float32)
            * score_scale
        ).astype(jnp.bfloat16)
    )
    value_a_grad = join_heads(
        jnp.einsum(
            "rhfg,rfhd->rghd", probs_a_low, mixed_a_grad, preferred_element_type=jnp.float32
        ).astype(jnp.bfloat16)
    )
    feat_query_grad = outer_sum(normed_a, query_a_grad)
    feat_key_grad = outer_sum(normed_a, key_a_grad)
    feat_value_grad = outer_sum(normed_a, value_a_grad)
    normed_a_grad = (
        project_back(query_a_grad, feat_query)
        + project_back(key_a_grad, feat_key)
        + project_back(value_a_grad, feat_value)
    )
    back_a, feat_gain_grad, feat_shift_grad = normalize_back(
        normed_a_grad, unit_a, inverse_a, feat_gain
    )
    cells_grad = (grad_a + back_a).astype(jnp.bfloat16)
    row_summed = (
        lax.psum_scatter(
            feat_gain_grad.astype(jnp.bfloat16), "row", scatter_dimension=0, tiled=True
        ).astype(jnp.float32),
        lax.psum_scatter(
            feat_shift_grad.astype(jnp.bfloat16), "row", scatter_dimension=0, tiled=True
        ).astype(jnp.float32),
        lax.psum_scatter(
            feat_query_grad.astype(jnp.bfloat16), "row", scatter_dimension=0, tiled=True
        ).astype(jnp.float32),
        lax.psum_scatter(
            feat_key_grad.astype(jnp.bfloat16), "row", scatter_dimension=0, tiled=True
        ).astype(jnp.float32),
        lax.psum_scatter(
            feat_value_grad.astype(jnp.bfloat16), "row", scatter_dimension=0, tiled=True
        ).astype(jnp.float32),
        lax.psum_scatter(
            feat_out_grad.astype(jnp.bfloat16), "row", scatter_dimension=0, tiled=True
        ).astype(jnp.float32),
        lax.psum_scatter(
            feat_bias_grad.astype(jnp.bfloat16), "row", scatter_dimension=0, tiled=True
        ).astype(jnp.float32),
        lax.psum_scatter(
            row_gain_grad.astype(jnp.bfloat16), "row", scatter_dimension=0, tiled=True
        ).astype(jnp.float32),
        lax.psum_scatter(
            row_shift_grad.astype(jnp.bfloat16), "row", scatter_dimension=0, tiled=True
        ).astype(jnp.float32),
        lax.psum_scatter(
            row_query_grad.astype(jnp.bfloat16), "row", scatter_dimension=0, tiled=True
        ).astype(jnp.float32),
        lax.psum_scatter(
            row_key_grad.astype(jnp.bfloat16), "row", scatter_dimension=0, tiled=True
        ).astype(jnp.float32),
        lax.psum_scatter(
            row_value_grad.astype(jnp.bfloat16), "row", scatter_dimension=0, tiled=True
        ).astype(jnp.float32),
        lax.psum_scatter(
            row_out_grad.astype(jnp.bfloat16), "row", scatter_dimension=0, tiled=True
        ).astype(jnp.float32),
        lax.psum_scatter(
            row_bias_grad.astype(jnp.bfloat16), "row", scatter_dimension=0, tiled=True
        ).astype(jnp.float32),
        lax.psum_scatter(
            mlp_gain_grad.astype(jnp.bfloat16), "row", scatter_dimension=0, tiled=True
        ).astype(jnp.float32),
        lax.psum_scatter(
            mlp_shift_grad.astype(jnp.bfloat16), "row", scatter_dimension=0, tiled=True
        ).astype(jnp.float32),
        lax.psum_scatter(
            up_weight_grad.astype(jnp.bfloat16), "row", scatter_dimension=0, tiled=True
        ).astype(jnp.float32),
        lax.psum_scatter(
            up_bias_grad.astype(jnp.bfloat16), "row", scatter_dimension=0, tiled=True
        ).astype(jnp.float32),
        lax.psum_scatter(
            down_weight_grad.astype(jnp.bfloat16), "row", scatter_dimension=0, tiled=True
        ).astype(jnp.float32),
        lax.psum_scatter(
            down_bias_grad.astype(jnp.bfloat16), "row", scatter_dimension=0, tiled=True
        ).astype(jnp.float32),
    )
    (
        part_fg,
        part_fs,
        part_fq,
        part_fk,
        part_fv,
        part_fo,
        part_fb,
        part_rg,
        part_rs,
        part_rq,
        part_rk,
        part_rv,
        part_ro,
        part_rb,
        part_mg,
        part_ms,
        part_uw,
        part_ub,
        part_dw,
        part_db,
    ) = row_summed
    summed = (
        lax.psum(part_fg.astype(jnp.bfloat16), "tab").astype(jnp.float32),
        lax.psum(part_fs.astype(jnp.bfloat16), "tab").astype(jnp.float32),
        lax.psum(part_fq.astype(jnp.bfloat16), "tab").astype(jnp.float32),
        lax.psum(part_fk.astype(jnp.bfloat16), "tab").astype(jnp.float32),
        lax.psum(part_fv.astype(jnp.bfloat16), "tab").astype(jnp.float32),
        lax.psum(part_fo.astype(jnp.bfloat16), "tab").astype(jnp.float32),
        lax.psum(part_fb.astype(jnp.bfloat16), "tab").astype(jnp.float32),
        lax.psum(part_rg.astype(jnp.bfloat16), "tab").astype(jnp.float32),
        lax.psum(part_rs.astype(jnp.bfloat16), "tab").astype(jnp.float32),
        lax.psum(part_rq.astype(jnp.bfloat16), "tab").astype(jnp.float32),
        lax.psum(part_rk.astype(jnp.bfloat16), "tab").astype(jnp.float32),
        lax.psum(part_rv.astype(jnp.bfloat16), "tab").astype(jnp.float32),
        lax.psum(part_ro.astype(jnp.bfloat16), "tab").astype(jnp.float32),
        lax.psum(part_rb.astype(jnp.bfloat16), "tab").astype(jnp.float32),
        lax.psum(part_mg.astype(jnp.bfloat16), "tab").astype(jnp.float32),
        lax.psum(part_ms.astype(jnp.bfloat16), "tab").astype(jnp.float32),
        lax.psum(part_uw.astype(jnp.bfloat16), "tab").astype(jnp.float32),
        lax.psum(part_ub.astype(jnp.bfloat16), "tab").astype(jnp.float32),
        lax.psum(part_dw.astype(jnp.bfloat16), "tab").astype(jnp.float32),
        lax.psum(part_db.astype(jnp.bfloat16), "tab").astype(jnp.float32),
    )
    return (
        layer_out[None],
        cells_grad[None],
        summed[0],
        summed[1],
        summed[2],
        summed[3],
        summed[4],
        summed[5],
        summed[6],
        summed[7],
        summed[8],
        summed[9],
        summed[10],
        summed[11],
        summed[12],
        summed[13],
        summed[14],
        summed[15],
        summed[16],
        summed[17],
        summed[18],
        summed[19],
    )


HEAD = 128
GROUP = 16
LOG2E = 1.4426950408889634
F32 = jnp.float32
BF16 = jnp.bfloat16


def dot_nn(a, b):
    return jnp.dot(a, b, preferred_element_type=F32)


def dot_nt(a, b):
    return lax.dot_general(a, b, (((1,), (1,)), ((), ())), preferred_element_type=F32)


def dot_tn(a, b):
    return lax.dot_general(a, b, (((0,), (0,)), ((), ())), preferred_element_type=F32)


def unit_of(values):
    centred = values - jnp.mean(values, -1, keepdims=True)
    inverse = lax.rsqrt(jnp.mean(centred * centred, -1, keepdims=True) + EPSILON)
    return centred * inverse, inverse


def norm_back(upstream, unit, inverse, gain):
    scaled = upstream * gain
    return inverse * (
        scaled
        - jnp.mean(scaled, -1, keepdims=True)
        - unit * jnp.mean(scaled * unit, -1, keepdims=True)
    )


def column_sum(values):
    return jnp.sum(values, 0, keepdims=True)


def vmem_spec():
    return pl.BlockSpec(memory_space=pltpu.VMEM)


def smem_spec():
    return pl.BlockSpec(memory_space=pltpu.SMEM)


def params_of(mib=56):
    return pltpu.CompilerParams(vmem_limit_bytes=mib * 1024 * 1024)


def piece_feature(me, index, group):
    return (me ^ (index // group)) * group + index % group


def fill_order(order_ref, me, feats, group):
    rows = lax.broadcasted_iota(jnp.int32, (GROUP, GROUP * GROUP), 0)
    cols = lax.broadcasted_iota(jnp.int32, (GROUP, GROUP * GROUP), 1)
    for index in range(feats):
        hit = cols == rows * GROUP + piece_feature(me, index, group)
        order_ref[index * GROUP : (index + 1) * GROUP, :] = jnp.where(hit, 1.0, 0.0).astype(BF16)


def same_row(size):
    rows = lax.broadcasted_iota(jnp.int32, (size, size), 0)
    cols = lax.broadcasted_iota(jnp.int32, (size, size), 1)
    return (rows % GROUP) == (cols % GROUP)


def to_pieces_kernel(group, me_ref, cells_ref, *rest):
    feats = cells_ref.shape[2]
    outs, (padded, order) = rest[:feats], rest[feats:]
    rows = cells_ref.shape[1]

    @pl.when(pl.program_id(0) == 0)
    def _():
        fill_order(order, me_ref[0], feats, group)
        padded[...] = jnp.zeros_like(padded)

    padded[:, :feats, :] = cells_ref[0]
    width = cells_ref.shape[3]
    flat = padded[...].reshape(rows * GROUP, width)
    for part in range(rows // GROUP):
        moved = dot_nn(order[...], flat[part * GROUP * GROUP : (part + 1) * GROUP * GROUP]).astype(BF16)
        for index in range(feats):
            outs[index][part * GROUP : (part + 1) * GROUP, :] = moved[index * GROUP : (index + 1) * GROUP]


def to_pieces(me, cells, group, block=64):
    _, rows, feats, width = cells.shape
    return pl.pallas_call(
        functools.partial(to_pieces_kernel, group),
        grid=(rows // block,),
        in_specs=[smem_spec(), pl.BlockSpec((1, block, feats, width), lambda i: (0, i, 0, 0))],
        out_specs=[pl.BlockSpec((block, width), lambda i: (i, 0))] * feats,
        out_shape=[jax.ShapeDtypeStruct((rows, width), BF16)] * feats,
        scratch_shapes=[
            pltpu.VMEM((block, GROUP, width), BF16),
            pltpu.VMEM((feats * GROUP, GROUP * GROUP), BF16),
        ],
        compiler_params=params_of(),
        name="to_pieces",
    )(me, cells)


def from_pieces_kernel(group, me_ref, *rest):
    feats = len(rest) - 2
    ins, out_ref, order = rest[:feats], rest[feats], rest[feats + 1]
    rows, width = ins[0].shape

    @pl.when(pl.program_id(0) == 0)
    def _():
        fill_order(order, me_ref[0], feats, group)

    for part in range(rows // GROUP):
        tall = jnp.concatenate([ref[part * GROUP : (part + 1) * GROUP, :] for ref in ins], 0)
        moved = dot_tn(order[...], tall).astype(BF16).reshape(GROUP, GROUP, width)
        out_ref[0, part * GROUP : (part + 1) * GROUP] = moved[:, :feats, :]


def from_pieces(me, pieces, group, block=64):
    rows, width = pieces[0].shape
    feats = len(pieces)
    return pl.pallas_call(
        functools.partial(from_pieces_kernel, group),
        grid=(rows // block,),
        in_specs=[smem_spec()] + [pl.BlockSpec((block, width), lambda i: (i, 0))] * feats,
        out_specs=pl.BlockSpec((1, block, feats, width), lambda i: (0, i, 0, 0)),
        out_shape=jax.ShapeDtypeStruct((1, rows, feats, width), BF16),
        scratch_shapes=[pltpu.VMEM((feats * GROUP, GROUP * GROUP), BF16)],
        compiler_params=params_of(),
        name="from_pieces",
    )(me, *pieces)


def feat_forward_kernel(
    group, me_ref, cells_ref, gain, shift, w_query, w_key, w_value, w_out, bias, *rest
):
    feats, rows, width = cells_ref.shape[2], cells_ref.shape[1], cells_ref.shape[3]
    outs = rest[:feats]
    x_ref, q_ref, k_ref, v_ref, mixed_ref, padded, order = rest[feats:]
    size = feats * GROUP
    scale = 1.0 / math.sqrt(HEAD)

    @pl.when(pl.program_id(0) == 0)
    def _():
        fill_order(order, me_ref[0], feats, group)
        padded[...] = jnp.zeros_like(padded)

    padded[:, :feats, :] = cells_ref[0]
    flat = padded[...].reshape(rows * GROUP, width)
    parts = rows // GROUP
    for part in range(parts):
        moved = dot_nn(order[...], flat[part * GROUP * GROUP : (part + 1) * GROUP * GROUP])
        x_ref[part * size : (part + 1) * size, :] = moved.astype(BF16)
    unit, _ = unit_of(x_ref[...].astype(F32))
    normed = (unit * gain[...] + shift[...]).astype(BF16)
    q_ref[...] = dot_nn(normed, w_query[...]).astype(BF16)
    k_ref[...] = dot_nn(normed, w_key[...]).astype(BF16)
    v_ref[...] = dot_nn(normed, w_value[...]).astype(BF16)
    own = same_row(size)
    for part in range(parts):
        span = slice(part * size, (part + 1) * size)
        for head in range(HEADS):
            lanes = slice(head * HEAD, (head + 1) * HEAD)
            scores = jnp.where(own, dot_nt(q_ref[span, lanes], k_ref[span, lanes]) * scale, NEGATIVE)
            grown = jnp.exp(scores - jnp.max(scores, -1, keepdims=True))
            probs = (grown / jnp.sum(grown, -1, keepdims=True)).astype(BF16)
            mixed_ref[span, lanes] = dot_nn(probs, v_ref[span, lanes]).astype(BF16)
    after = x_ref[...].astype(F32) + dot_nn(mixed_ref[...], w_out[...]) + bias[...]
    after = after.astype(BF16)
    for part in range(parts):
        for index in range(feats):
            start = part * size + index * GROUP
            outs[index][part * GROUP : (part + 1) * GROUP, :] = after[start : start + GROUP]


def feat_forward(me, cells, weights, group, block=64):
    _, rows, feats, width = cells.shape
    tokens = block * feats
    kept = jax.ShapeDtypeStruct((rows * feats, width), BF16)
    whole = pl.BlockSpec((width, width), lambda i: (0, 0))
    vector = pl.BlockSpec((1, width), lambda i: (0, 0))
    return pl.pallas_call(
        functools.partial(feat_forward_kernel, group),
        grid=(rows // block,),
        in_specs=[smem_spec(), pl.BlockSpec((1, block, feats, width), lambda i: (0, i, 0, 0))]
        + [vector, vector, whole, whole, whole, whole, vector],
        out_specs=[pl.BlockSpec((block, width), lambda i: (i, 0))] * feats
        + [pl.BlockSpec((tokens, width), lambda i: (i, 0))] * 5,
        out_shape=[jax.ShapeDtypeStruct((rows, width), BF16)] * feats + [kept] * 5,
        scratch_shapes=[
            pltpu.VMEM((block, GROUP, width), BF16),
            pltpu.VMEM((feats * GROUP, GROUP * GROUP), BF16),
        ],
        compiler_params=params_of(),
        name="feat_forward",
    )(me, cells, *weights)


def pick(lane, *values):
    out = jnp.zeros(lane.shape, F32)
    for index, value in enumerate(values):
        out = jnp.where(lane == index, value, out)
    return out


def thirds(values):
    high = values.astype(BF16).astype(F32)
    rest = values - high
    middle = rest.astype(BF16).astype(F32)
    return high, middle, rest - middle


def lane_of(rows):
    return lax.broadcasted_iota(jnp.int32, (rows, HEAD), 1)


def key_extra(info_ref, piece, rows):
    first = (info_ref[0] ^ piece) * rows
    row = lax.broadcasted_iota(jnp.int32, (rows, HEAD), 0) + first
    lane = lane_of(rows)
    bias = jnp.where(row < info_ref[2], 0.0, NEGATIVE)
    return jnp.where(lane == 0, bias, jnp.where(lane < 4, 1.0, 0.0)).astype(BF16)


def row_forward_kernel(pieces, info_ref, *rest):
    ins, rest = rest[:pieces], rest[pieces:]
    gain, shift, w_query, w_key, w_value, q_ref, k_ref, v_ref, mixed_ref, extra_ref, keys = rest
    rows = ins[0].shape[0]
    tile = 256
    scale = LOG2E / math.sqrt(HEAD)
    for piece in range(pieces):
        span = slice(piece * rows, (piece + 1) * rows)
        unit, _ = unit_of(ins[piece][...].astype(F32))
        normed = (unit * gain[...] + shift[...]).astype(BF16)
        q_ref[span, :] = dot_nn(normed, w_query[...]).astype(BF16)
        k_ref[span, :] = dot_nn(normed, w_key[...]).astype(BF16)
        v_ref[span, :] = dot_nn(normed, w_value[...]).astype(BF16)
        keys[span, :] = key_extra(info_ref, piece, rows)
    lane = lane_of(tile)
    ones = jnp.where(lane == 0, 1.0, 0.0).astype(BF16)

    def one_tile(index, carry):
        span = pl.ds(pl.multiple_of(index * tile, tile), tile)
        for head in range(HEADS):
            lanes = slice(head * HEAD, (head + 1) * HEAD)
            scores = dot_nt(
                jnp.concatenate([q_ref[span, lanes], ones], 1),
                jnp.concatenate([k_ref[:, lanes], keys[...]], 1),
            )
            highest = jnp.max(scores, -1, keepdims=True)
            grown = jnp.exp2((scores - highest) * scale)
            total = jnp.sum(grown, -1, keepdims=True)
            mixed = dot_nn(grown.astype(BF16), v_ref[:, lanes]) / total
            mixed_ref[span, lanes] = mixed.astype(BF16)
            high, middle, low = thirds(-(highest + jnp.log2(total) * (1.0 / scale)))
            extra_ref[span, lanes] = pick(lane, 1.0, high, middle, low).astype(BF16)
        return carry

    lax.fori_loop(0, q_ref.shape[0] // tile, one_tile, 0)


def row_forward(info, ins, weights):
    rows, width = ins[0].shape
    whole = jax.ShapeDtypeStruct((rows * len(ins), width), BF16)
    return pl.pallas_call(
        functools.partial(row_forward_kernel, len(ins)),
        in_specs=[smem_spec()] + [vmem_spec()] * (len(ins) + 5),
        out_specs=[vmem_spec()] * 5,
        out_shape=[whole] * 4 + [jax.ShapeDtypeStruct((rows * len(ins), HEADS * HEAD), BF16)],
        scratch_shapes=[pltpu.VMEM((rows * len(ins), HEAD), BF16)],
        compiler_params=params_of(),
        name="row_forward",
    )(info, *ins, *weights)


def mlp_kernel(pieces, first, info_ref, *rest):
    afters, cots, rest = rest[:pieces], rest[pieces : 2 * pieces], rest[2 * pieces :]
    mixed_ref, w_row, row_bias, gain, shift, w_up, up_bias, w_down, down_bias = rest[:9]
    rest = rest[9:]
    if not first:
        old, rest = rest[:4], rest[4:]
    outs, rest = rest[:pieces], rest[pieces:]
    mixed_grad_ref, grad_ref, up_ref, down_ref, row_ref, vec_ref = rest
    rows, width = afters[0].shape
    wide = w_up.shape[1]
    chunk = 512
    if first:
        for ref in (up_ref, down_ref, row_ref, vec_ref):
            ref[...] = jnp.zeros_like(ref)
    else:
        for ref, was in zip((up_ref, down_ref, row_ref, vec_ref), old):
            ref[...] = was[...]
    c_one, c_three = math.sqrt(2.0 / math.pi), math.sqrt(2.0 / math.pi) * 0.044715
    for piece in range(pieces):
        span = slice(piece * rows, (piece + 1) * rows)
        row = lax.broadcasted_iota(jnp.int32, (rows, 1), 0) + (info_ref[0] ^ piece) * rows
        keep = row < info_ref[1]
        mixed = mixed_ref[span, :]
        after_b = afters[piece][...].astype(F32) + dot_nn(mixed, w_row[...]) + row_bias[...]
        unit, inverse = unit_of(after_b)
        normed = (unit * gain[...] + shift[...]).astype(BF16)
        grad_c_low = jnp.where(keep, cots[piece][...], jnp.zeros((), BF16))
        grad_c = grad_c_low.astype(F32)
        normed_t = normed.T
        grad_t = grad_c_low.T
        total = after_b + down_bias[...]
        upstream = jnp.zeros((rows, width), F32)
        for part in range(wide // chunk):
            lanes = slice(part * chunk, (part + 1) * chunk)
            hidden = dot_nn(normed, w_up[:, lanes]) + up_bias[:, lanes]
            square = hidden * hidden
            bent = jnp.tanh(hidden * (c_one + c_three * square))
            half = 0.5 * (1.0 + bent)
            active = (hidden * half).astype(BF16)
            slope = half + (0.5 * hidden) * (1.0 - bent * bent) * (c_one + 3.0 * c_three * square)
            hidden_grad = (dot_nt(grad_c_low, w_down[lanes, :]) * slope).astype(BF16)
            total += dot_nn(active, w_down[lanes, :])
            down_ref[:, lanes] += dot_nn(grad_t, active)
            up_ref[:, lanes] += dot_nn(normed_t, hidden_grad)
            upstream += dot_nt(hidden_grad, w_up[:, lanes])
            vec_ref[part : part + 1, :] += column_sum(hidden_grad.astype(F32))
        outs[piece][...] = jnp.where(keep, total, 0.0).astype(BF16)
        grad_b = grad_c + norm_back(upstream, unit, inverse, gain[...])
        grad_low = grad_b.astype(BF16)
        grad_ref[span, :] = grad_b
        row_ref[...] += dot_tn(mixed, grad_low)
        mixed_grad_ref[span, :] = dot_nt(grad_low, w_row[...]).astype(BF16)
        vec_ref[4:5, :] += column_sum(grad_c)
        vec_ref[5:6, :] += column_sum(upstream * unit)
        vec_ref[6:7, :] += column_sum(upstream)
        vec_ref[7:8, :] += column_sum(grad_b)


def mlp(info, afters, cots, mixed, weights, old):
    rows, width = afters[0].shape
    count = len(afters)
    wide = weights[4].shape[1]
    first = old is None
    sums = [
        jax.ShapeDtypeStruct((width, wide), F32),
        jax.ShapeDtypeStruct((width, wide), F32),
        jax.ShapeDtypeStruct((width, width), F32),
        jax.ShapeDtypeStruct((8, width), F32),
    ]
    args = [*afters, *cots, mixed, *weights] + ([] if first else list(old))
    return pl.pallas_call(
        functools.partial(mlp_kernel, count, first),
        in_specs=[smem_spec()] + [vmem_spec()] * len(args),
        out_specs=[vmem_spec()] * (count + 6),
        out_shape=[jax.ShapeDtypeStruct((rows, width), BF16)] * count
        + [jax.ShapeDtypeStruct((rows * count, width), BF16), jax.ShapeDtypeStruct((rows * count, width), F32)]
        + sums,
        compiler_params=params_of(60),
        name="mlp",
    )(info, *args)


def row_backward_kernel(pieces, first, info_ref, *rest):
    afters, rest = rest[:pieces], rest[pieces:]
    q_ref, k_ref, v_ref, extra_ref, mixed_ref, mixed_grad_ref, grad_ref = rest[:7]
    gain, shift, w_query, w_key, w_value = rest[7:12]
    rest = rest[12:]
    if not first:
        old, rest = rest[:4], rest[4:]
    outs, rest = rest[:pieces], rest[pieces:]
    sum_query, sum_key, sum_value, vec_ref, keys, key_sum, value_sum, query_grad = rest
    rows, width = afters[0].shape
    tile = 256
    scale = LOG2E / math.sqrt(HEAD)
    score_scale = 1.0 / math.sqrt(HEAD)
    for piece in range(pieces):
        keys[piece * rows : (piece + 1) * rows, :] = key_extra(info_ref, piece, rows)
    key_sum[...] = jnp.zeros_like(key_sum)
    value_sum[...] = jnp.zeros_like(value_sum)
    lane = lane_of(tile)

    def one_tile(index, carry):
        span = pl.ds(pl.multiple_of(index * tile, tile), tile)
        for head in range(HEADS):
            lanes = slice(head * HEAD, (head + 1) * HEAD)
            query, upstream = q_ref[span, lanes], mixed_grad_ref[span, lanes]
            scores = dot_nt(
                jnp.concatenate([k_ref[:, lanes], keys[...]], 1),
                jnp.concatenate([query, extra_ref[span, lanes]], 1),
            )
            probs = jnp.exp2(scores * scale)
            row_dot = jnp.sum(
                upstream.astype(F32) * mixed_ref[span, lanes].astype(F32), -1, keepdims=True
            )
            high, middle, low = thirds(-row_dot)
            inner = dot_nt(
                jnp.concatenate([v_ref[:, lanes], keys[...]], 1),
                jnp.concatenate([upstream, pick(lane, 0.0, high, middle, low).astype(BF16)], 1),
            )
            value_sum[:, lanes] += dot_nn(probs.astype(BF16), upstream)
            score_grad = (probs * inner).astype(BF16)
            key_sum[:, lanes] += dot_nn(score_grad, query)
            query_grad[span, lanes] = (dot_tn(score_grad, k_ref[:, lanes]) * score_scale).astype(BF16)
        return carry

    lax.fori_loop(0, q_ref.shape[0] // tile, one_tile, 0)
    if first:
        for ref in (sum_query, sum_key, sum_value, vec_ref):
            ref[...] = jnp.zeros_like(ref)
    else:
        for ref, was in zip((sum_query, sum_key, sum_value, vec_ref), old):
            ref[...] = was[...]
    for piece in range(pieces):
        span = slice(piece * rows, (piece + 1) * rows)
        unit, inverse = unit_of(afters[piece][...].astype(F32))
        normed_t = (unit * gain[...] + shift[...]).astype(BF16).T
        d_query = query_grad[span, :]
        d_key = (key_sum[span, :] * score_scale).astype(BF16)
        d_value = value_sum[span, :].astype(BF16)
        sum_query[...] += dot_nn(normed_t, d_query)
        sum_key[...] += dot_nn(normed_t, d_key)
        sum_value[...] += dot_nn(normed_t, d_value)
        upstream = dot_nt(d_query, w_query[...]) + dot_nt(d_key, w_key[...]) + dot_nt(d_value, w_value[...])
        grad_a = grad_ref[span, :] + norm_back(upstream, unit, inverse, gain[...])
        outs[piece][...] = grad_a.astype(BF16)
        vec_ref[0:1, :] += column_sum(upstream * unit)
        vec_ref[1:2, :] += column_sum(upstream)
        vec_ref[2:3, :] += column_sum(grad_a)


def row_backward(info, afters, kept, mixed_grad, grad_b, weights, old):
    rows, width = afters[0].shape
    count = len(afters)
    query, key, value, mixed, extra = kept
    first = old is None
    args = [*afters, query, key, value, extra, mixed, mixed_grad, grad_b, *weights]
    args += [] if first else list(old)
    return pl.pallas_call(
        functools.partial(row_backward_kernel, count, first),
        in_specs=[smem_spec()] + [vmem_spec()] * len(args),
        out_specs=[vmem_spec()] * (count + 4),
        out_shape=[jax.ShapeDtypeStruct((rows, width), BF16)] * count
        + [jax.ShapeDtypeStruct((width, width), F32)] * 3
        + [jax.ShapeDtypeStruct((8, width), F32)],
        scratch_shapes=[
            pltpu.VMEM((rows * count, HEAD), BF16),
            pltpu.VMEM((rows * count, width), F32),
            pltpu.VMEM((rows * count, width), F32),
            pltpu.VMEM((rows * count, width), BF16),
        ],
        compiler_params=params_of(),
        name="row_backward",
    )(info, *args)


def feat_backward_kernel(
    group, feats, me_ref, x_ref, q_ref, k_ref, v_ref, mixed_ref, gain, shift, w_query, w_key, w_value, w_out, *rest
):
    grads, rest = rest[:feats], rest[feats:]
    out_ref, sum_query, sum_key, sum_value, sum_out, vec_ref, order, d_query, d_key, d_value = rest
    rows, width = grads[0].shape
    parts, size = rows // GROUP, feats * GROUP
    scale = 1.0 / math.sqrt(HEAD)

    @pl.when(pl.program_id(0) == 0)
    def _():
        fill_order(order, me_ref[0], feats, group)
        for ref in (sum_query, sum_key, sum_value, sum_out, vec_ref):
            ref[...] = jnp.zeros_like(ref)

    grad_low = jnp.concatenate(
        [ref[part * GROUP : (part + 1) * GROUP, :] for part in range(parts) for ref in grads], 0
    )
    grad_a = grad_low.astype(F32)
    sum_out[...] += dot_tn(mixed_ref[...], grad_low)
    mixed_grad = dot_nt(grad_low, w_out[...]).astype(BF16)
    own = same_row(size)
    for part in range(parts):
        span = slice(part * size, (part + 1) * size)
        for head in range(HEADS):
            lanes = slice(head * HEAD, (head + 1) * HEAD)
            query, key, value = q_ref[span, lanes], k_ref[span, lanes], v_ref[span, lanes]
            upstream = mixed_grad[span, lanes]
            scores = jnp.where(own, dot_nt(query, key) * scale, NEGATIVE)
            grown = jnp.exp(scores - jnp.max(scores, -1, keepdims=True))
            probs = grown / jnp.sum(grown, -1, keepdims=True)
            inner = dot_nt(upstream, value)
            score_grad = (probs * (inner - jnp.sum(probs * inner, -1, keepdims=True))).astype(BF16)
            d_query[span, lanes] = (dot_nn(score_grad, key) * scale).astype(BF16)
            d_key[span, lanes] = (dot_tn(score_grad, query) * scale).astype(BF16)
            d_value[span, lanes] = dot_tn(probs.astype(BF16), upstream).astype(BF16)
    unit, inverse = unit_of(x_ref[...].astype(F32))
    normed_t = (unit * gain[...] + shift[...]).astype(BF16).T
    sum_query[...] += dot_nn(normed_t, d_query[...])
    sum_key[...] += dot_nn(normed_t, d_key[...])
    sum_value[...] += dot_nn(normed_t, d_value[...])
    upstream = (
        dot_nt(d_query[...], w_query[...])
        + dot_nt(d_key[...], w_key[...])
        + dot_nt(d_value[...], w_value[...])
    )
    cells = (grad_a + norm_back(upstream, unit, inverse, gain[...])).astype(BF16)
    vec_ref[0:1, :] += column_sum(upstream * unit)
    vec_ref[1:2, :] += column_sum(upstream)
    for part in range(parts):
        moved = dot_tn(order[...], cells[part * size : (part + 1) * size])
        moved = moved.astype(BF16).reshape(GROUP, GROUP, width)
        out_ref[0, part * GROUP : (part + 1) * GROUP] = moved[:, :feats, :]


def feat_backward(me, kept, grads, weights, group, block=64):
    rows, width = grads[0].shape
    feats = len(grads)
    tokens = block * feats
    whole = pl.BlockSpec((width, width), lambda i: (0, 0))
    vector = pl.BlockSpec((1, width), lambda i: (0, 0))
    return pl.pallas_call(
        functools.partial(feat_backward_kernel, group, feats),
        grid=(rows // block,),
        in_specs=[smem_spec()]
        + [pl.BlockSpec((tokens, width), lambda i: (i, 0))] * 5
        + [vector, vector, whole, whole, whole, whole]
        + [pl.BlockSpec((block, width), lambda i: (i, 0))] * feats,
        out_specs=[pl.BlockSpec((1, block, feats, width), lambda i: (0, i, 0, 0))]
        + [whole] * 4
        + [pl.BlockSpec((8, width), lambda i: (0, 0))],
        out_shape=[jax.ShapeDtypeStruct((1, rows, feats, width), BF16)]
        + [jax.ShapeDtypeStruct((width, width), F32)] * 4
        + [jax.ShapeDtypeStruct((8, width), F32)],
        scratch_shapes=[pltpu.VMEM((feats * GROUP, GROUP * GROUP), BF16)]
        + [pltpu.VMEM((tokens, width), BF16)] * 3,
        compiler_params=params_of(),
        name="feat_backward",
    )(me, *kept, *weights, *grads)


def swap(values, step):
    count = lax.axis_size("row")
    if step == 0:
        return values
    return lax.ppermute(values, "row", [(index, index ^ step) for index in range(count)])


def total_over(values):
    part = lax.psum_scatter(values.astype(BF16), "row", scatter_dimension=0, tiled=True)
    return lax.psum(part, "tab").astype(F32)


def by_feature(
    table_cells,
    cotangent,
    row_counts,
    context_counts,
    feat_gain,
    feat_shift,
    feat_query,
    feat_key,
    feat_value,
    feat_out,
    feat_bias,
    row_gain,
    row_shift,
    row_query,
    row_key,
    row_value,
    row_out,
    row_bias,
    mlp_gain,
    mlp_shift,
    up_weight,
    up_bias,
    down_weight,
    down_bias,
):
    count = lax.axis_size("row")
    feats = table_cells.shape[2]
    group = feats // count
    me = lax.axis_index("row").astype(jnp.int32)
    place = me.reshape(1)
    info = jnp.stack([me, row_counts[0], context_counts[0]])

    def flat(vector):
        return vector.reshape(1, -1)

    cot_out = to_pieces(place, cotangent, group)
    feat_weights = (flat(feat_gain), flat(feat_shift), feat_query, feat_key, feat_value, feat_out)
    forward = feat_forward(place, table_cells, (*feat_weights, flat(feat_bias)), group)
    after_out, kept_a = forward[:feats], forward[feats:]

    row_weights = (flat(row_gain), flat(row_shift), row_query, row_key, row_value)
    mlp_weights = (
        row_out,
        flat(row_bias),
        flat(mlp_gain),
        flat(mlp_shift),
        up_weight,
        flat(up_bias),
        down_weight,
        flat(down_bias),
    )
    afters = [[swap(after_out[k * group + j], k) for k in range(count)] for j in range(group)]
    cots = [[swap(cot_out[k * group + j], k) for k in range(count)] for j in range(group)]
    mlp_sums, row_sums = None, None
    layer_back = [None] * feats
    grad_back = [None] * feats
    for j in range(group):
        kept = row_forward(info, afters[j], row_weights)
        found = mlp(info, afters[j], cots[j], kept[3], mlp_weights, mlp_sums)
        layer, mixed_grad, grad_b, mlp_sums = found[:count], found[count], found[count + 1], found[count + 2 :]
        back = row_backward(info, afters[j], kept, mixed_grad, grad_b, row_weights, row_sums)
        grad, row_sums = back[:count], back[count:]
        for k in range(count):
            layer_back[k * group + j] = swap(layer[k], k)
            grad_back[k * group + j] = swap(grad[k], k)
    layer_out = from_pieces(place, layer_back, group)
    cells_grad, *feat_sums = feat_backward(place, kept_a, grad_back, feat_weights, group)
    up_sum, down_sum, row_out_sum, mlp_vec = mlp_sums
    sum_rq, sum_rk, sum_rv, row_vec = row_sums
    sum_fq, sum_fk, sum_fv, sum_fo, feat_vec = feat_sums
    return (
        layer_out,
        cells_grad,
        total_over(feat_vec[0]),
        total_over(feat_vec[1]),
        total_over(sum_fq),
        total_over(sum_fk),
        total_over(sum_fv),
        total_over(sum_fo),
        total_over(row_vec[2]),
        total_over(row_vec[0]),
        total_over(row_vec[1]),
        total_over(sum_rq),
        total_over(sum_rk),
        total_over(sum_rv),
        total_over(row_out_sum),
        total_over(mlp_vec[7]),
        total_over(mlp_vec[5]),
        total_over(mlp_vec[6]),
        total_over(up_sum),
        total_over(mlp_vec[:4].reshape(-1)),
        total_over(down_sum.T),
        total_over(mlp_vec[4]),
    )


def solution(mesh):
    in_specs = (
        P("tab", "row", None, None),
        P("tab", "row", None, None),
        P("tab"),
        P("tab"),
        P(),
        P(),
        P(),
        P(),
        P(),
        P(),
        P(),
        P(),
        P(),
        P(),
        P(),
        P(),
        P(),
        P(),
        P(),
        P(),
        P(),
        P(),
        P(),
        P(),
    )
    out_specs = (
        P("tab", "row", None, None),
        P("tab", "row", None, None),
        P("row"),
        P("row"),
        P("row", None),
        P("row", None),
        P("row", None),
        P("row", None),
        P("row"),
        P("row"),
        P("row"),
        P("row", None),
        P("row", None),
        P("row", None),
        P("row", None),
        P("row"),
        P("row"),
        P("row"),
        P("row", None),
        P("row"),
        P("row", None),
        P("row"),
    )
    count = mesh.shape["row"]
    body = by_feature if count in (1, 2, 4) else shards
    return jax.shard_map(body, mesh=mesh, in_specs=in_specs, out_specs=out_specs, check_vma=False)
```

```python
import functools
import math

import jax
import jax.numpy as jnp
from jax import lax
from jax.experimental import pallas as pl
from jax.experimental.pallas import tpu as pltpu
from jax.sharding import PartitionSpec as P

HEADS = 4


EPSILON = 1e-05
NEGATIVE = -1e30


def normalize(values, gain_vec, shift_vec):
    row_mean = jnp.mean(values, -1, keepdims=True)
    centred = values - row_mean
    inverse = lax.rsqrt(jnp.mean(centred * centred, -1, keepdims=True) + EPSILON)
    unit_part = centred * inverse
    return (unit_part * gain_vec + shift_vec, unit_part, inverse)


def normalize_back(upstream, unit_part, inverse, gain_vec):
    scaled = upstream * gain_vec
    inner_part = (
        scaled
        - jnp.mean(scaled, -1, keepdims=True)
        - unit_part * jnp.mean(scaled * unit_part, -1, keepdims=True)
    )
    return (
        inverse * inner_part,
        jnp.sum(upstream * unit_part, axis=(0, 1)),
        jnp.sum(upstream, axis=(0, 1)),
    )


def project(left_side, weight):
    return jnp.einsum("rfd,de->rfe", left_side, weight, preferred_element_type=jnp.float32)


def project_back(upstream, weight):
    return jnp.einsum("rfe,de->rfd", upstream, weight, preferred_element_type=jnp.float32)


def outer_sum(left_side, upstream):
    return jnp.einsum("rfd,rfe->de", left_side, upstream, preferred_element_type=jnp.float32)


def split_heads(values):
    return values.reshape(values.shape[0], values.shape[1], HEADS, values.shape[2] // HEADS)


def join_heads(values):
    return values.reshape(values.shape[0], values.shape[1], values.shape[2] * values.shape[3])


def shards(
    table_cells,
    cotangent,
    row_counts,
    context_counts,
    feat_gain,
    feat_shift,
    feat_query,
    feat_key,
    feat_value,
    feat_out,
    feat_bias,
    row_gain,
    row_shift,
    row_query,
    row_key,
    row_value,
    row_out,
    row_bias,
    mlp_gain,
    mlp_shift,
    up_weight,
    up_bias,
    down_weight,
    down_bias,
):
    source = table_cells[0].astype(jnp.float32)
    local_rows, feat_count, model_width = source.shape
    score_scale = 1.0 / math.sqrt(model_width // HEADS)
    total_rows = local_rows * lax.axis_size("row")
    row_ids = lax.axis_index("row") * local_rows + jnp.arange(local_rows, dtype=jnp.int32)
    row_mask = (row_ids < row_counts[0]).astype(jnp.float32)[:, None, None]
    context_mask = jnp.arange(total_rows, dtype=jnp.int32) < context_counts[0]
    normed_a, unit_a, inverse_a = normalize(source, feat_gain, feat_shift)
    normed_a = normed_a.astype(jnp.bfloat16)
    query_a = split_heads(project(normed_a, feat_query).astype(jnp.bfloat16))
    key_a = split_heads(project(normed_a, feat_key).astype(jnp.bfloat16))
    value_a = split_heads(project(normed_a, feat_value).astype(jnp.bfloat16))
    scores_a = (
        jnp.einsum("rfhd,rghd->rhfg", query_a, key_a, preferred_element_type=jnp.float32)
        * score_scale
    )
    probs_a = jax.nn.softmax(scores_a, -1)
    probs_a_low = probs_a.astype(jnp.bfloat16)
    mixed_a = join_heads(
        jnp.einsum(
            "rhfg,rghd->rfhd", probs_a_low, value_a, preferred_element_type=jnp.float32
        ).astype(jnp.bfloat16)
    )
    after_a = source + project(mixed_a, feat_out) + feat_bias
    normed_b, unit_b, inverse_b = normalize(after_a, row_gain, row_shift)
    normed_b = normed_b.astype(jnp.bfloat16)
    query_b = split_heads(project(normed_b, row_query).astype(jnp.bfloat16))
    key_b = project(normed_b, row_key).astype(jnp.bfloat16)
    value_b = project(normed_b, row_value).astype(jnp.bfloat16)
    key_all, value_all = (
        lax.all_gather(key_b, "row", axis=0, tiled=True),
        lax.all_gather(value_b, "row", axis=0, tiled=True),
    )

    def row_scores(key_whole):
        raw_scores = (
            jnp.einsum(
                "ifhd,jfhd->fhij",
                query_b,
                split_heads(key_whole),
                preferred_element_type=jnp.float32,
            )
            * score_scale
        )
        return jnp.where(context_mask, raw_scores, NEGATIVE)

    scores_b = row_scores(key_all)
    highest = jnp.max(scores_b, -1, keepdims=True)
    log_total = highest + jnp.log(jnp.sum(jnp.exp(scores_b - highest), -1, keepdims=True))
    probs_b_low = jnp.exp(scores_b - log_total).astype(jnp.bfloat16)
    mixed_b = join_heads(
        jnp.einsum(
            "fhij,jfhd->ifhd",
            probs_b_low,
            split_heads(value_all),
            preferred_element_type=jnp.float32,
        ).astype(jnp.bfloat16)
    )
    after_b = after_a + project(mixed_b, row_out) + row_bias
    normed_c, unit_c, inverse_c = normalize(after_b, mlp_gain, mlp_shift)
    normed_c = normed_c.astype(jnp.bfloat16)
    hidden = project(normed_c, up_weight) + up_bias
    active, gelu_pull = jax.vjp(jax.nn.gelu, hidden)
    active = active.astype(jnp.bfloat16)
    after_c = after_b + project(active, down_weight) + down_bias
    layer_out = (after_c * row_mask).astype(jnp.bfloat16)
    grad_c = cotangent[0].astype(jnp.float32) * row_mask
    grad_c_low = grad_c.astype(jnp.bfloat16)
    down_bias_grad = jnp.sum(grad_c, axis=(0, 1))
    down_weight_grad = outer_sum(active, grad_c_low)
    active_grad = project_back(grad_c_low, down_weight)
    hidden_grad = gelu_pull(active_grad)[0].astype(jnp.bfloat16)
    up_bias_grad = jnp.sum(hidden_grad.astype(jnp.float32), axis=(0, 1))
    up_weight_grad = outer_sum(normed_c, hidden_grad)
    back_c, mlp_gain_grad, mlp_shift_grad = normalize_back(
        project_back(hidden_grad, up_weight), unit_c, inverse_c, mlp_gain
    )
    grad_b = grad_c + back_c
    grad_b_low = grad_b.astype(jnp.bfloat16)
    row_bias_grad = jnp.sum(grad_b, axis=(0, 1))
    row_out_grad = outer_sum(mixed_b, grad_b_low)
    mixed_b_grad = split_heads(project_back(grad_b_low, row_out).astype(jnp.bfloat16))
    key_back, value_back = (
        lax.all_gather(key_b, "row", axis=0, tiled=True),
        lax.all_gather(value_b, "row", axis=0, tiled=True),
    )
    probs_full = jnp.exp(row_scores(key_back) - log_total)
    probs_grad = jnp.einsum(
        "ifhd,jfhd->fhij", mixed_b_grad, split_heads(value_back), preferred_element_type=jnp.float32
    )
    row_dot = jnp.sum(probs_full * probs_grad, -1, keepdims=True)
    score_b_grad = (probs_full * (probs_grad - row_dot)).astype(jnp.bfloat16)
    query_b_grad = join_heads(
        (
            jnp.einsum(
                "fhij,jfhd->ifhd",
                score_b_grad,
                split_heads(key_back),
                preferred_element_type=jnp.float32,
            )
            * score_scale
        ).astype(jnp.bfloat16)
    )
    flat_rows = feat_count * HEADS
    log_all, dot_all = (
        lax.all_gather(log_total.reshape(flat_rows, local_rows), "row", axis=1, tiled=True),
        lax.all_gather(row_dot.reshape(flat_rows, local_rows), "row", axis=1, tiled=True),
    )
    own_mask = row_ids < context_counts[0]
    key_own = split_heads(key_b)
    value_own = split_heads(value_b)
    query_piece = lax.all_gather(query_b, "row", axis=0, tiled=True)
    grad_piece = lax.all_gather(mixed_b_grad, "row", axis=0, tiled=True)
    count = query_piece.shape[0]
    log_piece = log_all.reshape(feat_count, HEADS, count, 1)
    dot_piece = dot_all.reshape(feat_count, HEADS, count, 1)
    piece_scores = (
        jnp.einsum("ifhd,jfhd->fhij", query_piece, key_own, preferred_element_type=jnp.float32)
        * score_scale
    )
    piece_scores = jnp.where(own_mask, piece_scores, NEGATIVE)
    piece_probs = jnp.exp(piece_scores - log_piece)
    piece_inner = jnp.einsum(
        "ifhd,jfhd->fhij", grad_piece, value_own, preferred_element_type=jnp.float32
    )
    piece_grad = (piece_probs * (piece_inner - dot_piece)).astype(jnp.bfloat16)
    key_total = (
        jnp.einsum("fhij,ifhd->jfhd", piece_grad, query_piece, preferred_element_type=jnp.float32)
        * score_scale
    )
    value_total = jnp.einsum(
        "fhij,ifhd->jfhd",
        piece_probs.astype(jnp.bfloat16),
        grad_piece,
        preferred_element_type=jnp.float32,
    )
    key_total, value_total = (key_total, value_total)
    key_b_grad = join_heads(key_total).astype(jnp.bfloat16)
    value_b_grad = join_heads(value_total).astype(jnp.bfloat16)
    row_query_grad = outer_sum(normed_b, query_b_grad)
    row_key_grad = outer_sum(normed_b, key_b_grad)
    row_value_grad = outer_sum(normed_b, value_b_grad)
    normed_b_grad = (
        project_back(query_b_grad, row_query)
        + project_back(key_b_grad, row_key)
        + project_back(value_b_grad, row_value)
    )
    back_b, row_gain_grad, row_shift_grad = normalize_back(
        normed_b_grad, unit_b, inverse_b, row_gain
    )
    grad_a = grad_b + back_b
    grad_a_low = grad_a.astype(jnp.bfloat16)
    feat_bias_grad = jnp.sum(grad_a, axis=(0, 1))
    feat_out_grad = outer_sum(mixed_a, grad_a_low)
    mixed_a_grad = split_heads(project_back(grad_a_low, feat_out).astype(jnp.bfloat16))
    probs_a_grad = jnp.einsum(
        "rfhd,rghd->rhfg", mixed_a_grad, value_a, preferred_element_type=jnp.float32
    )
    score_a_grad = (
        probs_a * (probs_a_grad - jnp.sum(probs_a * probs_a_grad, -1, keepdims=True))
    ).astype(jnp.bfloat16)
    query_a_grad = join_heads(
        (
            jnp.einsum("rhfg,rghd->rfhd", score_a_grad, key_a, preferred_element_type=jnp.float32)
            * score_scale
        ).astype(jnp.bfloat16)
    )
    key_a_grad = join_heads(
        (
            jnp.einsum("rhfg,rfhd->rghd", score_a_grad, query_a, preferred_element_type=jnp.float32)
            * score_scale
        ).astype(jnp.bfloat16)
    )
    value_a_grad = join_heads(
        jnp.einsum(
            "rhfg,rfhd->rghd", probs_a_low, mixed_a_grad, preferred_element_type=jnp.float32
        ).astype(jnp.bfloat16)
    )
    feat_query_grad = outer_sum(normed_a, query_a_grad)
    feat_key_grad = outer_sum(normed_a, key_a_grad)
    feat_value_grad = outer_sum(normed_a, value_a_grad)
    normed_a_grad = (
        project_back(query_a_grad, feat_query)
        + project_back(key_a_grad, feat_key)
        + project_back(value_a_grad, feat_value)
    )
    back_a, feat_gain_grad, feat_shift_grad = normalize_back(
        normed_a_grad, unit_a, inverse_a, feat_gain
    )
    cells_grad = (grad_a + back_a).astype(jnp.bfloat16)
    row_summed = (
        lax.psum_scatter(
            feat_gain_grad.astype(jnp.bfloat16), "row", scatter_dimension=0, tiled=True
        ).astype(jnp.float32),
        lax.psum_scatter(
            feat_shift_grad.astype(jnp.bfloat16), "row", scatter_dimension=0, tiled=True
        ).astype(jnp.float32),
        lax.psum_scatter(
            feat_query_grad.astype(jnp.bfloat16), "row", scatter_dimension=0, tiled=True
        ).astype(jnp.float32),
        lax.psum_scatter(
            feat_key_grad.astype(jnp.bfloat16), "row", scatter_dimension=0, tiled=True
        ).astype(jnp.float32),
        lax.psum_scatter(
            feat_value_grad.astype(jnp.bfloat16), "row", scatter_dimension=0, tiled=True
        ).astype(jnp.float32),
        lax.psum_scatter(
            feat_out_grad.astype(jnp.bfloat16), "row", scatter_dimension=0, tiled=True
        ).astype(jnp.float32),
        lax.psum_scatter(
            feat_bias_grad.astype(jnp.bfloat16), "row", scatter_dimension=0, tiled=True
        ).astype(jnp.float32),
        lax.psum_scatter(
            row_gain_grad.astype(jnp.bfloat16), "row", scatter_dimension=0, tiled=True
        ).astype(jnp.float32),
        lax.psum_scatter(
            row_shift_grad.astype(jnp.bfloat16), "row", scatter_dimension=0, tiled=True
        ).astype(jnp.float32),
        lax.psum_scatter(
            row_query_grad.astype(jnp.bfloat16), "row", scatter_dimension=0, tiled=True
        ).astype(jnp.float32),
        lax.psum_scatter(
            row_key_grad.astype(jnp.bfloat16), "row", scatter_dimension=0, tiled=True
        ).astype(jnp.float32),
        lax.psum_scatter(
            row_value_grad.astype(jnp.bfloat16), "row", scatter_dimension=0, tiled=True
        ).astype(jnp.float32),
        lax.psum_scatter(
            row_out_grad.astype(jnp.bfloat16), "row", scatter_dimension=0, tiled=True
        ).astype(jnp.float32),
        lax.psum_scatter(
            row_bias_grad.astype(jnp.bfloat16), "row", scatter_dimension=0, tiled=True
        ).astype(jnp.float32),
        lax.psum_scatter(
            mlp_gain_grad.astype(jnp.bfloat16), "row", scatter_dimension=0, tiled=True
        ).astype(jnp.float32),
        lax.psum_scatter(
            mlp_shift_grad.astype(jnp.bfloat16), "row", scatter_dimension=0, tiled=True
        ).astype(jnp.float32),
        lax.psum_scatter(
            up_weight_grad.astype(jnp.bfloat16), "row", scatter_dimension=0, tiled=True
        ).astype(jnp.float32),
        lax.psum_scatter(
            up_bias_grad.astype(jnp.bfloat16), "row", scatter_dimension=0, tiled=True
        ).astype(jnp.float32),
        lax.psum_scatter(
            down_weight_grad.astype(jnp.bfloat16), "row", scatter_dimension=0, tiled=True
        ).astype(jnp.float32),
        lax.psum_scatter(
            down_bias_grad.astype(jnp.bfloat16), "row", scatter_dimension=0, tiled=True
        ).astype(jnp.float32),
    )
    (
        part_fg,
        part_fs,
        part_fq,
        part_fk,
        part_fv,
        part_fo,
        part_fb,
        part_rg,
        part_rs,
        part_rq,
        part_rk,
        part_rv,
        part_ro,
        part_rb,
        part_mg,
        part_ms,
        part_uw,
        part_ub,
        part_dw,
        part_db,
    ) = row_summed
    summed = (
        lax.psum(part_fg.astype(jnp.bfloat16), "tab").astype(jnp.float32),
        lax.psum(part_fs.astype(jnp.bfloat16), "tab").astype(jnp.float32),
        lax.psum(part_fq.astype(jnp.bfloat16), "tab").astype(jnp.float32),
        lax.psum(part_fk.astype(jnp.bfloat16), "tab").astype(jnp.float32),
        lax.psum(part_fv.astype(jnp.bfloat16), "tab").astype(jnp.float32),
        lax.psum(part_fo.astype(jnp.bfloat16), "tab").astype(jnp.float32),
        lax.psum(part_fb.astype(jnp.bfloat16), "tab").astype(jnp.float32),
        lax.psum(part_rg.astype(jnp.bfloat16), "tab").astype(jnp.float32),
        lax.psum(part_rs.astype(jnp.bfloat16), "tab").astype(jnp.float32),
        lax.psum(part_rq.astype(jnp.bfloat16), "tab").astype(jnp.float32),
        lax.psum(part_rk.astype(jnp.bfloat16), "tab").astype(jnp.float32),
        lax.psum(part_rv.astype(jnp.bfloat16), "tab").astype(jnp.float32),
        lax.psum(part_ro.astype(jnp.bfloat16), "tab").astype(jnp.float32),
        lax.psum(part_rb.astype(jnp.bfloat16), "tab").astype(jnp.float32),
        lax.psum(part_mg.astype(jnp.bfloat16), "tab").astype(jnp.float32),
        lax.psum(part_ms.astype(jnp.bfloat16), "tab").astype(jnp.float32),
        lax.psum(part_uw.astype(jnp.bfloat16), "tab").astype(jnp.float32),
        lax.psum(part_ub.astype(jnp.bfloat16), "tab").astype(jnp.float32),
        lax.psum(part_dw.astype(jnp.bfloat16), "tab").astype(jnp.float32),
        lax.psum(part_db.astype(jnp.bfloat16), "tab").astype(jnp.float32),
    )
    return (
        layer_out[None],
        cells_grad[None],
        summed[0],
        summed[1],
        summed[2],
        summed[3],
        summed[4],
        summed[5],
        summed[6],
        summed[7],
        summed[8],
        summed[9],
        summed[10],
        summed[11],
        summed[12],
        summed[13],
        summed[14],
        summed[15],
        summed[16],
        summed[17],
        summed[18],
        summed[19],
    )


HEAD = 128
GROUP = 16
LOG2E = 1.4426950408889634
F32 = jnp.float32
BF16 = jnp.bfloat16
SCORE = 1.0 / math.sqrt(HEAD)
SCALE = LOG2E * SCORE


def dot_nn(a, b):
    return jnp.dot(a, b, preferred_element_type=F32)


def dot_nt(a, b):
    return lax.dot_general(a, b, (((1,), (1,)), ((), ())), preferred_element_type=F32)


def dot_tn(a, b):
    return lax.dot_general(a, b, (((0,), (0,)), ((), ())), preferred_element_type=F32)


def unit_of(values):
    centred = values - jnp.mean(values, -1, keepdims=True)
    inverse = lax.rsqrt(jnp.mean(centred * centred, -1, keepdims=True) + EPSILON)
    return centred * inverse, inverse


def norm_back(upstream, unit, inverse, gain):
    scaled = upstream * gain
    return inverse * (
        scaled
        - jnp.mean(scaled, -1, keepdims=True)
        - unit * jnp.mean(scaled * unit, -1, keepdims=True)
    )


def column_sum(values):
    return jnp.sum(values, 0, keepdims=True)


def vmem_spec():
    return pl.BlockSpec(memory_space=pltpu.VMEM)


def smem_spec():
    return pl.BlockSpec(memory_space=pltpu.SMEM)


def any_spec():
    return pl.BlockSpec(memory_space=pl.ANY)


def fixed(shape):
    return pl.BlockSpec(shape, lambda *_: (0,) * len(shape))


def shape_of(shape, dtype=BF16):
    return jax.ShapeDtypeStruct(shape, dtype)


def params_of(mib=63):
    return pltpu.CompilerParams(vmem_limit_bytes=mib * 1024 * 1024)


def call(kernel, args, waits, in_specs, **rest):
    count = len(args)

    def body(*refs):
        kernel(*refs[:count], *refs[count + len(waits) :])

    specs = [*in_specs, *[any_spec() for _ in waits]]
    return pl.pallas_call(body, in_specs=specs, compiler_params=params_of(), **rest)(*args, *waits)


def cost_of(microseconds):
    return pl.CostEstimate(flops=int(microseconds * 900e6), bytes_accessed=1024, transcendentals=0)


def head_lanes(head):
    return slice(head * HEAD, (head + 1) * HEAD)


def lane_of(rows):
    return lax.broadcasted_iota(jnp.int32, (rows, HEAD), 1)


def put_thirds(lane, first, values, base):
    high = values.astype(BF16).astype(F32)
    rest = values - high
    middle = rest.astype(BF16).astype(F32)
    turn = (lane - first) % 3
    parts = jnp.where(turn == 0, high, jnp.where(turn == 1, middle, rest - middle))
    return jnp.where((lane >= first) & (lane < first + 3 * HEADS), parts, base).astype(BF16)


def own_lanes(lane, first, head):
    return (lane >= first + 3 * head) & (lane < first + 3 * head + 3)


def head_picker(first, width):
    head = lax.broadcasted_iota(jnp.int32, (width, HEAD), 0) // HEAD
    lane = lax.broadcasted_iota(jnp.int32, (width, HEAD), 1)
    hit = (lane >= first) & (lane < first + 3 * HEADS) & ((lane - first) // 3 == head)
    return jnp.where(hit, 1.0, 0.0).astype(BF16)


def head_dots(left, right, picker):
    product = left.astype(F32) * right.astype(F32)
    high = product.astype(BF16)
    low = (product - high.astype(F32)).astype(BF16)
    return dot_nn(high, picker) + dot_nn(low, picker)


def beside(left, right):
    return jnp.concatenate([left, right], 1)


def split_kernel(group, me_ref, whole_ref, *rest):
    outs, sems = rest[:-1], rest[-1]
    copies = []
    for index, (piece, first, size) in enumerate(split_plan(group)):
        source = whole_ref.at[pl.ds((me_ref[0] ^ piece) * group + first, size)]
        copies.append(pltpu.make_async_copy(source, outs[index], sems.at[index]))
        copies[-1].start()
    for copy in copies:
        copy.wait()


def split_plan(group):
    return [(0, 0, group), (1, 0, group)] + [(piece, j, 1) for j in range(group) for piece in (2, 3)]


def split(me, whole, group, waits=()):
    plan = split_plan(group)
    _, rows, width = whole.shape
    return call(
        functools.partial(split_kernel, group),
        (me, whole,),
        waits,
        in_specs=[smem_spec(), any_spec()],
        out_specs=[vmem_spec()] * len(plan),
        out_shape=[shape_of((size, rows, width)) for _, _, size in plan],
        scratch_shapes=[pltpu.SemaphoreType.DMA((len(plan),))],
        cost_estimate=cost_of(2),
        name="split",
    )


def query_mask(size):
    row = lax.broadcasted_iota(jnp.int32, (size, HEAD), 0) % GROUP
    lane = lane_of(size)
    return jnp.where((lane < GROUP) & (lane != row), NEGATIVE, 0.0)


def key_mask(size, head):
    row = lax.broadcasted_iota(jnp.int32, (size, HEAD), 0) % GROUP
    lane = lane_of(size)
    return jnp.where((lane == row) | own_lanes(lane, GROUP, head), 1.0, 0.0).astype(BF16)


def gather_cells(group, me_ref, cells_ref):
    feats, rows, _ = cells_ref.shape
    return jnp.concatenate(
        [
            cells_ref[(me_ref[0] ^ (index // group)) * group + index % group, part : part + GROUP, :]
            for part in range(0, rows, GROUP)
            for index in range(feats)
        ],
        0,
    )


def feat_forward_kernel(
    group, me_ref, cells_ref, gain, shift, w_query, w_key, w_value, w_out, bias, *rest
):
    feats, rows, width = cells_ref.shape
    outs = rest[:feats]
    q_ref, k_ref, v_ref, mixed_ref, extra_ref = rest[feats:]
    size, parts = feats * GROUP, rows // GROUP
    cells = gather_cells(group, me_ref, cells_ref)
    unit, _ = unit_of(cells.astype(F32))
    normed = (unit * gain[...] + shift[...]).astype(BF16)
    q_ref[...] = dot_nn(normed, w_query[...]).astype(BF16)
    k_ref[...] = dot_nn(normed, w_key[...]).astype(BF16)
    v_ref[...] = dot_nn(normed, w_value[...]).astype(BF16)
    mask = query_mask(size)
    mask_low = mask.astype(BF16)
    keys = [key_mask(size, head) for head in range(HEADS)]
    lane = lane_of(size)
    ones = jnp.ones((size, HEAD), BF16)
    pairs = [
        (slice(part * size, (part + 1) * size), head_lanes(head), head)
        for part in range(parts)
        for head in range(HEADS)
    ]
    scores = [
        dot_nt(beside(q_ref[span, lanes], mask_low), beside(k_ref[span, lanes], keys[head]))
        for span, lanes, head in pairs
    ]
    tops = [jnp.max(score, -1, keepdims=True) for score in scores]
    grown = [jnp.exp2((score - top) * SCALE).astype(BF16) for score, top in zip(scores, tops)]
    both = [dot_nn(grow, beside(v_ref[span, lanes], ones)) for (span, lanes, _), grow in zip(pairs, grown)]
    for (span, lanes, _), found in zip(pairs, both):
        mixed_ref[span, lanes] = (found[:, :HEAD] / found[:, HEAD:]).astype(BF16)
    for part in range(parts):
        top, total = jnp.zeros((size, HEAD), F32), jnp.ones((size, HEAD), F32)
        for head in range(HEADS):
            own = own_lanes(lane, GROUP, head)
            top = jnp.where(own, tops[part * HEADS + head], top)
            total = jnp.where(own, both[part * HEADS + head][:, HEAD:], total)
        minus = -(top + jnp.log2(total) * (1.0 / SCALE))
        extra_ref[part * size : (part + 1) * size, :] = put_thirds(lane, GROUP, minus, mask)
    after = cells.astype(F32) + dot_nn(mixed_ref[...], w_out[...]) + bias[...]
    after = after.astype(BF16)
    for part in range(parts):
        for index in range(feats):
            start = part * size + index * GROUP
            outs[index][part * GROUP : (part + 1) * GROUP, :] = after[start : start + GROUP]


def feat_forward(me, cells, weights, group, block=64, waits=()):
    feats, rows, width = cells.shape
    tokens = block * feats
    vector, whole = fixed((1, width)), fixed((width, width))
    return call(
        functools.partial(feat_forward_kernel, group),
        (me, cells, *weights,),
        waits,
        grid=(rows // block,),
        in_specs=[smem_spec(), pl.BlockSpec((feats, block, width), lambda i: (0, i, 0))]
        + [vector, vector, whole, whole, whole, whole, vector],
        out_specs=[pl.BlockSpec((block, width), lambda i: (i, 0))] * feats
        + [pl.BlockSpec((tokens, width), lambda i: (i, 0))] * 4
        + [pl.BlockSpec((tokens, HEAD), lambda i: (i, 0))],
        out_shape=[shape_of((rows, width))] * feats
        + [shape_of((rows * feats, width))] * 4
        + [shape_of((rows * feats, HEAD))],
        cost_estimate=cost_of(15),
        name="feat_forward",
    )


def feat_backward_kernel(
    group,
    place_ref,
    cells_ref,
    q_ref,
    k_ref,
    v_ref,
    mixed_ref,
    extra_ref,
    gain,
    shift,
    w_query,
    w_key,
    w_value,
    w_out,
    *rest,
):
    feats, rows, width = cells_ref.shape
    grads, rest = rest[:feats], rest[feats:]
    keep_ref, send_ref, d_query, d_key, d_value, sum_query, sum_key, sum_value, sum_out, vec_ref = rest
    parts, size = rows // GROUP, feats * GROUP

    @pl.when(pl.program_id(0) == 0)
    def _():
        for ref in (sum_query, sum_key, sum_value, sum_out, vec_ref):
            ref[...] = jnp.zeros_like(ref)

    grad_low = jnp.concatenate(
        [ref[part * GROUP : (part + 1) * GROUP, :] for part in range(parts) for ref in grads], 0
    )
    sum_out[...] += dot_tn(mixed_ref[...], grad_low)
    mixed_grad = dot_nt(grad_low, w_out[...]).astype(BF16)
    dots = head_dots(mixed_grad, mixed_ref[...], head_picker(GROUP, width))
    dots = put_thirds(lane_of(dots.shape[0]), GROUP, -dots, jnp.zeros((), F32))
    keys = [key_mask(size, head) for head in range(HEADS)]
    pairs = [
        (slice(part * size, (part + 1) * size), head_lanes(head), head)
        for part in range(parts)
        for head in range(HEADS)
    ]
    scores = [dot_nt(beside(k_ref[s, l], keys[h]), beside(q_ref[s, l], extra_ref[s, :])) for s, l, h in pairs]
    inners = [dot_nt(beside(v_ref[s, l], keys[h]), beside(mixed_grad[s, l], dots[s])) for s, l, h in pairs]
    probs = [jnp.exp2(score * SCALE) for score in scores]
    score_grads = [(prob * inner).astype(BF16) for prob, inner in zip(probs, inners)]
    for (s, l, _), prob in zip(pairs, probs):
        d_value[s, l] = dot_nn(prob.astype(BF16), mixed_grad[s, l]).astype(BF16)
    for (s, l, _), score_grad in zip(pairs, score_grads):
        d_key[s, l] = (dot_nn(score_grad, q_ref[s, l]) * SCORE).astype(BF16)
    for (s, l, _), score_grad in zip(pairs, score_grads):
        d_query[s, l] = (dot_tn(score_grad, k_ref[s, l]) * SCORE).astype(BF16)
    unit, _ = unit_of(gather_cells(group, place_ref, cells_ref).astype(F32))
    normed_t = (unit * gain[...] + shift[...]).astype(BF16).T
    sum_query[...] += dot_nn(normed_t, d_query[...])
    sum_key[...] += dot_nn(normed_t, d_key[...])
    sum_value[...] += dot_nn(normed_t, d_value[...])
    vec_ref[2:3, :] += column_sum(d_query[...].astype(F32))
    vec_ref[3:4, :] += column_sum(d_key[...].astype(F32))
    vec_ref[4:5, :] += column_sum(d_value[...].astype(F32))

    @pl.when(pl.program_id(0) == pl.num_programs(0) - 1)
    def _():
        ones = jnp.ones((8, width), BF16)
        crossed, plain = jnp.zeros((8, width), F32), jnp.zeros((8, width), F32)
        for index, (weight, total) in enumerate(
            ((w_query, sum_query), (w_key, sum_key), (w_value, sum_value))
        ):
            product = weight[...].astype(F32) * total[...]
            column = jnp.broadcast_to(vec_ref[2 + index : 3 + index, :], (8, width))
            for _ in range(3):
                crossed = crossed + dot_nt(ones, product.astype(BF16))
                product = product - product.astype(BF16).astype(F32)
                plain = plain + dot_nt(column.astype(BF16), weight[...])
                column = column - column.astype(BF16).astype(F32)
        vec_ref[0:1, :] = (crossed[:1] - shift[...] * plain[:1]) / gain[...]
        vec_ref[1:2, :] = plain[:1]

        def fill(out, place, quarter, piece):
            start = pl.multiple_of(quarter * HEAD + piece * GROUP, GROUP)
            for index, ref in enumerate((sum_query, sum_key, sum_value, sum_out)):
                out[place, index * GROUP : (index + 1) * GROUP, :] = ref[pl.ds(start, GROUP), :].astype(BF16)
            out[place, 4 * GROUP : 5 * GROUP, :] = padded_vec(vec_ref)

        fill_batch(place_ref, keep_ref, send_ref, fill, x_first)


def feat_backward(place, cells, kept, grads, weights, group, block=64, waits=()):
    feats, rows, width = cells.shape
    tokens = block * feats
    vector, whole = fixed((1, width)), fixed((width, width))
    batch = (BATCH, 5 * GROUP, width)
    row_block = pl.BlockSpec((tokens, width), lambda i: (i, 0))
    return call(
        functools.partial(feat_backward_kernel, group),
        (place, cells, *kept, *weights, *grads,),
        waits,
        grid=(rows // block,),
        in_specs=[smem_spec(), pl.BlockSpec((feats, block, width), lambda i: (0, i, 0))]
        + [row_block] * 4
        + [pl.BlockSpec((tokens, HEAD), lambda i: (i, 0))]
        + [vector, vector, whole, whole, whole, whole]
        + [pl.BlockSpec((block, width), lambda i: (i, 0))] * feats,
        out_specs=[fixed(batch)] * 2 + [row_block] * 3,
        out_shape=[shape_of(batch)] * 2 + [shape_of((rows * feats, width))] * 3,
        scratch_shapes=[pltpu.VMEM((width, width), F32)] * 4 + [pltpu.VMEM((8, width), F32)],
        cost_estimate=cost_of(20),
        name="feat_backward",
    )


def cells_backward_kernel(group, me_ref, cells_ref, d_query, d_key, d_value, gain, w_query, w_key, w_value, *rest):
    grads, (out_ref, mark_ref) = rest[:-2], rest[-2:]
    feats, rows, _ = cells_ref.shape
    mark_ref[...] = jnp.zeros_like(mark_ref)
    parts, size = rows // GROUP, feats * GROUP
    unit, inverse = unit_of(gather_cells(group, me_ref, cells_ref).astype(F32))
    upstream = (
        dot_nt(d_query[...], w_query[...])
        + dot_nt(d_key[...], w_key[...])
        + dot_nt(d_value[...], w_value[...])
    )
    back = norm_back(upstream, unit, inverse, gain[...])
    for index in range(feats):
        true = (me_ref[0] ^ (index // group)) * group + index % group
        for part in range(parts):
            start = part * size + index * GROUP
            span = slice(part * GROUP, (part + 1) * GROUP)
            cells = grads[index][span, :].astype(F32) + back[start : start + GROUP]
            out_ref[true, span, :] = cells.astype(BF16)


def cells_backward(me, cells, d_all, weights, grads, group, block=64, waits=()):
    feats, rows, width = cells.shape
    tokens = block * feats
    vector, whole = fixed((1, width)), fixed((width, width))
    row_block = pl.BlockSpec((tokens, width), lambda i: (i, 0))
    by_rows = pl.BlockSpec((feats, block, width), lambda i: (0, i, 0))
    return call(
        functools.partial(cells_backward_kernel, group),
        (me, cells, *d_all, *weights, *grads,),
        waits,
        grid=(rows // block,),
        in_specs=[smem_spec(), by_rows]
        + [row_block] * 3
        + [vector, whole, whole, whole]
        + [pl.BlockSpec((block, width), lambda i: (i, 0))] * feats,
        out_specs=[by_rows, fixed((8, HEAD))],
        out_shape=[shape_of((feats, rows, width)), shape_of((8, HEAD), F32)],
        cost_estimate=cost_of(12),
        name="cells_backward",
    )


def key_extra(info_ref, piece, rows, head):
    first = (info_ref[0] ^ piece) * rows
    row = lax.broadcasted_iota(jnp.int32, (rows, HEAD), 0) + first
    lane = lane_of(rows)
    bias = jnp.where(row < info_ref[2], 0.0, NEGATIVE)
    return jnp.where(lane == 0, bias, jnp.where(own_lanes(lane, 1, head), 1.0, 0.0)).astype(BF16)


def row_backward_kernel(pieces, info_ref, *rest):
    q_ref, k_ref, v_ref, extra_ref, mixed_grad_ref, dots_ref, rest = *rest[:6], rest[6:]
    afters, rest = rest[:pieces], rest[pieces:]
    grad_hbm, gain, w_query_hbm, w_key_hbm, w_value_hbm = rest[:5]
    outs, rest = rest[5 : 5 + pieces], rest[5 + pieces :]
    d_query, d_key, d_value, vec_ref = rest[:4]
    after, grad, w_query, w_key, w_value, query_all, key_all, value_all, query_sum, sems = rest[4:]
    rows, width = outs[0].shape
    full = rows * pieces
    head = pl.program_id(0)
    copies = [
        pltpu.make_async_copy(afters[piece], after.at[pl.ds(piece * rows, rows), :], sems.at[piece])
        for piece in range(pieces)
    ]
    copies.append(pltpu.make_async_copy(grad_hbm, grad, sems.at[pieces]))
    for index, (source, target) in enumerate(
        ((w_query_hbm, w_query), (w_key_hbm, w_key), (w_value_hbm, w_value))
    ):
        copies.append(pltpu.make_async_copy(source, target, sems.at[pieces + 1 + index]))

    @pl.when(head == 0)
    def _():
        for copy in copies:
            copy.start()

    query = beside(q_ref[...], extra_ref[...])
    upstream = beside(mixed_grad_ref[...], dots_ref[...])
    spans = [slice(index * rows, (index + 1) * rows) for index in range(pieces)]
    keys = [key_extra(info_ref, index, rows, head) for index in range(pieces)]
    scores = [dot_nt(beside(k_ref[span, :], extra), query) for span, extra in zip(spans, keys)]
    inners = [dot_nt(beside(v_ref[span, :], extra), upstream) for span, extra in zip(spans, keys)]
    probs = [jnp.exp2(score * SCALE) for score in scores]
    score_grads = [(prob * inner).astype(BF16) for prob, inner in zip(probs, inners)]
    for span, prob in zip(spans, probs):
        value_all[head, span, :] = dot_nn(prob.astype(BF16), mixed_grad_ref[...]).astype(BF16)
    for span, score_grad in zip(spans, score_grads):
        key_all[head, span, :] = (dot_nn(score_grad, q_ref[...]) * SCORE).astype(BF16)
    query_sum[...] = dot_tn(jnp.concatenate(score_grads, 0), k_ref[...])
    query_all[head] = (query_sum[...] * SCORE).astype(BF16)

    @pl.when(head == HEADS - 1)
    def _():
        for copy in copies:
            copy.wait()
        vec_ref[...] = jnp.zeros_like(vec_ref)
        for piece in range(pieces):
            span = slice(piece * rows, (piece + 1) * rows)
            unit, inverse = unit_of(after[span, :].astype(F32))
            upstream = None
            for ref, weight, out in (
                (query_all, w_query, d_query),
                (key_all, w_key, d_key),
                (value_all, w_value, d_value),
            ):
                flat = jnp.concatenate([ref[index, span, :] for index in range(HEADS)], 1)
                out[span, :] = flat
                part = dot_nt(flat, weight[...])
                upstream = part if upstream is None else upstream + part
            grad_a = grad[span, :] + norm_back(upstream, unit, inverse, gain[...])
            outs[piece][...] = grad_a.astype(BF16)
            vec_ref[0:1, :] += column_sum(upstream * unit)
            vec_ref[1:2, :] += column_sum(upstream)
            vec_ref[2:3, :] += column_sum(grad_a)


def row_backward(info, kept, back, afters, weights, waits=()):
    rows, width = afters[0].shape
    count = len(afters)
    full = rows * count
    query, key, value, extra = kept
    mixed_grad, grad_b, dots = back
    by_head = pl.BlockSpec((full, HEAD), lambda h: (0, h))
    return call(
        functools.partial(row_backward_kernel, count),
        (info, query, key, value, extra, mixed_grad, dots, *afters, grad_b, *weights,),
        waits,
        grid=(HEADS,),
        in_specs=[smem_spec()]
        + [by_head] * 3
        + [fixed((full, HEAD)), by_head, fixed((full, HEAD))]
        + [any_spec()] * (count + 1)
        + [fixed((1, width))]
        + [any_spec()] * 3,
        out_specs=[fixed((rows, width))] * count + [fixed((full, width))] * 3 + [fixed((8, width))],
        out_shape=[shape_of((rows, width))] * count + [shape_of((full, width))] * 3 + [shape_of((8, width), F32)],
        scratch_shapes=[
            pltpu.VMEM((full, width), BF16),
            pltpu.VMEM((full, width), F32),
            pltpu.VMEM((width, width), BF16),
            pltpu.VMEM((width, width), BF16),
            pltpu.VMEM((width, width), BF16),
            pltpu.VMEM((HEADS, full, HEAD), BF16),
            pltpu.VMEM((HEADS, full, HEAD), BF16),
            pltpu.VMEM((HEADS, full, HEAD), BF16),
            pltpu.VMEM((full, HEAD), F32),
            pltpu.SemaphoreType.DMA((count + 4,)),
        ],
        cost_estimate=cost_of(15),
        name="row_backward",
    )


def row_weights_kernel(group, place_ref, *rest):
    normeds, rest = rest[:group], rest[group:]
    grads, rest = rest[: 3 * group], rest[3 * group :]
    vecs, rest = rest[:group], rest[group:]
    keep_ref, send_ref, normed, grad, totals, sems = rest
    copies = []
    for j in range(group):
        mine = [pltpu.make_async_copy(normeds[j], normed.at[j], sems.at[4 * j])]
        for index in range(3):
            mine.append(pltpu.make_async_copy(grads[3 * j + index], grad.at[j, index], sems.at[4 * j + 1 + index]))
        for copy in mine:
            copy.start()
        copies.append(mine)
    for j in range(group):
        for copy in copies[j]:
            copy.wait()
        turned = normed[j].T
        for index in range(3):
            part = dot_nn(turned, grad[j, index])
            if j == 0:
                totals[index] = part
            else:
                totals[index] += part
    vec = sum((ref[...] for ref in vecs[1:]), vecs[0][...])

    def fill(out, place, quarter, piece):
        start = pl.multiple_of(quarter * HEAD + piece * GROUP, GROUP)
        for index in range(3):
            out[place, index * GROUP : (index + 1) * GROUP, :] = totals[index, pl.ds(start, GROUP), :].astype(BF16)
        out[place, 3 * GROUP : 4 * GROUP, :] = padded_vec(vec)

    fill_batch(place_ref, keep_ref, send_ref, fill, x_first)


def row_weights(place, normeds, grads, vecs, waits=()):
    group = len(normeds)
    full, width = normeds[0].shape
    batch = (BATCH, 4 * GROUP, width)
    return call(
        functools.partial(row_weights_kernel, group),
        (place, *normeds, *grads, *vecs,),
        waits,
        in_specs=[smem_spec()] + [any_spec()] * (4 * group) + [vmem_spec()] * group,
        out_specs=[vmem_spec()] * 2,
        out_shape=[shape_of(batch)] * 2,
        scratch_shapes=[
            pltpu.VMEM((group, full, width), BF16),
            pltpu.VMEM((group, 3, full, width), BF16),
            pltpu.VMEM((3, width, width), F32),
            pltpu.SemaphoreType.DMA((4 * group,)),
        ],
        cost_estimate=cost_of(8),
        name="row_weights",
    )


CHUNK = 512
UP_ROWS, DOWN_ROWS = GROUP * 4, 4 * GROUP


def units_of(parts):
    centred = [part - jnp.mean(part, -1, keepdims=True) for part in parts]
    inverses = [lax.rsqrt(jnp.mean(part * part, -1, keepdims=True) + EPSILON) for part in centred]
    return [part * inverse for part, inverse in zip(centred, inverses)], inverses


def norms_back(upstreams, units, inverses, gain):
    scaled = [upstream * gain for upstream in upstreams]
    means = [jnp.mean(part, -1, keepdims=True) for part in scaled]
    along = [jnp.mean(part * unit, -1, keepdims=True) for part, unit in zip(scaled, units)]
    return [
        inverse * (part - mean - unit * cross)
        for part, mean, cross, unit, inverse in zip(scaled, means, along, units, inverses)
    ]


def row_and_mlp_kernel(pieces, first, last, with_old, cot_at, info_ref, place_ref, *rest):
    afters, cots, rest = rest[:pieces], rest[pieces : 2 * pieces], rest[2 * pieces :]
    row_gain, row_shift, w_query_hbm, w_key_hbm, w_value_hbm = rest[:5]
    rest = rest[5:]
    w_row_hbm, row_bias, gain, shift, w_up_hbm, up_bias, w_down_hbm, down_bias = rest[:8]
    rest = rest[8:]
    if not first:
        (old_up, old_down, old_row, old_vec), rest = rest[:4], rest[4:]
    if with_old:
        old_layers, rest = rest[: pieces - 1], rest[pieces - 1 :]
    kept, rest = rest[:5], rest[5:]
    outs, (mixed_grad_ref, grad_ref, dots_ref), rest = rest[:pieces], rest[pieces : pieces + 3], rest[pieces + 3 :]
    if last:
        (keep_ref, send_ref), rest = rest[:2], rest[2:]
    else:
        (new_up, new_down, new_row, vec_ref), rest = rest[:4], rest[4:]
    q_ref, k_ref, v_ref, extra_ref, normed_ref, w_query, w_key, w_value = rest[:8]
    rest = rest[8:]
    after, cot, mixed, w_row, w_up, w_down, active_all, hidden_grad_all, up_sum, down_sum, row_sum, sems = rest[:12]
    if last:
        vec_ref = rest[12]
    _, rows, width = outs[0].shape
    full = rows * pieces
    wide = w_up.shape[1]
    spans = [slice(piece * rows, (piece + 1) * rows) for piece in range(pieces)]
    count = iter(range(32))

    def start(source, target):
        copy = pltpu.make_async_copy(source, target, sems.at[next(count)])
        copy.start()
        return copy

    get_after = [start(ref, after.at[pl.ds(piece * rows, rows), :]) for piece, ref in enumerate(afters)]
    get_row = [start(w_query_hbm, w_query), start(w_key_hbm, w_key), start(w_value_hbm, w_value)]
    get_out = [start(w_row_hbm, w_row)]
    get_up = [start(w_up_hbm, w_up)]
    get_down = [
        start(ref.at[cot_at[piece]], cot.at[pl.ds(piece * rows, rows), :]) for piece, ref in enumerate(cots)
    ]
    get_down.append(start(w_down_hbm, w_down))
    get_old = [] if first else [start(old_down, down_sum), start(old_up, up_sum), start(old_row, row_sum)]

    for copy in get_after:
        copy.wait()
    units, _ = units_of([after[span, :].astype(F32) for span in spans])
    normed = [(unit * row_gain[...] + row_shift[...]).astype(BF16) for unit in units]
    for copy in get_row:
        copy.wait()
    for weight, ref in ((w_query, q_ref), (w_key, k_ref), (w_value, v_ref)):
        for span, part in zip(spans, normed):
            ref[span, :] = dot_nn(part, weight[...]).astype(BF16)
    for span, part in zip(spans, normed):
        normed_ref[span, :] = part
    puts = [start(source, target) for source, target in zip((q_ref, k_ref, v_ref, normed_ref), kept)]
    lane = lane_of(rows)
    one_lane = jnp.where(lane == 0, 1.0, 0.0)
    query_low = one_lane.astype(BF16)
    biases = jnp.concatenate([key_extra(info_ref, piece, rows, 0) for piece in range(pieces)], 0)
    ones = jnp.ones((full, HEAD), BF16)
    tops = [jnp.zeros((rows, HEAD), F32) for _ in spans]
    totals = [jnp.ones((rows, HEAD), F32) for _ in spans]
    for head in range(HEADS):
        lanes = head_lanes(head)
        own = own_lanes(lane, 1, head)
        key, value = beside(k_ref[:, lanes], biases), beside(v_ref[:, lanes], ones)
        scores = [dot_nt(beside(q_ref[span, lanes], query_low), key) for span in spans]
        highest = [jnp.max(score, -1, keepdims=True) for score in scores]
        grown = [jnp.exp2((score - top) * SCALE).astype(BF16) for score, top in zip(scores, highest)]
        both = [dot_nn(grow, value) for grow in grown]
        for span, found in zip(spans, both):
            mixed[span, lanes] = (found[:, :HEAD] / found[:, HEAD:]).astype(BF16)
        tops = [jnp.where(own, top, old) for top, old in zip(highest, tops)]
        totals = [jnp.where(own, found[:, HEAD:], old) for found, old in zip(both, totals)]
    for span, top, total in zip(spans, tops, totals):
        extra_ref[span, :] = put_thirds(lane, 1, -(top + jnp.log2(total) * (1.0 / SCALE)), one_lane)
    puts.append(start(extra_ref, kept[4]))
    for copy in get_out:
        copy.wait()
    after_b = [
        after[span, :].astype(F32) + dot_nn(mixed[span, :], w_row[...]) + row_bias[...] for span in spans
    ]
    units, inverses = units_of(after_b)
    normed = [(unit * gain[...] + shift[...]).astype(BF16) for unit in units]
    normed_t = jnp.concatenate([part.T for part in normed], 1)
    for copy in get_up + get_down:
        copy.wait()
    keeps = [
        lax.broadcasted_iota(jnp.int32, (rows, 1), 0) + (info_ref[0] ^ piece) * rows < info_ref[1]
        for piece in range(pieces)
    ]
    grad_c = [jnp.where(keep, cot[span, :], jnp.zeros((), BF16)) for keep, span in zip(keeps, spans)]
    grad_t = jnp.concatenate([part.T for part in grad_c], 1)
    ones = jnp.ones((8, full), BF16)
    parts = [slice(at, at + CHUNK) for at in range(0, wide, CHUNK)]

    def widen(lanes):
        hiddens = [dot_nn(part, w_up[:, lanes]) + up_bias[:, lanes] for part in normed]
        return hiddens, [dot_nt(part, w_down[lanes, :]) for part in grad_c]

    c_one, c_three = math.sqrt(2.0 / math.pi), math.sqrt(2.0 / math.pi) * 0.044715
    ahead = widen(parts[0])
    bias_sums = []
    for index, lanes in enumerate(parts):
        hiddens, active_grads = ahead
        if index + 1 < len(parts):
            ahead = widen(parts[index + 1])
        for span, hidden, active_grad in zip(spans, hiddens, active_grads):
            square = hidden * hidden
            half = 0.5 + 0.5 * jnp.tanh(hidden * (c_one + c_three * square))
            active = hidden * half
            slope = half + active * (1.0 - half) * (2.0 * c_one + 6.0 * c_three * square)
            active_all[span, lanes] = active.astype(BF16)
            hidden_grad_all[span, lanes] = (active_grad * slope).astype(BF16)
        if index == 0:
            for copy in get_old:
                copy.wait()
        to_down = dot_nn(grad_t, active_all[:, lanes])
        to_up = dot_nn(normed_t, hidden_grad_all[:, lanes])
        down_sum[:, lanes] = to_down if first else down_sum[:, lanes] + to_down
        up_sum[:, lanes] = to_up if first else up_sum[:, lanes] + to_up
        bias_sums.append(dot_nn(ones, hidden_grad_all[:, lanes])[:1])
    if not last:
        puts += [start(down_sum, new_down), start(up_sum, new_up)]
    upstreams = [dot_nt(hidden_grad_all[span, :], w_up[...]) for span in spans]
    totals = [dot_nn(active_all[span, :], w_down[...]) for span in spans]
    backs = norms_back(upstreams, units, inverses, gain[...])
    grad_b = [part.astype(F32) + back for part, back in zip(grad_c, backs)]
    grad_low = [part.astype(BF16) for part in grad_b]
    if with_old:
        for out, ref in zip(outs[1:], old_layers):
            out[0] = ref[0]
    for out, total, base, keep in zip(outs, totals, after_b, keeps):
        out[out.shape[0] - 1] = jnp.where(keep, total + base + down_bias[...], 0.0).astype(BF16)
    mixed_grads = [dot_nt(part, w_row[...]).astype(BF16) for part in grad_low]
    to_row = dot_tn(mixed[...], jnp.concatenate(grad_low, 0))
    row_sum[...] = to_row if first else row_sum[...] + to_row
    if not last:
        puts.append(start(row_sum, new_row))
    picker = head_picker(1, width)
    for span, part, mixed_grad in zip(spans, grad_b, mixed_grads):
        grad_ref[span, :] = part
        mixed_grad_ref[span, :] = mixed_grad
    dots = [head_dots(part, mixed[span, :], picker) for part, span in zip(mixed_grads, spans)]
    for span, dot in zip(spans, dots):
        dots_ref[span, :] = put_thirds(lane, 1, -dot, jnp.zeros((), F32))
    sums = bias_sums + [
        dot_nn(ones, jnp.concatenate(grad_c, 0))[:1],
        sum(column_sum(upstream * unit) for upstream, unit in zip(upstreams, units)),
        sum(column_sum(upstream) for upstream in upstreams),
        sum(column_sum(part) for part in grad_b),
    ]
    sums = jnp.concatenate(sums, 0)
    vec_ref[...] = sums if first else old_vec[...] + sums
    if last:

        def fill(out, place, quarter, tab):
            start_row = pl.multiple_of(quarter * HEAD + tab * GROUP, GROUP)
            for index, lanes in enumerate(parts):
                out[place, index * GROUP : (index + 1) * GROUP, :] = up_sum[
                    pl.ds(start_row, GROUP), lanes
                ].astype(BF16)
            rows_of = pl.ds(pl.multiple_of(tab * DOWN_ROWS, GROUP), DOWN_ROWS)
            lanes = pl.ds(pl.multiple_of(quarter * CHUNK, CHUNK), CHUNK)
            out[place, UP_ROWS : UP_ROWS + DOWN_ROWS, :] = down_sum[rows_of, lanes].astype(BF16)
            at = UP_ROWS + DOWN_ROWS
            out[place, at : at + GROUP, :] = row_sum[pl.ds(start_row, GROUP), :].astype(BF16)
            out[place, at + GROUP : at + 2 * GROUP, :] = padded_vec(vec_ref)

        fill_batch(place_ref, keep_ref, send_ref, fill, y_first)
    for copy in puts:
        copy.wait()


def row_and_mlp(info, place, afters, cots, cot_at, row_weights, weights, last, old, old_layers, waits=()):
    rows, width = afters[0].shape
    pieces = len(afters)
    full = rows * pieces
    wide = weights[4].shape[1]
    first = old is None
    batch = (BATCH, UP_ROWS + DOWN_ROWS + 2 * GROUP, width)
    sums = [shape_of((width, wide), F32)] * 2 + [shape_of((width, width), F32), shape_of((8, width), F32)]
    weights = (*row_weights, *weights)
    weight_specs = [any_spec() if weight.shape[0] > 1 else vmem_spec() for weight in weights]
    return call(
        functools.partial(row_and_mlp_kernel, pieces, first, last, bool(old_layers), cot_at),
        (info, place, *afters, *cots, *weights, *([] if first else old), *old_layers,),
        waits,
        in_specs=[smem_spec()] * 2
        + [any_spec()] * (2 * pieces)
        + weight_specs
        + ([] if first else [any_spec()] * 3 + [vmem_spec()])
        + [vmem_spec()] * len(old_layers),
        out_specs=[any_spec()] * 5
        + [vmem_spec()] * (pieces + 3)
        + ([vmem_spec()] * 2 if last else [any_spec()] * 3 + [vmem_spec()]),
        out_shape=[shape_of((full, width))] * 4
        + [shape_of((full, HEAD))]
        + [shape_of((1 + (k > 0 and bool(old_layers)), rows, width)) for k in range(pieces)]
        + [shape_of((full, width)), shape_of((full, width), F32), shape_of((full, HEAD))]
        + ([shape_of(batch)] * 2 if last else sums),
        scratch_shapes=[pltpu.VMEM((full, width), BF16)] * 3
        + [pltpu.VMEM((full, HEAD), BF16), pltpu.VMEM((full, width), BF16)]
        + [pltpu.VMEM((width, width), BF16)] * 3
        + [
            pltpu.VMEM((full, width), BF16),
            pltpu.VMEM((full, width), BF16),
            pltpu.VMEM((full, width), BF16),
            pltpu.VMEM((width, width), BF16),
            pltpu.VMEM((width, wide), BF16),
            pltpu.VMEM((wide, width), BF16),
            pltpu.VMEM((full, wide), BF16),
            pltpu.VMEM((full, wide), BF16),
            pltpu.VMEM((width, wide), F32),
            pltpu.VMEM((width, wide), F32),
            pltpu.VMEM((width, width), F32),
            pltpu.SemaphoreType.DMA((32,)),
        ]
        + ([pltpu.VMEM((8, width), F32)] if last else []),
        cost_estimate=cost_of(28),
        name="row_and_mlp",
    )


BATCH = 16


def padded_vec(vec_ref):
    values = vec_ref[...]
    return jnp.concatenate([values, jnp.zeros_like(values)], 0).astype(BF16)


def y_first(x, y, z):
    return (y * 4 + z) * 2 + x


def x_first(x, y, z):
    return (x * 2 + y) * 4 + z


def fill_batch(place_ref, keep_ref, send_ref, fill, order):
    for core, out in ((0, keep_ref), (1, send_ref)):
        for y in range(2):
            for z in range(4):
                for x in range(2):
                    fill(out, order(x, y, z), place_ref[0] ^ (core + 2 * x), place_ref[1] ^ (y + 2 * z))


def row_swap(values, step):
    if step == 0:
        return values
    return lax.ppermute(values, "row", [(index, index ^ step) for index in range(4)])


def tab_swap(values, step):
    return lax.ppermute(values, "tab", [(index, index ^ step) for index in range(8)])


def add(*parts):
    total = parts[0].astype(F32)
    for part in parts[1:]:
        total = total + part.astype(F32)
    return total.astype(BF16)


def gather_near(own):
    return [own] + [tab_swap(own, 2 * z) for z in range(1, 4)]


def tie(first, second):
    return lax.optimization_barrier((first, second))


def finish_kernel(sizes, place_ref, near_ref, far_ref, *outs):
    at = 0
    for (rows, columns, turned), out in zip(sizes, outs):
        parts = columns // 512
        for y, ref in ((0, near_ref), (1, far_ref)):
            for z in range(4):
                tab = place_ref[1] ^ (y + 2 * z)
                for part in range(parts):
                    block = ref[z, at + part * rows : at + (part + 1) * rows, :].astype(F32)
                    span = pl.ds(pl.multiple_of(tab * rows, GROUP), rows)
                    out[span, part * 512 : (part + 1) * 512] = block
        at += rows * parts


def finish(place, near, far, sizes, waits=()):
    return call(
        functools.partial(finish_kernel, sizes),
        (place, near, far,),
        waits,
        in_specs=[smem_spec(), vmem_spec(), vmem_spec()],
        out_specs=[vmem_spec()] * len(sizes),
        out_shape=[shape_of((rows * 8, columns), F32) for rows, columns, _ in sizes],
        cost_estimate=cost_of(2),
        name="finish",
    )


def join_pieces_kernel(group, starts, me_ref, *rest):
    ins, out_ref = rest[:-1], rest[-1]
    for (piece, start), ref in zip(starts, ins):
        out_ref[pl.ds((me_ref[0] ^ piece) * group + start, ref.shape[0])] = ref[...]


def join_pieces(me, blocks, group, waits=()):
    _, rows, width = blocks[0][2].shape
    starts = tuple(block[:2] for block in blocks)
    return call(
        functools.partial(join_pieces_kernel, group, starts),
        (me, *(block[2] for block in blocks)),
        waits,
        in_specs=[smem_spec()] + [vmem_spec()] * len(blocks),
        out_specs=vmem_spec(),
        out_shape=shape_of((4 * group, rows, width)),
        cost_estimate=cost_of(2),
        name="join_pieces",
    )


def by_feature(
    table_cells,
    cotangent,
    row_counts,
    context_counts,
    feat_gain,
    feat_shift,
    feat_query,
    feat_key,
    feat_value,
    feat_out,
    feat_bias,
    row_gain,
    row_shift,
    row_query,
    row_key,
    row_value,
    row_out,
    row_bias,
    mlp_gain,
    mlp_shift,
    up_weight,
    up_bias,
    down_weight,
    down_bias,
):
    count = lax.axis_size("row")
    feats = table_cells.shape[2]
    group = feats // count
    me = lax.axis_index("row").astype(jnp.int32)
    own = me.reshape(1)
    place = jnp.stack([me, lax.axis_index("tab").astype(jnp.int32)])
    info = jnp.stack([me, row_counts[0], context_counts[0]])

    def flat(vector):
        return vector.reshape(1, -1)

    cells = table_cells[0].transpose(1, 0, 2)
    upstream = cotangent[0].transpose(1, 0, 2)
    feat_weights = (flat(feat_gain), flat(feat_shift), feat_query, feat_key, feat_value, feat_out)
    row_weight = (row_query, row_key, row_value)
    mlp_weights = (
        row_out,
        flat(row_bias),
        flat(mlp_gain),
        flat(mlp_shift),
        up_weight,
        flat(up_bias),
        down_weight,
        flat(down_bias),
    )
    cot_own, cot_near, *cot_far = split(own, upstream, group)
    cot_near = row_swap(cot_near, 1)
    cot_first = [row_swap(cot_far[0], 2), row_swap(cot_far[1], 3)]
    forward = feat_forward(own, cells, (*feat_weights, flat(feat_bias)), group)
    after_out, kept_a = list(forward[:feats]), forward[feats:]
    leaving = [after_out[k * group] for k in range(1, count)]
    leaving, (cot_near, cot_first) = tie(leaving, (cot_near, cot_first))
    after_out[group :: group] = leaving
    afters, own_layers, kept_b, backs, mlp_sums, old_layers, late = [], [], [], [], None, [], []
    for j in range(group):
        afters.append([row_swap(after_out[k * group + j], k) for k in range(count)])
        cot = cot_first if j == 0 else [row_swap(cot_far[2 * j], 2), row_swap(cot_far[2 * j + 1], 3)]
        found = row_and_mlp(
            info,
            place,
            afters[j],
            [cot_own, cot_near, *cot],
            (j, j, 0, 0),
            (flat(row_gain), flat(row_shift), *row_weight),
            mlp_weights,
            j == group - 1,
            mlp_sums,
            old_layers,
        )
        kept_b.append(found[:5])
        layer = found[5 : 5 + count]
        own_layers.append(layer[0])
        old_layers = layer[1:] if j == 0 else []
        if j > 0:
            early, late = late, [row_swap(layer[k], k) for k in range(1, count)]
        backs.append(found[5 + count : 8 + count])
        mlp_sums = found[8 + count :]
    mlp_keep, send = mlp_sums
    send, early = tie(send, early)
    mlp_came = row_swap(send, 1)
    mlp_line = tab_swap(add(mlp_keep[8:], mlp_came[8:]), 1)
    grads, d_rows, vecs = [], [], []
    for j in range(group):
        query, key, value, _, extra = kept_b[j]
        if j == 0:
            waits = [backs[-1][2]]
        elif j == 1:
            waits = [vecs[-1], *late]
        else:
            parts = [
                add(*(ref[2 * z : 2 * z + 2] for ref in (mlp_keep, mlp_came, mlp_line))) for z in range(4)
            ]
            waits = [vecs[-1], *grads[0][2:], parts[0]]
        found = row_backward(
            info, (query, key, value, extra), backs[j], afters[j], (flat(row_gain), *row_weight), waits
        )
        d_rows += found[count : count + 3]
        vecs.append(found[count + 3])
        grads.append([row_swap(found[k], k) for k in range(count)])
    parts[1:] = [tab_swap(parts[z], 2 * z) for z in range(1, 4)]
    row_keep, send = row_weights(place, [kept[3] for kept in kept_b], d_rows, vecs, grads[1][2:])
    away = add(*(part[1] for part in parts))
    (away, send), grads[2][1:] = tie((away, send), grads[2][1:])
    row_came = row_swap(send, 1)
    mlp_own = add(*(part[0] for part in parts), row_swap(away, 2))
    mlp_near = gather_near(mlp_own[:-GROUP])
    row_away = add(row_keep[8:], row_came[8:])
    row_line = row_swap(row_away, 2)
    grad_back = [grads[j][k] for k in range(count) for j in range(group)]

    keep, send, *d_all = feat_backward(place, cells, kept_a, grad_back, feat_weights, group, waits=(mlp_own, row_away))
    send, (row_line, mlp_near) = tie(send, (row_line, mlp_near))
    came = row_swap(send, 1)
    mlp_near = jnp.stack(mlp_near)
    mlp_far = tab_swap(mlp_near, 1)
    row_turned = tab_swap(add(row_keep[4:8], row_came[4:8], row_line[4:8]), 1)
    away = add(keep[8:], came[8:])
    cells_grad, mark = cells_backward(
        own, cells, d_all, (flat(feat_gain), feat_query, feat_key, feat_value), grad_back, group, waits=(away,)
    )
    line, mark = tie(row_swap(away, 2), mark)
    away = add(keep[4:8], came[4:8], line[4:8])
    away, (row_turned, mlp_far) = tie(away, (row_turned, mlp_far))
    turned = tab_swap(away, 1)
    parts = [add(*(ref[z] for ref in (row_keep, row_came, row_line, row_turned))) for z in range(4)]
    row_own = add(parts[0], *(tab_swap(parts[z], 2 * z) for z in range(1, 4)))
    row_near = jnp.stack(gather_near(row_own[:-GROUP]))
    parts = [add(*(ref[z] for ref in (keep, came, line, turned))) for z in range(4)]
    row_far = tab_swap(row_near, 1)
    feat_own = add(parts[0], *(tab_swap(parts[z], 2 * z) for z in range(1, 4)))
    feat_near = jnp.stack(gather_near(feat_own[:-GROUP]))
    feat_far = tab_swap(feat_near, 1)
    mlp_vec, row_vec, feat_vec = mlp_own[-GROUP:], row_own[-GROUP:], feat_own[-GROUP:]
    blocks = [(0, j, part) for j, part in enumerate(own_layers)]
    blocks += [(k, 0, part) for k, part in enumerate(early, 1)]
    blocks += [(k, group - 1, part) for k, part in enumerate(late, 1)]
    layer_out = join_pieces(own, blocks, group, (feat_own,))

    up_sum, down_sum, row_out_sum = finish(
        place,
        mlp_near,
        mlp_far,
        ((GROUP, 2048, False), (4 * GROUP, 512, True), (GROUP, 512, False)),
        (feat_own,),
    )
    small = ((GROUP, 512, False),)
    sum_rq, sum_rk, sum_rv = finish(place, row_near, row_far, small * 3, (feat_own,))
    sum_fq, sum_fk, sum_fv, sum_fo = finish(place, feat_near, feat_far, small * 4, (mark,))

    mlp_vec, row_vec, feat_vec = (part.astype(F32) for part in (mlp_vec, row_vec, feat_vec))
    rows = sum_fq.shape[0]

    def quarter(vector):
        return lax.dynamic_slice_in_dim(vector, me * rows, rows, 0)

    return (
        layer_out.transpose(1, 0, 2)[None],
        cells_grad.transpose(1, 0, 2)[None],
        quarter(feat_vec[0]),
        quarter(feat_vec[1]),
        sum_fq,
        sum_fk,
        sum_fv,
        sum_fo,
        quarter(row_vec[2]),
        quarter(row_vec[0]),
        quarter(row_vec[1]),
        sum_rq,
        sum_rk,
        sum_rv,
        row_out_sum,
        quarter(mlp_vec[7]),
        quarter(mlp_vec[5]),
        quarter(mlp_vec[6]),
        up_sum,
        lax.dynamic_index_in_dim(mlp_vec[:4], me, 0, keepdims=False),
        down_sum.T,
        quarter(mlp_vec[4]),
    )


def solution(mesh):
    in_specs = (
        P("tab", "row", None, None),
        P("tab", "row", None, None),
        P("tab"),
        P("tab"),
        P(),
        P(),
        P(),
        P(),
        P(),
        P(),
        P(),
        P(),
        P(),
        P(),
        P(),
        P(),
        P(),
        P(),
        P(),
        P(),
        P(),
        P(),
        P(),
        P(),
    )
    out_specs = (
        P("tab", "row", None, None),
        P("tab", "row", None, None),
        P("row"),
        P("row"),
        P("row", None),
        P("row", None),
        P("row", None),
        P("row", None),
        P("row"),
        P("row"),
        P("row"),
        P("row", None),
        P("row", None),
        P("row", None),
        P("row", None),
        P("row"),
        P("row"),
        P("row"),
        P("row", None),
        P("row"),
        P("row", None),
        P("row"),
    )

    near = (mesh.shape["tab"], mesh.shape["row"]) == (8, 4)
    body = by_feature if near else shards
    return jax.shard_map(body, mesh=mesh, in_specs=in_specs, out_specs=out_specs, check_vma=False)
```

```python
import functools
import math

import jax
import jax.numpy as jnp
from jax import lax
from jax.experimental import pallas as pl
from jax.experimental.pallas import tpu as pltpu
from jax.sharding import PartitionSpec as P

HEADS = 4


EPSILON = 1e-05
NEGATIVE = -1e30


def normalize(values, gain_vec, shift_vec):
    row_mean = jnp.mean(values, -1, keepdims=True)
    centred = values - row_mean
    inverse = lax.rsqrt(jnp.mean(centred * centred, -1, keepdims=True) + EPSILON)
    unit_part = centred * inverse
    return (unit_part * gain_vec + shift_vec, unit_part, inverse)


def normalize_back(upstream, unit_part, inverse, gain_vec):
    scaled = upstream * gain_vec
    inner_part = (
        scaled
        - jnp.mean(scaled, -1, keepdims=True)
        - unit_part * jnp.mean(scaled * unit_part, -1, keepdims=True)
    )
    return (
        inverse * inner_part,
        jnp.sum(upstream * unit_part, axis=(0, 1)),
        jnp.sum(upstream, axis=(0, 1)),
    )


def project(left_side, weight):
    return jnp.einsum("rfd,de->rfe", left_side, weight, preferred_element_type=jnp.float32)


def project_back(upstream, weight):
    return jnp.einsum("rfe,de->rfd", upstream, weight, preferred_element_type=jnp.float32)


def outer_sum(left_side, upstream):
    return jnp.einsum("rfd,rfe->de", left_side, upstream, preferred_element_type=jnp.float32)


def split_heads(values):
    return values.reshape(values.shape[0], values.shape[1], HEADS, values.shape[2] // HEADS)


def join_heads(values):
    return values.reshape(values.shape[0], values.shape[1], values.shape[2] * values.shape[3])


def shards(
    table_cells,
    cotangent,
    row_counts,
    context_counts,
    feat_gain,
    feat_shift,
    feat_query,
    feat_key,
    feat_value,
    feat_out,
    feat_bias,
    row_gain,
    row_shift,
    row_query,
    row_key,
    row_value,
    row_out,
    row_bias,
    mlp_gain,
    mlp_shift,
    up_weight,
    up_bias,
    down_weight,
    down_bias,
):
    source = table_cells[0].astype(jnp.float32)
    local_rows, feat_count, model_width = source.shape
    score_scale = 1.0 / math.sqrt(model_width // HEADS)
    total_rows = local_rows * lax.axis_size("row")
    row_ids = lax.axis_index("row") * local_rows + jnp.arange(local_rows, dtype=jnp.int32)
    row_mask = (row_ids < row_counts[0]).astype(jnp.float32)[:, None, None]
    context_mask = jnp.arange(total_rows, dtype=jnp.int32) < context_counts[0]
    normed_a, unit_a, inverse_a = normalize(source, feat_gain, feat_shift)
    normed_a = normed_a.astype(jnp.bfloat16)
    query_a = split_heads(project(normed_a, feat_query).astype(jnp.bfloat16))
    key_a = split_heads(project(normed_a, feat_key).astype(jnp.bfloat16))
    value_a = split_heads(project(normed_a, feat_value).astype(jnp.bfloat16))
    scores_a = (
        jnp.einsum("rfhd,rghd->rhfg", query_a, key_a, preferred_element_type=jnp.float32)
        * score_scale
    )
    probs_a = jax.nn.softmax(scores_a, -1)
    probs_a_low = probs_a.astype(jnp.bfloat16)
    mixed_a = join_heads(
        jnp.einsum(
            "rhfg,rghd->rfhd", probs_a_low, value_a, preferred_element_type=jnp.float32
        ).astype(jnp.bfloat16)
    )
    after_a = source + project(mixed_a, feat_out) + feat_bias
    normed_b, unit_b, inverse_b = normalize(after_a, row_gain, row_shift)
    normed_b = normed_b.astype(jnp.bfloat16)
    query_b = split_heads(project(normed_b, row_query).astype(jnp.bfloat16))
    key_b = project(normed_b, row_key).astype(jnp.bfloat16)
    value_b = project(normed_b, row_value).astype(jnp.bfloat16)
    key_all, value_all = (
        lax.all_gather(key_b, "row", axis=0, tiled=True),
        lax.all_gather(value_b, "row", axis=0, tiled=True),
    )

    def row_scores(key_whole):
        raw_scores = (
            jnp.einsum(
                "ifhd,jfhd->fhij",
                query_b,
                split_heads(key_whole),
                preferred_element_type=jnp.float32,
            )
            * score_scale
        )
        return jnp.where(context_mask, raw_scores, NEGATIVE)

    scores_b = row_scores(key_all)
    highest = jnp.max(scores_b, -1, keepdims=True)
    log_total = highest + jnp.log(jnp.sum(jnp.exp(scores_b - highest), -1, keepdims=True))
    probs_b_low = jnp.exp(scores_b - log_total).astype(jnp.bfloat16)
    mixed_b = join_heads(
        jnp.einsum(
            "fhij,jfhd->ifhd",
            probs_b_low,
            split_heads(value_all),
            preferred_element_type=jnp.float32,
        ).astype(jnp.bfloat16)
    )
    after_b = after_a + project(mixed_b, row_out) + row_bias
    normed_c, unit_c, inverse_c = normalize(after_b, mlp_gain, mlp_shift)
    normed_c = normed_c.astype(jnp.bfloat16)
    hidden = project(normed_c, up_weight) + up_bias
    active, gelu_pull = jax.vjp(jax.nn.gelu, hidden)
    active = active.astype(jnp.bfloat16)
    after_c = after_b + project(active, down_weight) + down_bias
    layer_out = (after_c * row_mask).astype(jnp.bfloat16)
    grad_c = cotangent[0].astype(jnp.float32) * row_mask
    grad_c_low = grad_c.astype(jnp.bfloat16)
    down_bias_grad = jnp.sum(grad_c, axis=(0, 1))
    down_weight_grad = outer_sum(active, grad_c_low)
    active_grad = project_back(grad_c_low, down_weight)
    hidden_grad = gelu_pull(active_grad)[0].astype(jnp.bfloat16)
    up_bias_grad = jnp.sum(hidden_grad.astype(jnp.float32), axis=(0, 1))
    up_weight_grad = outer_sum(normed_c, hidden_grad)
    back_c, mlp_gain_grad, mlp_shift_grad = normalize_back(
        project_back(hidden_grad, up_weight), unit_c, inverse_c, mlp_gain
    )
    grad_b = grad_c + back_c
    grad_b_low = grad_b.astype(jnp.bfloat16)
    row_bias_grad = jnp.sum(grad_b, axis=(0, 1))
    row_out_grad = outer_sum(mixed_b, grad_b_low)
    mixed_b_grad = split_heads(project_back(grad_b_low, row_out).astype(jnp.bfloat16))
    key_back, value_back = (
        lax.all_gather(key_b, "row", axis=0, tiled=True),
        lax.all_gather(value_b, "row", axis=0, tiled=True),
    )
    probs_full = jnp.exp(row_scores(key_back) - log_total)
    probs_grad = jnp.einsum(
        "ifhd,jfhd->fhij", mixed_b_grad, split_heads(value_back), preferred_element_type=jnp.float32
    )
    row_dot = jnp.sum(probs_full * probs_grad, -1, keepdims=True)
    score_b_grad = (probs_full * (probs_grad - row_dot)).astype(jnp.bfloat16)
    query_b_grad = join_heads(
        (
            jnp.einsum(
                "fhij,jfhd->ifhd",
                score_b_grad,
                split_heads(key_back),
                preferred_element_type=jnp.float32,
            )
            * score_scale
        ).astype(jnp.bfloat16)
    )
    flat_rows = feat_count * HEADS
    log_all, dot_all = (
        lax.all_gather(log_total.reshape(flat_rows, local_rows), "row", axis=1, tiled=True),
        lax.all_gather(row_dot.reshape(flat_rows, local_rows), "row", axis=1, tiled=True),
    )
    own_mask = row_ids < context_counts[0]
    key_own = split_heads(key_b)
    value_own = split_heads(value_b)
    query_piece = lax.all_gather(query_b, "row", axis=0, tiled=True)
    grad_piece = lax.all_gather(mixed_b_grad, "row", axis=0, tiled=True)
    count = query_piece.shape[0]
    log_piece = log_all.reshape(feat_count, HEADS, count, 1)
    dot_piece = dot_all.reshape(feat_count, HEADS, count, 1)
    piece_scores = (
        jnp.einsum("ifhd,jfhd->fhij", query_piece, key_own, preferred_element_type=jnp.float32)
        * score_scale
    )
    piece_scores = jnp.where(own_mask, piece_scores, NEGATIVE)
    piece_probs = jnp.exp(piece_scores - log_piece)
    piece_inner = jnp.einsum(
        "ifhd,jfhd->fhij", grad_piece, value_own, preferred_element_type=jnp.float32
    )
    piece_grad = (piece_probs * (piece_inner - dot_piece)).astype(jnp.bfloat16)
    key_total = (
        jnp.einsum("fhij,ifhd->jfhd", piece_grad, query_piece, preferred_element_type=jnp.float32)
        * score_scale
    )
    value_total = jnp.einsum(
        "fhij,ifhd->jfhd",
        piece_probs.astype(jnp.bfloat16),
        grad_piece,
        preferred_element_type=jnp.float32,
    )
    key_total, value_total = (key_total, value_total)
    key_b_grad = join_heads(key_total).astype(jnp.bfloat16)
    value_b_grad = join_heads(value_total).astype(jnp.bfloat16)
    row_query_grad = outer_sum(normed_b, query_b_grad)
    row_key_grad = outer_sum(normed_b, key_b_grad)
    row_value_grad = outer_sum(normed_b, value_b_grad)
    normed_b_grad = (
        project_back(query_b_grad, row_query)
        + project_back(key_b_grad, row_key)
        + project_back(value_b_grad, row_value)
    )
    back_b, row_gain_grad, row_shift_grad = normalize_back(
        normed_b_grad, unit_b, inverse_b, row_gain
    )
    grad_a = grad_b + back_b
    grad_a_low = grad_a.astype(jnp.bfloat16)
    feat_bias_grad = jnp.sum(grad_a, axis=(0, 1))
    feat_out_grad = outer_sum(mixed_a, grad_a_low)
    mixed_a_grad = split_heads(project_back(grad_a_low, feat_out).astype(jnp.bfloat16))
    probs_a_grad = jnp.einsum(
        "rfhd,rghd->rhfg", mixed_a_grad, value_a, preferred_element_type=jnp.float32
    )
    score_a_grad = (
        probs_a * (probs_a_grad - jnp.sum(probs_a * probs_a_grad, -1, keepdims=True))
    ).astype(jnp.bfloat16)
    query_a_grad = join_heads(
        (
            jnp.einsum("rhfg,rghd->rfhd", score_a_grad, key_a, preferred_element_type=jnp.float32)
            * score_scale
        ).astype(jnp.bfloat16)
    )
    key_a_grad = join_heads(
        (
            jnp.einsum("rhfg,rfhd->rghd", score_a_grad, query_a, preferred_element_type=jnp.float32)
            * score_scale
        ).astype(jnp.bfloat16)
    )
    value_a_grad = join_heads(
        jnp.einsum(
            "rhfg,rfhd->rghd", probs_a_low, mixed_a_grad, preferred_element_type=jnp.float32
        ).astype(jnp.bfloat16)
    )
    feat_query_grad = outer_sum(normed_a, query_a_grad)
    feat_key_grad = outer_sum(normed_a, key_a_grad)
    feat_value_grad = outer_sum(normed_a, value_a_grad)
    normed_a_grad = (
        project_back(query_a_grad, feat_query)
        + project_back(key_a_grad, feat_key)
        + project_back(value_a_grad, feat_value)
    )
    back_a, feat_gain_grad, feat_shift_grad = normalize_back(
        normed_a_grad, unit_a, inverse_a, feat_gain
    )
    cells_grad = (grad_a + back_a).astype(jnp.bfloat16)
    row_summed = (
        lax.psum_scatter(
            feat_gain_grad.astype(jnp.bfloat16), "row", scatter_dimension=0, tiled=True
        ).astype(jnp.float32),
        lax.psum_scatter(
            feat_shift_grad.astype(jnp.bfloat16), "row", scatter_dimension=0, tiled=True
        ).astype(jnp.float32),
        lax.psum_scatter(
            feat_query_grad.astype(jnp.bfloat16), "row", scatter_dimension=0, tiled=True
        ).astype(jnp.float32),
        lax.psum_scatter(
            feat_key_grad.astype(jnp.bfloat16), "row", scatter_dimension=0, tiled=True
        ).astype(jnp.float32),
        lax.psum_scatter(
            feat_value_grad.astype(jnp.bfloat16), "row", scatter_dimension=0, tiled=True
        ).astype(jnp.float32),
        lax.psum_scatter(
            feat_out_grad.astype(jnp.bfloat16), "row", scatter_dimension=0, tiled=True
        ).astype(jnp.float32),
        lax.psum_scatter(
            feat_bias_grad.astype(jnp.bfloat16), "row", scatter_dimension=0, tiled=True
        ).astype(jnp.float32),
        lax.psum_scatter(
            row_gain_grad.astype(jnp.bfloat16), "row", scatter_dimension=0, tiled=True
        ).astype(jnp.float32),
        lax.psum_scatter(
            row_shift_grad.astype(jnp.bfloat16), "row", scatter_dimension=0, tiled=True
        ).astype(jnp.float32),
        lax.psum_scatter(
            row_query_grad.astype(jnp.bfloat16), "row", scatter_dimension=0, tiled=True
        ).astype(jnp.float32),
        lax.psum_scatter(
            row_key_grad.astype(jnp.bfloat16), "row", scatter_dimension=0, tiled=True
        ).astype(jnp.float32),
        lax.psum_scatter(
            row_value_grad.astype(jnp.bfloat16), "row", scatter_dimension=0, tiled=True
        ).astype(jnp.float32),
        lax.psum_scatter(
            row_out_grad.astype(jnp.bfloat16), "row", scatter_dimension=0, tiled=True
        ).astype(jnp.float32),
        lax.psum_scatter(
            row_bias_grad.astype(jnp.bfloat16), "row", scatter_dimension=0, tiled=True
        ).astype(jnp.float32),
        lax.psum_scatter(
            mlp_gain_grad.astype(jnp.bfloat16), "row", scatter_dimension=0, tiled=True
        ).astype(jnp.float32),
        lax.psum_scatter(
            mlp_shift_grad.astype(jnp.bfloat16), "row", scatter_dimension=0, tiled=True
        ).astype(jnp.float32),
        lax.psum_scatter(
            up_weight_grad.astype(jnp.bfloat16), "row", scatter_dimension=0, tiled=True
        ).astype(jnp.float32),
        lax.psum_scatter(
            up_bias_grad.astype(jnp.bfloat16), "row", scatter_dimension=0, tiled=True
        ).astype(jnp.float32),
        lax.psum_scatter(
            down_weight_grad.astype(jnp.bfloat16), "row", scatter_dimension=0, tiled=True
        ).astype(jnp.float32),
        lax.psum_scatter(
            down_bias_grad.astype(jnp.bfloat16), "row", scatter_dimension=0, tiled=True
        ).astype(jnp.float32),
    )
    (
        part_fg,
        part_fs,
        part_fq,
        part_fk,
        part_fv,
        part_fo,
        part_fb,
        part_rg,
        part_rs,
        part_rq,
        part_rk,
        part_rv,
        part_ro,
        part_rb,
        part_mg,
        part_ms,
        part_uw,
        part_ub,
        part_dw,
        part_db,
    ) = row_summed
    summed = (
        lax.psum(part_fg.astype(jnp.bfloat16), "tab").astype(jnp.float32),
        lax.psum(part_fs.astype(jnp.bfloat16), "tab").astype(jnp.float32),
        lax.psum(part_fq.astype(jnp.bfloat16), "tab").astype(jnp.float32),
        lax.psum(part_fk.astype(jnp.bfloat16), "tab").astype(jnp.float32),
        lax.psum(part_fv.astype(jnp.bfloat16), "tab").astype(jnp.float32),
        lax.psum(part_fo.astype(jnp.bfloat16), "tab").astype(jnp.float32),
        lax.psum(part_fb.astype(jnp.bfloat16), "tab").astype(jnp.float32),
        lax.psum(part_rg.astype(jnp.bfloat16), "tab").astype(jnp.float32),
        lax.psum(part_rs.astype(jnp.bfloat16), "tab").astype(jnp.float32),
        lax.psum(part_rq.astype(jnp.bfloat16), "tab").astype(jnp.float32),
        lax.psum(part_rk.astype(jnp.bfloat16), "tab").astype(jnp.float32),
        lax.psum(part_rv.astype(jnp.bfloat16), "tab").astype(jnp.float32),
        lax.psum(part_ro.astype(jnp.bfloat16), "tab").astype(jnp.float32),
        lax.psum(part_rb.astype(jnp.bfloat16), "tab").astype(jnp.float32),
        lax.psum(part_mg.astype(jnp.bfloat16), "tab").astype(jnp.float32),
        lax.psum(part_ms.astype(jnp.bfloat16), "tab").astype(jnp.float32),
        lax.psum(part_uw.astype(jnp.bfloat16), "tab").astype(jnp.float32),
        lax.psum(part_ub.astype(jnp.bfloat16), "tab").astype(jnp.float32),
        lax.psum(part_dw.astype(jnp.bfloat16), "tab").astype(jnp.float32),
        lax.psum(part_db.astype(jnp.bfloat16), "tab").astype(jnp.float32),
    )
    return (
        layer_out[None],
        cells_grad[None],
        summed[0],
        summed[1],
        summed[2],
        summed[3],
        summed[4],
        summed[5],
        summed[6],
        summed[7],
        summed[8],
        summed[9],
        summed[10],
        summed[11],
        summed[12],
        summed[13],
        summed[14],
        summed[15],
        summed[16],
        summed[17],
        summed[18],
        summed[19],
    )


HEAD = 128
GROUP = 16
LOG2E = 1.4426950408889634
F32 = jnp.float32
BF16 = jnp.bfloat16
SCORE = 1.0 / math.sqrt(HEAD)
SCALE = LOG2E * SCORE


def dot_nn(a, b):
    return jnp.dot(a, b, preferred_element_type=F32)


def dot_nt(a, b):
    return lax.dot_general(a, b, (((1,), (1,)), ((), ())), preferred_element_type=F32)


def dot_tn(a, b):
    return lax.dot_general(a, b, (((0,), (0,)), ((), ())), preferred_element_type=F32)


def unit_of(values):
    centred = values - jnp.mean(values, -1, keepdims=True)
    inverse = lax.rsqrt(jnp.mean(centred * centred, -1, keepdims=True) + EPSILON)
    return centred * inverse, inverse


def norm_back(upstream, unit, inverse, gain):
    scaled = upstream * gain
    return inverse * (
        scaled
        - jnp.mean(scaled, -1, keepdims=True)
        - unit * jnp.mean(scaled * unit, -1, keepdims=True)
    )


def column_sum(values):
    return jnp.sum(values, 0, keepdims=True)


def vmem_spec():
    return pl.BlockSpec(memory_space=pltpu.VMEM)


def smem_spec():
    return pl.BlockSpec(memory_space=pltpu.SMEM)


def any_spec():
    return pl.BlockSpec(memory_space=pl.ANY)


def fixed(shape):
    return pl.BlockSpec(shape, lambda *_: (0,) * len(shape))


def shape_of(shape, dtype=BF16):
    return jax.ShapeDtypeStruct(shape, dtype)


def params_of(mib=63):
    return pltpu.CompilerParams(vmem_limit_bytes=mib * 1024 * 1024)


def call(kernel, args, waits, in_specs, **rest):
    count = len(args)

    def body(*refs):
        kernel(*refs[:count], *refs[count + len(waits) :])

    specs = [*in_specs, *[any_spec() for _ in waits]]
    return pl.pallas_call(body, in_specs=specs, compiler_params=params_of(), **rest)(*args, *waits)


def cost_of(microseconds):
    return pl.CostEstimate(flops=int(microseconds * 900e6), bytes_accessed=1024, transcendentals=0)


def head_lanes(head):
    return slice(head * HEAD, (head + 1) * HEAD)


def lane_of(rows):
    return lax.broadcasted_iota(jnp.int32, (rows, HEAD), 1)


def put_thirds(lane, first, values, base):
    high = values.astype(BF16).astype(F32)
    rest = values - high
    middle = rest.astype(BF16).astype(F32)
    turn = (lane - first) % 3
    parts = jnp.where(turn == 0, high, jnp.where(turn == 1, middle, rest - middle))
    return jnp.where((lane >= first) & (lane < first + 3 * HEADS), parts, base).astype(BF16)


def own_lanes(lane, first, head):
    return (lane >= first + 3 * head) & (lane < first + 3 * head + 3)


def head_picker(first, width):
    head = lax.broadcasted_iota(jnp.int32, (width, HEAD), 0) // HEAD
    lane = lax.broadcasted_iota(jnp.int32, (width, HEAD), 1)
    hit = (lane >= first) & (lane < first + 3 * HEADS) & ((lane - first) // 3 == head)
    return jnp.where(hit, 1.0, 0.0).astype(BF16)


def head_dots(left, right, picker):
    product = left.astype(F32) * right.astype(F32)
    high = product.astype(BF16)
    low = (product - high.astype(F32)).astype(BF16)
    return dot_nn(high, picker) + dot_nn(low, picker)


def beside(left, right):
    return jnp.concatenate([left, right], 1)


def split_kernel(group, plan, me_ref, whole_ref, *rest):
    outs, sems = rest[:-1], rest[-1]
    copies = []
    for index, (piece, first, size) in enumerate(plan):
        source = whole_ref.at[pl.ds((me_ref[0] ^ piece) * group + first, size)]
        copies.append(pltpu.make_async_copy(source, outs[index], sems.at[index]))
        copies[-1].start()
    for copy in copies:
        copy.wait()


def split(me, whole, group, plan, waits=()):
    _, rows, width = whole.shape
    return call(
        functools.partial(split_kernel, group, plan),
        (me, whole),
        waits,
        in_specs=[smem_spec(), any_spec()],
        out_specs=[vmem_spec()] * len(plan),
        out_shape=[shape_of((size, rows, width)) for _, _, size in plan],
        scratch_shapes=[pltpu.SemaphoreType.DMA((len(plan),))],
        cost_estimate=cost_of(2),
        name="split",
    )


def query_mask(size):
    row = lax.broadcasted_iota(jnp.int32, (size, HEAD), 0) % GROUP
    lane = lane_of(size)
    return jnp.where((lane < GROUP) & (lane != row), NEGATIVE, 0.0)


def key_mask(size, head):
    row = lax.broadcasted_iota(jnp.int32, (size, HEAD), 0) % GROUP
    lane = lane_of(size)
    return jnp.where((lane == row) | own_lanes(lane, GROUP, head), 1.0, 0.0).astype(BF16)


def gather_cells(group, me_ref, cells_ref):
    feats, rows, _ = cells_ref.shape
    return jnp.concatenate(
        [
            cells_ref[(me_ref[0] ^ (index // group)) * group + index % group, part : part + GROUP, :]
            for part in range(0, rows, GROUP)
            for index in range(feats)
        ],
        0,
    )


def feat_forward_kernel(
    group, plan, me_ref, cells_ref, cot_ref, gain, shift, w_query, w_key, w_value, w_out, bias, *rest
):
    feats, rows, width = cells_ref.shape
    outs = rest[:feats]
    q_ref, k_ref, v_ref, mixed_ref, extra_ref = rest[feats : feats + 5]
    for (piece, first, count), out in zip(plan, rest[feats + 5 :]):
        out[...] = cot_ref[pl.ds((me_ref[0] ^ piece) * group + first, count)]
    size, parts = feats * GROUP, rows // GROUP
    cells = gather_cells(group, me_ref, cells_ref)
    unit, _ = unit_of(cells.astype(F32))
    normed = (unit * gain[...] + shift[...]).astype(BF16)
    q_ref[...] = dot_nn(normed, w_query[...]).astype(BF16)
    k_ref[...] = dot_nn(normed, w_key[...]).astype(BF16)
    v_ref[...] = dot_nn(normed, w_value[...]).astype(BF16)
    mask = query_mask(size)
    mask_low = mask.astype(BF16)
    keys = [key_mask(size, head) for head in range(HEADS)]
    lane = lane_of(size)
    ones = jnp.ones((size, HEAD), BF16)
    pairs = [
        (slice(part * size, (part + 1) * size), head_lanes(head), head)
        for part in range(parts)
        for head in range(HEADS)
    ]
    scores = [
        dot_nt(beside(q_ref[span, lanes], mask_low), beside(k_ref[span, lanes], keys[head]))
        for span, lanes, head in pairs
    ]
    tops = [jnp.max(score, -1, keepdims=True) for score in scores]
    grown = [jnp.exp2((score - top) * SCALE).astype(BF16) for score, top in zip(scores, tops)]
    both = [dot_nn(grow, beside(v_ref[span, lanes], ones)) for (span, lanes, _), grow in zip(pairs, grown)]
    for (span, lanes, _), found in zip(pairs, both):
        mixed_ref[span, lanes] = (found[:, :HEAD] / found[:, HEAD:]).astype(BF16)
    for part in range(parts):
        top, total = jnp.zeros((size, HEAD), F32), jnp.ones((size, HEAD), F32)
        for head in range(HEADS):
            own = own_lanes(lane, GROUP, head)
            top = jnp.where(own, tops[part * HEADS + head], top)
            total = jnp.where(own, both[part * HEADS + head][:, HEAD:], total)
        minus = -(top + jnp.log2(total) * (1.0 / SCALE))
        extra_ref[part * size : (part + 1) * size, :] = put_thirds(lane, GROUP, minus, mask)
    after = cells.astype(F32) + dot_nn(mixed_ref[...], w_out[...]) + bias[...]
    after = after.astype(BF16)
    for part in range(parts):
        for index in range(feats):
            start = part * size + index * GROUP
            outs[index][part * GROUP : (part + 1) * GROUP, :] = after[start : start + GROUP]


def feat_forward(me, cells, cot, weights, group, plan, block=64, waits=()):
    feats, rows, width = cells.shape
    tokens = block * feats
    vector, whole = fixed((1, width)), fixed((width, width))
    return call(
        functools.partial(feat_forward_kernel, group, plan),
        (me, cells, cot, *weights),
        waits,
        grid=(rows // block,),
        in_specs=[smem_spec()]
        + [pl.BlockSpec((feats, block, width), lambda i: (0, i, 0))] * 2
        + [vector, vector, whole, whole, whole, whole, vector],
        out_specs=[pl.BlockSpec((block, width), lambda i: (i, 0))] * feats
        + [pl.BlockSpec((tokens, width), lambda i: (i, 0))] * 4
        + [pl.BlockSpec((tokens, HEAD), lambda i: (i, 0))]
        + [pl.BlockSpec((size, block, width), lambda i: (0, i, 0)) for _, _, size in plan],
        out_shape=[shape_of((rows, width))] * feats
        + [shape_of((rows * feats, width))] * 4
        + [shape_of((rows * feats, HEAD))]
        + [shape_of((size, rows, width)) for _, _, size in plan],
        cost_estimate=cost_of(15),
        name="feat_forward",
    )


def feat_backward_kernel(
    group,
    place_ref,
    cells_ref,
    q_ref,
    k_ref,
    v_ref,
    mixed_ref,
    extra_ref,
    gain,
    shift,
    w_query,
    w_key,
    w_value,
    w_out,
    *rest,
):
    feats, rows, width = cells_ref.shape
    grads, rest = rest[:feats], rest[feats:]
    keep_ref, send_ref, d_query, d_key, d_value, sum_query, sum_key, sum_value, sum_out, vec_ref = rest
    parts, size = rows // GROUP, feats * GROUP

    @pl.when(pl.program_id(0) == 0)
    def _():
        for ref in (sum_query, sum_key, sum_value, sum_out, vec_ref):
            ref[...] = jnp.zeros_like(ref)

    grad_low = jnp.concatenate(
        [ref[part * GROUP : (part + 1) * GROUP, :] for part in range(parts) for ref in grads], 0
    )
    sum_out[...] += dot_tn(mixed_ref[...], grad_low)
    mixed_grad = dot_nt(grad_low, w_out[...]).astype(BF16)
    dots = head_dots(mixed_grad, mixed_ref[...], head_picker(GROUP, width))
    dots = put_thirds(lane_of(dots.shape[0]), GROUP, -dots, jnp.zeros((), F32))
    keys = [key_mask(size, head) for head in range(HEADS)]
    pairs = [
        (slice(part * size, (part + 1) * size), head_lanes(head), head)
        for part in range(parts)
        for head in range(HEADS)
    ]
    scores = [dot_nt(beside(k_ref[s, l], keys[h]), beside(q_ref[s, l], extra_ref[s, :])) for s, l, h in pairs]
    inners = [dot_nt(beside(v_ref[s, l], keys[h]), beside(mixed_grad[s, l], dots[s])) for s, l, h in pairs]
    probs = [jnp.exp2(score * SCALE) for score in scores]
    score_grads = [(prob * inner).astype(BF16) for prob, inner in zip(probs, inners)]
    for (s, l, _), prob in zip(pairs, probs):
        d_value[s, l] = dot_nn(prob.astype(BF16), mixed_grad[s, l]).astype(BF16)
    for (s, l, _), score_grad in zip(pairs, score_grads):
        d_key[s, l] = (dot_nn(score_grad, q_ref[s, l]) * SCORE).astype(BF16)
    for (s, l, _), score_grad in zip(pairs, score_grads):
        d_query[s, l] = (dot_tn(score_grad, k_ref[s, l]) * SCORE).astype(BF16)
    unit, _ = unit_of(gather_cells(group, place_ref, cells_ref).astype(F32))
    normed_t = (unit * gain[...] + shift[...]).astype(BF16).T
    sum_query[...] += dot_nn(normed_t, d_query[...])
    sum_key[...] += dot_nn(normed_t, d_key[...])
    sum_value[...] += dot_nn(normed_t, d_value[...])
    vec_ref[2:3, :] += column_sum(d_query[...].astype(F32))
    vec_ref[3:4, :] += column_sum(d_key[...].astype(F32))
    vec_ref[4:5, :] += column_sum(d_value[...].astype(F32))

    @pl.when(pl.program_id(0) == pl.num_programs(0) - 1)
    def _():
        ones = jnp.ones((8, width), BF16)
        crossed, plain = jnp.zeros((8, width), F32), jnp.zeros((8, width), F32)
        for index, (weight, total) in enumerate(
            ((w_query, sum_query), (w_key, sum_key), (w_value, sum_value))
        ):
            product = weight[...].astype(F32) * total[...]
            column = jnp.broadcast_to(vec_ref[2 + index : 3 + index, :], (8, width))
            for _ in range(3):
                crossed = crossed + dot_nt(ones, product.astype(BF16))
                product = product - product.astype(BF16).astype(F32)
                plain = plain + dot_nt(column.astype(BF16), weight[...])
                column = column - column.astype(BF16).astype(F32)
        vec_ref[0:1, :] = (crossed[:1] - shift[...] * plain[:1]) / gain[...]
        vec_ref[1:2, :] = plain[:1]

        def fill(out, place, quarter, piece):
            start = pl.multiple_of(quarter * HEAD + piece * GROUP, GROUP)
            for index, ref in enumerate((sum_query, sum_key, sum_value, sum_out)):
                out[place, index * GROUP : (index + 1) * GROUP, :] = ref[pl.ds(start, GROUP), :].astype(BF16)
            out[place, 4 * GROUP : 5 * GROUP, :] = padded_vec(vec_ref)

        fill_batch(place_ref, keep_ref, send_ref, fill, x_first)


def feat_backward(place, cells, kept, grads, weights, group, block=64, waits=()):
    feats, rows, width = cells.shape
    tokens = block * feats
    vector, whole = fixed((1, width)), fixed((width, width))
    batch = (BATCH, 5 * GROUP, width)
    row_block = pl.BlockSpec((tokens, width), lambda i: (i, 0))
    return call(
        functools.partial(feat_backward_kernel, group),
        (place, cells, *kept, *weights, *grads,),
        waits,
        grid=(rows // block,),
        in_specs=[smem_spec(), pl.BlockSpec((feats, block, width), lambda i: (0, i, 0))]
        + [row_block] * 4
        + [pl.BlockSpec((tokens, HEAD), lambda i: (i, 0))]
        + [vector, vector, whole, whole, whole, whole]
        + [pl.BlockSpec((block, width), lambda i: (i, 0))] * feats,
        out_specs=[fixed(batch)] * 2 + [row_block] * 3,
        out_shape=[shape_of(batch)] * 2 + [shape_of((rows * feats, width))] * 3,
        scratch_shapes=[pltpu.VMEM((width, width), F32)] * 4 + [pltpu.VMEM((8, width), F32)],
        cost_estimate=cost_of(20),
        name="feat_backward",
    )


def cells_backward_kernel(group, me_ref, cells_ref, d_query, d_key, d_value, gain, w_query, w_key, w_value, *rest):
    grads, (out_ref, mark_ref) = rest[:-2], rest[-2:]
    feats, rows, _ = cells_ref.shape
    mark_ref[...] = jnp.zeros_like(mark_ref)
    parts, size = rows // GROUP, feats * GROUP
    unit, inverse = unit_of(gather_cells(group, me_ref, cells_ref).astype(F32))
    upstream = (
        dot_nt(d_query[...], w_query[...])
        + dot_nt(d_key[...], w_key[...])
        + dot_nt(d_value[...], w_value[...])
    )
    back = norm_back(upstream, unit, inverse, gain[...])
    for index in range(feats):
        true = (me_ref[0] ^ (index // group)) * group + index % group
        for part in range(parts):
            start = part * size + index * GROUP
            span = slice(part * GROUP, (part + 1) * GROUP)
            cells = grads[index][span, :].astype(F32) + back[start : start + GROUP]
            out_ref[true, span, :] = cells.astype(BF16)


def cells_backward(me, cells, d_all, weights, grads, group, block=64, waits=()):
    feats, rows, width = cells.shape
    tokens = block * feats
    vector, whole = fixed((1, width)), fixed((width, width))
    row_block = pl.BlockSpec((tokens, width), lambda i: (i, 0))
    by_rows = pl.BlockSpec((feats, block, width), lambda i: (0, i, 0))
    return call(
        functools.partial(cells_backward_kernel, group),
        (me, cells, *d_all, *weights, *grads,),
        waits,
        grid=(rows // block,),
        in_specs=[smem_spec(), by_rows]
        + [row_block] * 3
        + [vector, whole, whole, whole]
        + [pl.BlockSpec((block, width), lambda i: (i, 0))] * feats,
        out_specs=[by_rows, fixed((8, HEAD))],
        out_shape=[shape_of((feats, rows, width)), shape_of((8, HEAD), F32)],
        cost_estimate=cost_of(12),
        name="cells_backward",
    )


def key_extra(info_ref, piece, rows, head):
    first = (info_ref[0] ^ piece) * rows
    row = lax.broadcasted_iota(jnp.int32, (rows, HEAD), 0) + first
    lane = lane_of(rows)
    bias = jnp.where(row < info_ref[2], 0.0, NEGATIVE)
    return jnp.where(lane == 0, bias, jnp.where(own_lanes(lane, 1, head), 1.0, 0.0)).astype(BF16)


def row_backward_kernel(pieces, info_ref, *rest):
    q_ref, k_ref, v_ref, extra_ref, mixed_grad_ref, dots_ref, rest = *rest[:6], rest[6:]
    afters, rest = rest[:pieces], rest[pieces:]
    grad_hbm, gain, w_query_hbm, w_key_hbm, w_value_hbm = rest[:5]
    outs, rest = rest[5 : 5 + pieces], rest[5 + pieces :]
    d_query, d_key, d_value, vec_ref = rest[:4]
    after, grad, w_query, w_key, w_value, query_all, key_all, value_all, query_sum, sems = rest[4:]
    rows, width = outs[0].shape
    full = rows * pieces
    head = pl.program_id(0)
    copies = [
        pltpu.make_async_copy(afters[piece], after.at[pl.ds(piece * rows, rows), :], sems.at[piece])
        for piece in range(pieces)
    ]
    copies.append(pltpu.make_async_copy(grad_hbm, grad, sems.at[pieces]))
    for index, (source, target) in enumerate(
        ((w_query_hbm, w_query), (w_key_hbm, w_key), (w_value_hbm, w_value))
    ):
        copies.append(pltpu.make_async_copy(source, target, sems.at[pieces + 1 + index]))

    @pl.when(head == 0)
    def _():
        for copy in copies:
            copy.start()

    query = beside(q_ref[...], extra_ref[...])
    upstream = beside(mixed_grad_ref[...], dots_ref[...])
    spans = [slice(index * rows, (index + 1) * rows) for index in range(pieces)]
    keys = [key_extra(info_ref, index, rows, head) for index in range(pieces)]
    scores = [dot_nt(beside(k_ref[span, :], extra), query) for span, extra in zip(spans, keys)]
    inners = [dot_nt(beside(v_ref[span, :], extra), upstream) for span, extra in zip(spans, keys)]
    probs = [jnp.exp2(score * SCALE) for score in scores]
    score_grads = [(prob * inner).astype(BF16) for prob, inner in zip(probs, inners)]
    for span, prob in zip(spans, probs):
        value_all[head, span, :] = dot_nn(prob.astype(BF16), mixed_grad_ref[...]).astype(BF16)
    for span, score_grad in zip(spans, score_grads):
        key_all[head, span, :] = (dot_nn(score_grad, q_ref[...]) * SCORE).astype(BF16)
    query_sum[...] = dot_nn(k_ref[...].T, jnp.concatenate(score_grads, 0)).T
    query_all[head] = (query_sum[...] * SCORE).astype(BF16)

    @pl.when(head == HEADS - 1)
    def _():
        for copy in copies:
            copy.wait()
        vec_ref[...] = jnp.zeros_like(vec_ref)
        for piece in range(pieces):
            span = slice(piece * rows, (piece + 1) * rows)
            unit, inverse = unit_of(after[span, :].astype(F32))
            upstream = None
            for ref, weight, out in (
                (query_all, w_query, d_query),
                (key_all, w_key, d_key),
                (value_all, w_value, d_value),
            ):
                flat = jnp.concatenate([ref[index, span, :] for index in range(HEADS)], 1)
                out[span, :] = flat
                part = dot_nt(flat, weight[...])
                upstream = part if upstream is None else upstream + part
            grad_a = grad[span, :] + norm_back(upstream, unit, inverse, gain[...])
            outs[piece][...] = grad_a.astype(BF16)
            vec_ref[0:1, :] += column_sum(upstream * unit)
            vec_ref[1:2, :] += column_sum(upstream)
            vec_ref[2:3, :] += column_sum(grad_a)


def row_backward(info, kept, back, afters, weights, waits=()):
    rows, width = afters[0].shape
    count = len(afters)
    full = rows * count
    query, key, value, extra = kept
    mixed_grad, grad_b, dots = back
    by_head = pl.BlockSpec((full, HEAD), lambda h: (0, h))
    return call(
        functools.partial(row_backward_kernel, count),
        (info, query, key, value, extra, mixed_grad, dots, *afters, grad_b, *weights,),
        waits,
        grid=(HEADS,),
        in_specs=[smem_spec()]
        + [by_head] * 3
        + [fixed((full, HEAD)), by_head, fixed((full, HEAD))]
        + [any_spec()] * (count + 1)
        + [fixed((1, width))]
        + [any_spec()] * 3,
        out_specs=[fixed((rows, width))] * count + [fixed((full, width))] * 3 + [fixed((8, width))],
        out_shape=[shape_of((rows, width))] * count + [shape_of((full, width))] * 3 + [shape_of((8, width), F32)],
        scratch_shapes=[
            pltpu.VMEM((full, width), BF16),
            pltpu.VMEM((full, width), F32),
            pltpu.VMEM((width, width), BF16),
            pltpu.VMEM((width, width), BF16),
            pltpu.VMEM((width, width), BF16),
            pltpu.VMEM((HEADS, full, HEAD), BF16),
            pltpu.VMEM((HEADS, full, HEAD), BF16),
            pltpu.VMEM((HEADS, full, HEAD), BF16),
            pltpu.VMEM((full, HEAD), F32),
            pltpu.SemaphoreType.DMA((count + 4,)),
        ],
        cost_estimate=cost_of(15),
        name="row_backward",
    )


def row_weights_kernel(group, place_ref, *rest):
    normeds, rest = rest[:group], rest[group:]
    grads, rest = rest[: 3 * group], rest[3 * group :]
    vecs, rest = rest[:group], rest[group:]
    keep_ref, send_ref, normed, grad, totals, sems = rest
    copies = []
    for j in range(group):
        mine = [pltpu.make_async_copy(normeds[j], normed.at[j], sems.at[4 * j])]
        for index in range(3):
            mine.append(pltpu.make_async_copy(grads[3 * j + index], grad.at[j, index], sems.at[4 * j + 1 + index]))
        for copy in mine:
            copy.start()
        copies.append(mine)
    for j in range(group):
        for copy in copies[j]:
            copy.wait()
        turned = normed[j].T
        for index in range(3):
            part = dot_nn(turned, grad[j, index])
            if j == 0:
                totals[index] = part
            else:
                totals[index] += part
    vec = sum((ref[...] for ref in vecs[1:]), vecs[0][...])

    def fill(out, place, quarter, piece):
        start = pl.multiple_of(quarter * HEAD + piece * GROUP, GROUP)
        for index in range(3):
            out[place, index * GROUP : (index + 1) * GROUP, :] = totals[index, pl.ds(start, GROUP), :].astype(BF16)
        out[place, 3 * GROUP : 4 * GROUP, :] = padded_vec(vec)

    fill_batch(place_ref, keep_ref, send_ref, fill, x_first)


def row_weights(place, normeds, grads, vecs, waits=()):
    group = len(normeds)
    full, width = normeds[0].shape
    batch = (BATCH, 4 * GROUP, width)
    return call(
        functools.partial(row_weights_kernel, group),
        (place, *normeds, *grads, *vecs,),
        waits,
        in_specs=[smem_spec()] + [any_spec()] * (4 * group) + [vmem_spec()] * group,
        out_specs=[vmem_spec()] * 2,
        out_shape=[shape_of(batch)] * 2,
        scratch_shapes=[
            pltpu.VMEM((group, full, width), BF16),
            pltpu.VMEM((group, 3, full, width), BF16),
            pltpu.VMEM((3, width, width), F32),
            pltpu.SemaphoreType.DMA((4 * group,)),
        ],
        cost_estimate=cost_of(8),
        name="row_weights",
    )


CHUNK = 512
UP_ROWS, DOWN_ROWS = GROUP * 4, 4 * GROUP


def units_of(parts):
    centred = [part - jnp.mean(part, -1, keepdims=True) for part in parts]
    inverses = [lax.rsqrt(jnp.mean(part * part, -1, keepdims=True) + EPSILON) for part in centred]
    return [part * inverse for part, inverse in zip(centred, inverses)], inverses


def norms_back(upstreams, units, inverses, gain):
    scaled = [upstream * gain for upstream in upstreams]
    means = [jnp.mean(part, -1, keepdims=True) for part in scaled]
    along = [jnp.mean(part * unit, -1, keepdims=True) for part, unit in zip(scaled, units)]
    return [
        inverse * (part - mean - unit * cross)
        for part, mean, cross, unit, inverse in zip(scaled, means, along, units, inverses)
    ]


def row_and_mlp_kernel(pieces, first, last, with_old, cot_at, info_ref, place_ref, *rest):
    afters, cots, rest = rest[:pieces], rest[pieces : 2 * pieces], rest[2 * pieces :]
    row_gain, row_shift, w_query_hbm, w_key_hbm, w_value_hbm = rest[:5]
    rest = rest[5:]
    w_row_hbm, row_bias, gain, shift, w_up_hbm, up_bias, w_down_hbm, down_bias = rest[:8]
    rest = rest[8:]
    if not first:
        (old_up, old_down, old_row, old_vec), rest = rest[:4], rest[4:]
    if with_old:
        old_layers, rest = rest[: pieces - 1], rest[pieces - 1 :]
    kept, rest = rest[:5], rest[5:]
    outs, (mixed_grad_ref, grad_ref, dots_ref), rest = rest[:pieces], rest[pieces : pieces + 3], rest[pieces + 3 :]
    if last:
        (keep_ref, send_ref), rest = rest[:2], rest[2:]
    else:
        (new_up, new_down, new_row, vec_ref), rest = rest[:4], rest[4:]
    q_ref, k_ref, v_ref, extra_ref, normed_ref, w_query, w_key, w_value = rest[:8]
    rest = rest[8:]
    after, cot, mixed, w_row, w_up, w_down, active_all, hidden_grad_all, up_sum, down_sum, row_sum, sems = rest[:12]
    if last:
        vec_ref = rest[12]
    _, rows, width = outs[0].shape
    full = rows * pieces
    wide = w_up.shape[1]
    spans = [slice(piece * rows, (piece + 1) * rows) for piece in range(pieces)]
    count = iter(range(32))

    def start(source, target):
        copy = pltpu.make_async_copy(source, target, sems.at[next(count)])
        copy.start()
        return copy

    get_after = [start(ref, after.at[pl.ds(piece * rows, rows), :]) for piece, ref in enumerate(afters)]
    get_row = [start(w_query_hbm, w_query), start(w_key_hbm, w_key), start(w_value_hbm, w_value)]
    get_out = [start(w_row_hbm, w_row)]
    get_up = [start(w_up_hbm, w_up)]
    get_down = [
        start(ref.at[cot_at[piece]], cot.at[pl.ds(piece * rows, rows), :]) for piece, ref in enumerate(cots)
    ]
    get_down.append(start(w_down_hbm, w_down))
    get_old = [] if first else [start(old_down, down_sum), start(old_up, up_sum), start(old_row, row_sum)]

    for copy in get_after:
        copy.wait()
    units, _ = units_of([after[span, :].astype(F32) for span in spans])
    normed = [(unit * row_gain[...] + row_shift[...]).astype(BF16) for unit in units]
    for copy in get_row:
        copy.wait()
    for weight, ref in ((w_query, q_ref), (w_key, k_ref), (w_value, v_ref)):
        for span, part in zip(spans, normed):
            ref[span, :] = dot_nn(part, weight[...]).astype(BF16)
    for span, part in zip(spans, normed):
        normed_ref[span, :] = part
    puts = [start(source, target) for source, target in zip((q_ref, k_ref, v_ref, normed_ref), kept)]
    lane = lane_of(rows)
    one_lane = jnp.where(lane == 0, 1.0, 0.0)
    query_low = one_lane.astype(BF16)
    biases = jnp.concatenate([key_extra(info_ref, piece, rows, 0) for piece in range(pieces)], 0)
    ones = jnp.ones((full, HEAD), BF16)
    tops = [jnp.zeros((rows, HEAD), F32) for _ in spans]
    totals = [jnp.ones((rows, HEAD), F32) for _ in spans]
    for head in range(HEADS):
        lanes = head_lanes(head)
        own = own_lanes(lane, 1, head)
        key, value = beside(k_ref[:, lanes], biases), beside(v_ref[:, lanes], ones)
        scores = [dot_nt(beside(q_ref[span, lanes], query_low), key) for span in spans]
        highest = [jnp.max(score, -1, keepdims=True) for score in scores]
        grown = [jnp.exp2((score - top) * SCALE).astype(BF16) for score, top in zip(scores, highest)]
        both = [dot_nn(grow, value) for grow in grown]
        for span, found in zip(spans, both):
            mixed[span, lanes] = (found[:, :HEAD] / found[:, HEAD:]).astype(BF16)
        tops = [jnp.where(own, top, old) for top, old in zip(highest, tops)]
        totals = [jnp.where(own, found[:, HEAD:], old) for found, old in zip(both, totals)]
    for span, top, total in zip(spans, tops, totals):
        extra_ref[span, :] = put_thirds(lane, 1, -(top + jnp.log2(total) * (1.0 / SCALE)), one_lane)
    puts.append(start(extra_ref, kept[4]))
    for copy in get_out:
        copy.wait()
    after_b = [
        after[span, :].astype(F32) + dot_nn(mixed[span, :], w_row[...]) + row_bias[...] for span in spans
    ]
    units, inverses = units_of(after_b)
    normed = [(unit * gain[...] + shift[...]).astype(BF16) for unit in units]
    normed_t = jnp.concatenate([part.T for part in normed], 1)
    for copy in get_up + get_down:
        copy.wait()
    keeps = [
        lax.broadcasted_iota(jnp.int32, (rows, 1), 0) + (info_ref[0] ^ piece) * rows < info_ref[1]
        for piece in range(pieces)
    ]
    grad_c = [jnp.where(keep, cot[span, :], jnp.zeros((), BF16)) for keep, span in zip(keeps, spans)]
    grad_t = jnp.concatenate([part.T for part in grad_c], 1)
    ones = jnp.ones((8, full), BF16)
    parts = [slice(at, at + CHUNK) for at in range(0, wide, CHUNK)]

    def widen(lanes):
        hiddens = [dot_nn(part, w_up[:, lanes]) + up_bias[:, lanes] for part in normed]
        return hiddens, [dot_nt(part, w_down[lanes, :]) for part in grad_c]

    c_one, c_three = math.sqrt(2.0 / math.pi), math.sqrt(2.0 / math.pi) * 0.044715
    ahead = widen(parts[0])
    bias_sums = []
    for index, lanes in enumerate(parts):
        hiddens, active_grads = ahead
        if index + 1 < len(parts):
            ahead = widen(parts[index + 1])
        for span, hidden, active_grad in zip(spans, hiddens, active_grads):
            square = hidden * hidden
            half = 0.5 + 0.5 * jnp.tanh(hidden * (c_one + c_three * square))
            active = hidden * half
            slope = half + active * (1.0 - half) * (2.0 * c_one + 6.0 * c_three * square)
            active_all[span, lanes] = active.astype(BF16)
            hidden_grad_all[span, lanes] = (active_grad * slope).astype(BF16)
        if index == 0:
            for copy in get_old:
                copy.wait()
        to_down = dot_nn(grad_t, active_all[:, lanes])
        to_up = dot_nn(normed_t, hidden_grad_all[:, lanes])
        down_sum[:, lanes] = to_down if first else down_sum[:, lanes] + to_down
        up_sum[:, lanes] = to_up if first else up_sum[:, lanes] + to_up
        bias_sums.append(dot_nn(ones, hidden_grad_all[:, lanes])[:1])
    if not last:
        puts += [start(down_sum, new_down), start(up_sum, new_up)]
    upstreams = [dot_nt(hidden_grad_all[span, :], w_up[...]) for span in spans]
    totals = [dot_nn(active_all[span, :], w_down[...]) for span in spans]
    backs = norms_back(upstreams, units, inverses, gain[...])
    grad_b = [part.astype(F32) + back for part, back in zip(grad_c, backs)]
    grad_low = [part.astype(BF16) for part in grad_b]
    if with_old:
        for out, ref in zip(outs[1:], old_layers):
            out[0] = ref[0]
    for out, total, base, keep in zip(outs, totals, after_b, keeps):
        out[out.shape[0] - 1] = jnp.where(keep, total + base + down_bias[...], 0.0).astype(BF16)
    mixed_grads = [dot_nt(part, w_row[...]).astype(BF16) for part in grad_low]
    to_row = dot_tn(mixed[...], jnp.concatenate(grad_low, 0))
    row_sum[...] = to_row if first else row_sum[...] + to_row
    if not last:
        puts.append(start(row_sum, new_row))
    picker = head_picker(1, width)
    for span, part, mixed_grad in zip(spans, grad_b, mixed_grads):
        grad_ref[span, :] = part
        mixed_grad_ref[span, :] = mixed_grad
    dots = [head_dots(part, mixed[span, :], picker) for part, span in zip(mixed_grads, spans)]
    for span, dot in zip(spans, dots):
        dots_ref[span, :] = put_thirds(lane, 1, -dot, jnp.zeros((), F32))
    sums = bias_sums + [
        dot_nn(ones, jnp.concatenate(grad_c, 0))[:1],
        sum(column_sum(upstream * unit) for upstream, unit in zip(upstreams, units)),
        sum(column_sum(upstream) for upstream in upstreams),
        sum(column_sum(part) for part in grad_b),
    ]
    sums = jnp.concatenate(sums, 0)
    vec_ref[...] = sums if first else old_vec[...] + sums
    if last:

        def fill(out, place, quarter, tab):
            start_row = pl.multiple_of(quarter * HEAD + tab * GROUP, GROUP)
            for index, lanes in enumerate(parts):
                out[place, index * GROUP : (index + 1) * GROUP, :] = up_sum[
                    pl.ds(start_row, GROUP), lanes
                ].astype(BF16)
            rows_of = pl.ds(pl.multiple_of(tab * DOWN_ROWS, GROUP), DOWN_ROWS)
            lanes = pl.ds(pl.multiple_of(quarter * CHUNK, CHUNK), CHUNK)
            out[place, UP_ROWS : UP_ROWS + DOWN_ROWS, :] = down_sum[rows_of, lanes].astype(BF16)
            at = UP_ROWS + DOWN_ROWS
            out[place, at : at + GROUP, :] = row_sum[pl.ds(start_row, GROUP), :].astype(BF16)
            out[place, at + GROUP : at + 2 * GROUP, :] = padded_vec(vec_ref)

        fill_batch(place_ref, keep_ref, send_ref, fill, y_first)
    for copy in puts:
        copy.wait()


def row_and_mlp(info, place, afters, cots, cot_at, row_weights, weights, last, old, old_layers, waits=()):
    rows, width = afters[0].shape
    pieces = len(afters)
    full = rows * pieces
    wide = weights[4].shape[1]
    first = old is None
    batch = (BATCH, UP_ROWS + DOWN_ROWS + 2 * GROUP, width)
    sums = [shape_of((width, wide), F32)] * 2 + [shape_of((width, width), F32), shape_of((8, width), F32)]
    weights = (*row_weights, *weights)
    weight_specs = [any_spec() if weight.shape[0] > 1 else vmem_spec() for weight in weights]
    return call(
        functools.partial(row_and_mlp_kernel, pieces, first, last, bool(old_layers), cot_at),
        (info, place, *afters, *cots, *weights, *([] if first else old), *old_layers,),
        waits,
        in_specs=[smem_spec()] * 2
        + [any_spec()] * (2 * pieces)
        + weight_specs
        + ([] if first else [any_spec()] * 3 + [vmem_spec()])
        + [vmem_spec()] * len(old_layers),
        out_specs=[any_spec()] * 5
        + [vmem_spec()] * (pieces + 3)
        + ([vmem_spec()] * 2 if last else [any_spec()] * 3 + [vmem_spec()]),
        out_shape=[shape_of((full, width))] * 4
        + [shape_of((full, HEAD))]
        + [shape_of((1 + (k > 0 and bool(old_layers)), rows, width)) for k in range(pieces)]
        + [shape_of((full, width)), shape_of((full, width), F32), shape_of((full, HEAD))]
        + ([shape_of(batch)] * 2 if last else sums),
        scratch_shapes=[pltpu.VMEM((full, width), BF16)] * 3
        + [pltpu.VMEM((full, HEAD), BF16), pltpu.VMEM((full, width), BF16)]
        + [pltpu.VMEM((width, width), BF16)] * 3
        + [
            pltpu.VMEM((full, width), BF16),
            pltpu.VMEM((full, width), BF16),
            pltpu.VMEM((full, width), BF16),
            pltpu.VMEM((width, width), BF16),
            pltpu.VMEM((width, wide), BF16),
            pltpu.VMEM((wide, width), BF16),
            pltpu.VMEM((full, wide), BF16),
            pltpu.VMEM((full, wide), BF16),
            pltpu.VMEM((width, wide), F32),
            pltpu.VMEM((width, wide), F32),
            pltpu.VMEM((width, width), F32),
            pltpu.SemaphoreType.DMA((32,)),
        ]
        + ([pltpu.VMEM((8, width), F32)] if last else []),
        cost_estimate=cost_of(28),
        name="row_and_mlp",
    )


BATCH = 16


def padded_vec(vec_ref):
    values = vec_ref[...]
    return jnp.concatenate([values, jnp.zeros_like(values)], 0).astype(BF16)


def y_first(x, y, z):
    return (y * 4 + z) * 2 + x


def x_first(x, y, z):
    return (x * 2 + y) * 4 + z


def fill_batch(place_ref, keep_ref, send_ref, fill, order):
    for core, out in ((0, keep_ref), (1, send_ref)):
        for y in range(2):
            for z in range(4):
                for x in range(2):
                    fill(out, order(x, y, z), place_ref[0] ^ (core + 2 * x), place_ref[1] ^ (y + 2 * z))


def row_swap(values, step):
    if step == 0:
        return values
    return lax.ppermute(values, "row", [(index, index ^ step) for index in range(4)])


def tab_swap(values, step):
    return lax.ppermute(values, "tab", [(index, index ^ step) for index in range(8)])


def add(*parts):
    total = parts[0].astype(F32)
    for part in parts[1:]:
        total = total + part.astype(F32)
    return total.astype(BF16)


def gather_near(own):
    return [own] + [tab_swap(own, 2 * z) for z in range(1, 4)]


def tie(first, second):
    return lax.optimization_barrier((first, second))


def finish_kernel(sizes, place_ref, near_ref, far_ref, *outs):
    at = 0
    for (rows, columns, turned), out in zip(sizes, outs):
        parts = columns // 512
        for y, ref in ((0, near_ref), (1, far_ref)):
            for z in range(4):
                tab = place_ref[1] ^ (y + 2 * z)
                for part in range(parts):
                    block = ref[z, at + part * rows : at + (part + 1) * rows, :].astype(F32)
                    span = pl.ds(pl.multiple_of(tab * rows, GROUP), rows)
                    out[span, part * 512 : (part + 1) * 512] = block
        at += rows * parts


def finish(place, near, far, sizes, waits=()):
    return call(
        functools.partial(finish_kernel, sizes),
        (place, near, far,),
        waits,
        in_specs=[smem_spec(), vmem_spec(), vmem_spec()],
        out_specs=[vmem_spec()] * len(sizes),
        out_shape=[shape_of((rows * 8, columns), F32) for rows, columns, _ in sizes],
        cost_estimate=cost_of(2),
        name="finish",
    )


def join_pieces_kernel(group, starts, me_ref, *rest):
    ins, out_ref = rest[:-1], rest[-1]
    for (piece, start), ref in zip(starts, ins):
        out_ref[pl.ds((me_ref[0] ^ piece) * group + start, ref.shape[0])] = ref[...]


def join_pieces(me, blocks, group, waits=()):
    _, rows, width = blocks[0][2].shape
    starts = tuple(block[:2] for block in blocks)
    return call(
        functools.partial(join_pieces_kernel, group, starts),
        (me, *(block[2] for block in blocks)),
        waits,
        in_specs=[smem_spec()] + [vmem_spec()] * len(blocks),
        out_specs=vmem_spec(),
        out_shape=shape_of((4 * group, rows, width)),
        cost_estimate=cost_of(2),
        name="join_pieces",
    )


def by_feature(
    table_cells,
    cotangent,
    row_counts,
    context_counts,
    feat_gain,
    feat_shift,
    feat_query,
    feat_key,
    feat_value,
    feat_out,
    feat_bias,
    row_gain,
    row_shift,
    row_query,
    row_key,
    row_value,
    row_out,
    row_bias,
    mlp_gain,
    mlp_shift,
    up_weight,
    up_bias,
    down_weight,
    down_bias,
):
    count = lax.axis_size("row")
    feats = table_cells.shape[2]
    group = feats // count
    me = lax.axis_index("row").astype(jnp.int32)
    own = me.reshape(1)
    place = jnp.stack([me, lax.axis_index("tab").astype(jnp.int32)])
    info = jnp.stack([me, row_counts[0], context_counts[0]])

    def flat(vector):
        return vector.reshape(1, -1)

    cells = table_cells[0].transpose(1, 0, 2)
    upstream = cotangent[0].transpose(1, 0, 2)
    feat_weights = (flat(feat_gain), flat(feat_shift), feat_query, feat_key, feat_value, feat_out)
    row_weight = (row_query, row_key, row_value)
    mlp_weights = (
        row_out,
        flat(row_bias),
        flat(mlp_gain),
        flat(mlp_shift),
        up_weight,
        flat(up_bias),
        down_weight,
        flat(down_bias),
    )
    far = split(own, upstream, group, ((2, 0, 1), (3, 0, 1)))
    cot_first = [row_swap(far[0], 2), row_swap(far[1], 3)]
    plan = ((0, 0, group), (1, 0, group)) + tuple((k, j, 1) for j in range(1, group) for k in (2, 3))
    forward = feat_forward(own, cells, upstream, (*feat_weights, flat(feat_bias)), group, plan, waits=(far[0],))
    after_out, kept_a = list(forward[:feats]), forward[feats : feats + 5]
    cot_own, cot_near, *cot_far = forward[feats + 5 :]
    leaving = [after_out[k * group] for k in range(1, count)]
    (leaving, cot_near), cot_first = tie((leaving, cot_near), cot_first)
    after_out[group :: group] = leaving
    cot_near = row_swap(cot_near, 1)
    first = [row_swap(after_out[k * group], k) for k in range(count)]
    leaving = [after_out[k * group + 1] for k in range(1, count)]
    leaving, first = tie(leaving, first)
    after_out[group + 1 :: group] = leaving
    afters, own_layers, kept_b, backs, mlp_sums, old_layers, late = [], [], [], [], None, [], []
    for j in range(group):
        afters.append(first if j == 0 else [row_swap(after_out[k * group + j], k) for k in range(count)])
        cot = cot_first if j == 0 else [row_swap(cot_far[2 * j - 2], 2), row_swap(cot_far[2 * j - 1], 3)]
        found = row_and_mlp(
            info,
            place,
            afters[j],
            [cot_own, cot_near, *cot],
            (j, j, 0, 0),
            (flat(row_gain), flat(row_shift), *row_weight),
            mlp_weights,
            j == group - 1,
            mlp_sums,
            old_layers,
        )
        kept_b.append(found[:5])
        layer = found[5 : 5 + count]
        own_layers.append(layer[0])
        old_layers = layer[1:] if j == 0 else []
        if j > 0:
            early, late = late, [row_swap(layer[k], k) for k in range(1, count)]
        backs.append(found[5 + count : 8 + count])
        mlp_sums = found[8 + count :]
    mlp_keep, send = mlp_sums
    send, early = tie(send, early)
    mlp_came = row_swap(send, 1)
    mlp_line = tab_swap(add(mlp_keep[8:], mlp_came[8:]), 1)
    grads, d_rows, vecs = [], [], []
    for j in range(group):
        query, key, value, _, extra = kept_b[j]
        if j == 0:
            waits = [backs[-1][2]]
        elif j == 1:
            waits = [vecs[-1], *late]
        else:
            parts = [
                add(*(ref[2 * z : 2 * z + 2] for ref in (mlp_keep, mlp_came, mlp_line))) for z in range(4)
            ]
            waits = [vecs[-1], *grads[0][2:], parts[0]]
        found = row_backward(
            info, (query, key, value, extra), backs[j], afters[j], (flat(row_gain), *row_weight), waits
        )
        d_rows += found[count : count + 3]
        vecs.append(found[count + 3])
        grads.append([row_swap(found[k], k) for k in range(count)])
    parts[1:] = [tab_swap(parts[z], 2 * z) for z in range(1, 4)]
    row_keep, send = row_weights(place, [kept[3] for kept in kept_b], d_rows, vecs, grads[1][2:])
    away = add(*(part[1] for part in parts))
    (away, send), grads[2][1:] = tie((away, send), grads[2][1:])
    row_came = row_swap(send, 1)
    mlp_line = row_swap(away, 2)
    row_away = add(row_keep[8:], row_came[8:])
    row_line = row_swap(row_away, 2)
    mlp_parts = parts
    grad_back = [grads[j][k] for k in range(count) for j in range(group)]

    keep, send, *d_all = feat_backward(place, cells, kept_a, grad_back, feat_weights, group, waits=(row_away,))
    send, (row_line, mlp_line) = tie(send, (row_line, mlp_line))
    came = row_swap(send, 1)
    mlp_own = add(*(part[0] for part in mlp_parts), mlp_line)
    mlp_near = gather_near(mlp_own[:-GROUP])
    row_turned = tab_swap(add(row_keep[4:8], row_came[4:8], row_line[4:8]), 1)
    away = add(keep[8:], came[8:])
    cells_grad, mark = cells_backward(
        own, cells, d_all, (flat(feat_gain), feat_query, feat_key, feat_value), grad_back, group, waits=(away,)
    )
    line, mark = tie(row_swap(away, 2), mark)
    away = add(keep[4:8], came[4:8], line[4:8])
    away, (row_turned, mlp_near) = tie(away, (row_turned, mlp_near))
    turned = tab_swap(away, 1)
    parts = [add(*(ref[z] for ref in (row_keep, row_came, row_line, row_turned))) for z in range(4)]
    row_parts = [parts[0]] + [tab_swap(parts[z], 2 * z) for z in range(1, 4)]
    parts = [add(*(ref[z] for ref in (keep, came, line, turned))) for z in range(4)]
    parts, mlp_near = tie(parts, mlp_near)
    mlp_near = jnp.stack(mlp_near)
    mlp_far = tab_swap(mlp_near, 1)
    parts[1:] = [tab_swap(parts[z], 2 * z) for z in range(1, 4)]
    parts, row_parts = tie(parts, row_parts)
    row_own, feat_own = add(*row_parts), add(*parts)
    near = jnp.stack(gather_near(jnp.concatenate([row_own[:-GROUP], feat_own[:-GROUP]], 0)))
    far = tab_swap(near, 1)
    mlp_vec, row_vec, feat_vec = mlp_own[-GROUP:], row_own[-GROUP:], feat_own[-GROUP:]
    blocks = [(0, j, part) for j, part in enumerate(own_layers)]
    blocks += [(k, 0, part) for k, part in enumerate(early, 1)]
    blocks += [(k, group - 1, part) for k, part in enumerate(late, 1)]
    layer_out = join_pieces(own, blocks, group, (feat_own,))

    up_sum, down_sum, row_out_sum = finish(
        place,
        mlp_near,
        mlp_far,
        ((GROUP, 2048, False), (4 * GROUP, 512, True), (GROUP, 512, False)),
        (feat_own,),
    )
    small = ((GROUP, 512, False),) * 7
    sum_rq, sum_rk, sum_rv, sum_fq, sum_fk, sum_fv, sum_fo = finish(place, near, far, small, (mark, row_out_sum))

    mlp_vec, row_vec, feat_vec = (part.astype(F32) for part in (mlp_vec, row_vec, feat_vec))
    rows = sum_fq.shape[0]

    def quarter(vector):
        return lax.dynamic_slice_in_dim(vector, me * rows, rows, 0)

    return (
        layer_out.transpose(1, 0, 2)[None],
        cells_grad.transpose(1, 0, 2)[None],
        quarter(feat_vec[0]),
        quarter(feat_vec[1]),
        sum_fq,
        sum_fk,
        sum_fv,
        sum_fo,
        quarter(row_vec[2]),
        quarter(row_vec[0]),
        quarter(row_vec[1]),
        sum_rq,
        sum_rk,
        sum_rv,
        row_out_sum,
        quarter(mlp_vec[7]),
        quarter(mlp_vec[5]),
        quarter(mlp_vec[6]),
        up_sum,
        lax.dynamic_index_in_dim(mlp_vec[:4], me, 0, keepdims=False),
        down_sum.T,
        quarter(mlp_vec[4]),
    )


def solution(mesh):
    in_specs = (
        P("tab", "row", None, None),
        P("tab", "row", None, None),
        P("tab"),
        P("tab"),
        P(),
        P(),
        P(),
        P(),
        P(),
        P(),
        P(),
        P(),
        P(),
        P(),
        P(),
        P(),
        P(),
        P(),
        P(),
        P(),
        P(),
        P(),
        P(),
        P(),
    )
    out_specs = (
        P("tab", "row", None, None),
        P("tab", "row", None, None),
        P("row"),
        P("row"),
        P("row", None),
        P("row", None),
        P("row", None),
        P("row", None),
        P("row"),
        P("row"),
        P("row"),
        P("row", None),
        P("row", None),
        P("row", None),
        P("row", None),
        P("row"),
        P("row"),
        P("row"),
        P("row", None),
        P("row"),
        P("row", None),
        P("row"),
    )

    near = (mesh.shape["tab"], mesh.shape["row"]) == (8, 4)
    body = by_feature if near else shards
    return jax.shard_map(body, mesh=mesh, in_specs=in_specs, out_specs=out_specs, check_vma=False)
```

```python
import functools
import math

import jax
import jax.numpy as jnp
from jax import lax
from jax.experimental import pallas as pl
from jax.experimental.pallas import tpu as pltpu
from jax.sharding import PartitionSpec as P

HEADS = 4


EPSILON = 1e-05
NEGATIVE = -1e30


def normalize(values, gain_vec, shift_vec):
    row_mean = jnp.mean(values, -1, keepdims=True)
    centred = values - row_mean
    inverse = lax.rsqrt(jnp.mean(centred * centred, -1, keepdims=True) + EPSILON)
    unit_part = centred * inverse
    return (unit_part * gain_vec + shift_vec, unit_part, inverse)


def normalize_back(upstream, unit_part, inverse, gain_vec):
    scaled = upstream * gain_vec
    inner_part = (
        scaled
        - jnp.mean(scaled, -1, keepdims=True)
        - unit_part * jnp.mean(scaled * unit_part, -1, keepdims=True)
    )
    return (
        inverse * inner_part,
        jnp.sum(upstream * unit_part, axis=(0, 1)),
        jnp.sum(upstream, axis=(0, 1)),
    )


def project(left_side, weight):
    return jnp.einsum("rfd,de->rfe", left_side, weight, preferred_element_type=jnp.float32)


def project_back(upstream, weight):
    return jnp.einsum("rfe,de->rfd", upstream, weight, preferred_element_type=jnp.float32)


def outer_sum(left_side, upstream):
    return jnp.einsum("rfd,rfe->de", left_side, upstream, preferred_element_type=jnp.float32)


def split_heads(values):
    return values.reshape(values.shape[0], values.shape[1], HEADS, values.shape[2] // HEADS)


def join_heads(values):
    return values.reshape(values.shape[0], values.shape[1], values.shape[2] * values.shape[3])


def shards(
    table_cells,
    cotangent,
    row_counts,
    context_counts,
    feat_gain,
    feat_shift,
    feat_query,
    feat_key,
    feat_value,
    feat_out,
    feat_bias,
    row_gain,
    row_shift,
    row_query,
    row_key,
    row_value,
    row_out,
    row_bias,
    mlp_gain,
    mlp_shift,
    up_weight,
    up_bias,
    down_weight,
    down_bias,
):
    source = table_cells[0].astype(jnp.float32)
    local_rows, feat_count, model_width = source.shape
    score_scale = 1.0 / math.sqrt(model_width // HEADS)
    total_rows = local_rows * lax.axis_size("row")
    row_ids = lax.axis_index("row") * local_rows + jnp.arange(local_rows, dtype=jnp.int32)
    row_mask = (row_ids < row_counts[0]).astype(jnp.float32)[:, None, None]
    context_mask = jnp.arange(total_rows, dtype=jnp.int32) < context_counts[0]
    normed_a, unit_a, inverse_a = normalize(source, feat_gain, feat_shift)
    normed_a = normed_a.astype(jnp.bfloat16)
    query_a = split_heads(project(normed_a, feat_query).astype(jnp.bfloat16))
    key_a = split_heads(project(normed_a, feat_key).astype(jnp.bfloat16))
    value_a = split_heads(project(normed_a, feat_value).astype(jnp.bfloat16))
    scores_a = (
        jnp.einsum("rfhd,rghd->rhfg", query_a, key_a, preferred_element_type=jnp.float32)
        * score_scale
    )
    probs_a = jax.nn.softmax(scores_a, -1)
    probs_a_low = probs_a.astype(jnp.bfloat16)
    mixed_a = join_heads(
        jnp.einsum(
            "rhfg,rghd->rfhd", probs_a_low, value_a, preferred_element_type=jnp.float32
        ).astype(jnp.bfloat16)
    )
    after_a = source + project(mixed_a, feat_out) + feat_bias
    normed_b, unit_b, inverse_b = normalize(after_a, row_gain, row_shift)
    normed_b = normed_b.astype(jnp.bfloat16)
    query_b = split_heads(project(normed_b, row_query).astype(jnp.bfloat16))
    key_b = project(normed_b, row_key).astype(jnp.bfloat16)
    value_b = project(normed_b, row_value).astype(jnp.bfloat16)
    key_all, value_all = (
        lax.all_gather(key_b, "row", axis=0, tiled=True),
        lax.all_gather(value_b, "row", axis=0, tiled=True),
    )

    def row_scores(key_whole):
        raw_scores = (
            jnp.einsum(
                "ifhd,jfhd->fhij",
                query_b,
                split_heads(key_whole),
                preferred_element_type=jnp.float32,
            )
            * score_scale
        )
        return jnp.where(context_mask, raw_scores, NEGATIVE)

    scores_b = row_scores(key_all)
    highest = jnp.max(scores_b, -1, keepdims=True)
    log_total = highest + jnp.log(jnp.sum(jnp.exp(scores_b - highest), -1, keepdims=True))
    probs_b_low = jnp.exp(scores_b - log_total).astype(jnp.bfloat16)
    mixed_b = join_heads(
        jnp.einsum(
            "fhij,jfhd->ifhd",
            probs_b_low,
            split_heads(value_all),
            preferred_element_type=jnp.float32,
        ).astype(jnp.bfloat16)
    )
    after_b = after_a + project(mixed_b, row_out) + row_bias
    normed_c, unit_c, inverse_c = normalize(after_b, mlp_gain, mlp_shift)
    normed_c = normed_c.astype(jnp.bfloat16)
    hidden = project(normed_c, up_weight) + up_bias
    active, gelu_pull = jax.vjp(jax.nn.gelu, hidden)
    active = active.astype(jnp.bfloat16)
    after_c = after_b + project(active, down_weight) + down_bias
    layer_out = (after_c * row_mask).astype(jnp.bfloat16)
    grad_c = cotangent[0].astype(jnp.float32) * row_mask
    grad_c_low = grad_c.astype(jnp.bfloat16)
    down_bias_grad = jnp.sum(grad_c, axis=(0, 1))
    down_weight_grad = outer_sum(active, grad_c_low)
    active_grad = project_back(grad_c_low, down_weight)
    hidden_grad = gelu_pull(active_grad)[0].astype(jnp.bfloat16)
    up_bias_grad = jnp.sum(hidden_grad.astype(jnp.float32), axis=(0, 1))
    up_weight_grad = outer_sum(normed_c, hidden_grad)
    back_c, mlp_gain_grad, mlp_shift_grad = normalize_back(
        project_back(hidden_grad, up_weight), unit_c, inverse_c, mlp_gain
    )
    grad_b = grad_c + back_c
    grad_b_low = grad_b.astype(jnp.bfloat16)
    row_bias_grad = jnp.sum(grad_b, axis=(0, 1))
    row_out_grad = outer_sum(mixed_b, grad_b_low)
    mixed_b_grad = split_heads(project_back(grad_b_low, row_out).astype(jnp.bfloat16))
    key_back, value_back = (
        lax.all_gather(key_b, "row", axis=0, tiled=True),
        lax.all_gather(value_b, "row", axis=0, tiled=True),
    )
    probs_full = jnp.exp(row_scores(key_back) - log_total)
    probs_grad = jnp.einsum(
        "ifhd,jfhd->fhij", mixed_b_grad, split_heads(value_back), preferred_element_type=jnp.float32
    )
    row_dot = jnp.sum(probs_full * probs_grad, -1, keepdims=True)
    score_b_grad = (probs_full * (probs_grad - row_dot)).astype(jnp.bfloat16)
    query_b_grad = join_heads(
        (
            jnp.einsum(
                "fhij,jfhd->ifhd",
                score_b_grad,
                split_heads(key_back),
                preferred_element_type=jnp.float32,
            )
            * score_scale
        ).astype(jnp.bfloat16)
    )
    flat_rows = feat_count * HEADS
    log_all, dot_all = (
        lax.all_gather(log_total.reshape(flat_rows, local_rows), "row", axis=1, tiled=True),
        lax.all_gather(row_dot.reshape(flat_rows, local_rows), "row", axis=1, tiled=True),
    )
    own_mask = row_ids < context_counts[0]
    key_own = split_heads(key_b)
    value_own = split_heads(value_b)
    query_piece = lax.all_gather(query_b, "row", axis=0, tiled=True)
    grad_piece = lax.all_gather(mixed_b_grad, "row", axis=0, tiled=True)
    count = query_piece.shape[0]
    log_piece = log_all.reshape(feat_count, HEADS, count, 1)
    dot_piece = dot_all.reshape(feat_count, HEADS, count, 1)
    piece_scores = (
        jnp.einsum("ifhd,jfhd->fhij", query_piece, key_own, preferred_element_type=jnp.float32)
        * score_scale
    )
    piece_scores = jnp.where(own_mask, piece_scores, NEGATIVE)
    piece_probs = jnp.exp(piece_scores - log_piece)
    piece_inner = jnp.einsum(
        "ifhd,jfhd->fhij", grad_piece, value_own, preferred_element_type=jnp.float32
    )
    piece_grad = (piece_probs * (piece_inner - dot_piece)).astype(jnp.bfloat16)
    key_total = (
        jnp.einsum("fhij,ifhd->jfhd", piece_grad, query_piece, preferred_element_type=jnp.float32)
        * score_scale
    )
    value_total = jnp.einsum(
        "fhij,ifhd->jfhd",
        piece_probs.astype(jnp.bfloat16),
        grad_piece,
        preferred_element_type=jnp.float32,
    )
    key_total, value_total = (key_total, value_total)
    key_b_grad = join_heads(key_total).astype(jnp.bfloat16)
    value_b_grad = join_heads(value_total).astype(jnp.bfloat16)
    row_query_grad = outer_sum(normed_b, query_b_grad)
    row_key_grad = outer_sum(normed_b, key_b_grad)
    row_value_grad = outer_sum(normed_b, value_b_grad)
    normed_b_grad = (
        project_back(query_b_grad, row_query)
        + project_back(key_b_grad, row_key)
        + project_back(value_b_grad, row_value)
    )
    back_b, row_gain_grad, row_shift_grad = normalize_back(
        normed_b_grad, unit_b, inverse_b, row_gain
    )
    grad_a = grad_b + back_b
    grad_a_low = grad_a.astype(jnp.bfloat16)
    feat_bias_grad = jnp.sum(grad_a, axis=(0, 1))
    feat_out_grad = outer_sum(mixed_a, grad_a_low)
    mixed_a_grad = split_heads(project_back(grad_a_low, feat_out).astype(jnp.bfloat16))
    probs_a_grad = jnp.einsum(
        "rfhd,rghd->rhfg", mixed_a_grad, value_a, preferred_element_type=jnp.float32
    )
    score_a_grad = (
        probs_a * (probs_a_grad - jnp.sum(probs_a * probs_a_grad, -1, keepdims=True))
    ).astype(jnp.bfloat16)
    query_a_grad = join_heads(
        (
            jnp.einsum("rhfg,rghd->rfhd", score_a_grad, key_a, preferred_element_type=jnp.float32)
            * score_scale
        ).astype(jnp.bfloat16)
    )
    key_a_grad = join_heads(
        (
            jnp.einsum("rhfg,rfhd->rghd", score_a_grad, query_a, preferred_element_type=jnp.float32)
            * score_scale
        ).astype(jnp.bfloat16)
    )
    value_a_grad = join_heads(
        jnp.einsum(
            "rhfg,rfhd->rghd", probs_a_low, mixed_a_grad, preferred_element_type=jnp.float32
        ).astype(jnp.bfloat16)
    )
    feat_query_grad = outer_sum(normed_a, query_a_grad)
    feat_key_grad = outer_sum(normed_a, key_a_grad)
    feat_value_grad = outer_sum(normed_a, value_a_grad)
    normed_a_grad = (
        project_back(query_a_grad, feat_query)
        + project_back(key_a_grad, feat_key)
        + project_back(value_a_grad, feat_value)
    )
    back_a, feat_gain_grad, feat_shift_grad = normalize_back(
        normed_a_grad, unit_a, inverse_a, feat_gain
    )
    cells_grad = (grad_a + back_a).astype(jnp.bfloat16)
    row_summed = (
        lax.psum_scatter(
            feat_gain_grad.astype(jnp.bfloat16), "row", scatter_dimension=0, tiled=True
        ).astype(jnp.float32),
        lax.psum_scatter(
            feat_shift_grad.astype(jnp.bfloat16), "row", scatter_dimension=0, tiled=True
        ).astype(jnp.float32),
        lax.psum_scatter(
            feat_query_grad.astype(jnp.bfloat16), "row", scatter_dimension=0, tiled=True
        ).astype(jnp.float32),
        lax.psum_scatter(
            feat_key_grad.astype(jnp.bfloat16), "row", scatter_dimension=0, tiled=True
        ).astype(jnp.float32),
        lax.psum_scatter(
            feat_value_grad.astype(jnp.bfloat16), "row", scatter_dimension=0, tiled=True
        ).astype(jnp.float32),
        lax.psum_scatter(
            feat_out_grad.astype(jnp.bfloat16), "row", scatter_dimension=0, tiled=True
        ).astype(jnp.float32),
        lax.psum_scatter(
            feat_bias_grad.astype(jnp.bfloat16), "row", scatter_dimension=0, tiled=True
        ).astype(jnp.float32),
        lax.psum_scatter(
            row_gain_grad.astype(jnp.bfloat16), "row", scatter_dimension=0, tiled=True
        ).astype(jnp.float32),
        lax.psum_scatter(
            row_shift_grad.astype(jnp.bfloat16), "row", scatter_dimension=0, tiled=True
        ).astype(jnp.float32),
        lax.psum_scatter(
            row_query_grad.astype(jnp.bfloat16), "row", scatter_dimension=0, tiled=True
        ).astype(jnp.float32),
        lax.psum_scatter(
            row_key_grad.astype(jnp.bfloat16), "row", scatter_dimension=0, tiled=True
        ).astype(jnp.float32),
        lax.psum_scatter(
            row_value_grad.astype(jnp.bfloat16), "row", scatter_dimension=0, tiled=True
        ).astype(jnp.float32),
        lax.psum_scatter(
            row_out_grad.astype(jnp.bfloat16), "row", scatter_dimension=0, tiled=True
        ).astype(jnp.float32),
        lax.psum_scatter(
            row_bias_grad.astype(jnp.bfloat16), "row", scatter_dimension=0, tiled=True
        ).astype(jnp.float32),
        lax.psum_scatter(
            mlp_gain_grad.astype(jnp.bfloat16), "row", scatter_dimension=0, tiled=True
        ).astype(jnp.float32),
        lax.psum_scatter(
            mlp_shift_grad.astype(jnp.bfloat16), "row", scatter_dimension=0, tiled=True
        ).astype(jnp.float32),
        lax.psum_scatter(
            up_weight_grad.astype(jnp.bfloat16), "row", scatter_dimension=0, tiled=True
        ).astype(jnp.float32),
        lax.psum_scatter(
            up_bias_grad.astype(jnp.bfloat16), "row", scatter_dimension=0, tiled=True
        ).astype(jnp.float32),
        lax.psum_scatter(
            down_weight_grad.astype(jnp.bfloat16), "row", scatter_dimension=0, tiled=True
        ).astype(jnp.float32),
        lax.psum_scatter(
            down_bias_grad.astype(jnp.bfloat16), "row", scatter_dimension=0, tiled=True
        ).astype(jnp.float32),
    )
    (
        part_fg,
        part_fs,
        part_fq,
        part_fk,
        part_fv,
        part_fo,
        part_fb,
        part_rg,
        part_rs,
        part_rq,
        part_rk,
        part_rv,
        part_ro,
        part_rb,
        part_mg,
        part_ms,
        part_uw,
        part_ub,
        part_dw,
        part_db,
    ) = row_summed
    summed = (
        lax.psum(part_fg.astype(jnp.bfloat16), "tab").astype(jnp.float32),
        lax.psum(part_fs.astype(jnp.bfloat16), "tab").astype(jnp.float32),
        lax.psum(part_fq.astype(jnp.bfloat16), "tab").astype(jnp.float32),
        lax.psum(part_fk.astype(jnp.bfloat16), "tab").astype(jnp.float32),
        lax.psum(part_fv.astype(jnp.bfloat16), "tab").astype(jnp.float32),
        lax.psum(part_fo.astype(jnp.bfloat16), "tab").astype(jnp.float32),
        lax.psum(part_fb.astype(jnp.bfloat16), "tab").astype(jnp.float32),
        lax.psum(part_rg.astype(jnp.bfloat16), "tab").astype(jnp.float32),
        lax.psum(part_rs.astype(jnp.bfloat16), "tab").astype(jnp.float32),
        lax.psum(part_rq.astype(jnp.bfloat16), "tab").astype(jnp.float32),
        lax.psum(part_rk.astype(jnp.bfloat16), "tab").astype(jnp.float32),
        lax.psum(part_rv.astype(jnp.bfloat16), "tab").astype(jnp.float32),
        lax.psum(part_ro.astype(jnp.bfloat16), "tab").astype(jnp.float32),
        lax.psum(part_rb.astype(jnp.bfloat16), "tab").astype(jnp.float32),
        lax.psum(part_mg.astype(jnp.bfloat16), "tab").astype(jnp.float32),
        lax.psum(part_ms.astype(jnp.bfloat16), "tab").astype(jnp.float32),
        lax.psum(part_uw.astype(jnp.bfloat16), "tab").astype(jnp.float32),
        lax.psum(part_ub.astype(jnp.bfloat16), "tab").astype(jnp.float32),
        lax.psum(part_dw.astype(jnp.bfloat16), "tab").astype(jnp.float32),
        lax.psum(part_db.astype(jnp.bfloat16), "tab").astype(jnp.float32),
    )
    return (
        layer_out[None],
        cells_grad[None],
        summed[0],
        summed[1],
        summed[2],
        summed[3],
        summed[4],
        summed[5],
        summed[6],
        summed[7],
        summed[8],
        summed[9],
        summed[10],
        summed[11],
        summed[12],
        summed[13],
        summed[14],
        summed[15],
        summed[16],
        summed[17],
        summed[18],
        summed[19],
    )


HEAD = 128
GROUP = 16
LOG2E = 1.4426950408889634
F32 = jnp.float32
BF16 = jnp.bfloat16
SCORE = 1.0 / math.sqrt(HEAD)
SCALE = LOG2E * SCORE


def dot_nn(a, b):
    return jnp.dot(a, b, preferred_element_type=F32)


def dot_nt(a, b):
    return lax.dot_general(a, b, (((1,), (1,)), ((), ())), preferred_element_type=F32)


def dot_tn(a, b):
    return lax.dot_general(a, b, (((0,), (0,)), ((), ())), preferred_element_type=F32)


def unit_of(values):
    centred = values - jnp.mean(values, -1, keepdims=True)
    inverse = lax.rsqrt(jnp.mean(centred * centred, -1, keepdims=True) + EPSILON)
    return centred * inverse, inverse


def norm_back(upstream, unit, inverse, gain):
    scaled = upstream * gain
    return inverse * (
        scaled
        - jnp.mean(scaled, -1, keepdims=True)
        - unit * jnp.mean(scaled * unit, -1, keepdims=True)
    )


def column_sum(values):
    return jnp.sum(values, 0, keepdims=True)


def vmem_spec():
    return pl.BlockSpec(memory_space=pltpu.VMEM)


def smem_spec():
    return pl.BlockSpec(memory_space=pltpu.SMEM)


def any_spec():
    return pl.BlockSpec(memory_space=pl.ANY)


def fixed(shape):
    return pl.BlockSpec(shape, lambda *_: (0,) * len(shape))


def shape_of(shape, dtype=BF16):
    return jax.ShapeDtypeStruct(shape, dtype)


def params_of(mib=63):
    return pltpu.CompilerParams(vmem_limit_bytes=mib * 1024 * 1024)


def call(kernel, args, waits, in_specs, **rest):
    count = len(args)

    def body(*refs):
        kernel(*refs[:count], *refs[count + len(waits) :])

    specs = [*in_specs, *[any_spec() for _ in waits]]
    return pl.pallas_call(body, in_specs=specs, compiler_params=params_of(), **rest)(*args, *waits)


def cost_of(microseconds):
    return pl.CostEstimate(flops=int(microseconds * 900e6), bytes_accessed=1024, transcendentals=0)


def head_lanes(head):
    return slice(head * HEAD, (head + 1) * HEAD)


def lane_of(rows):
    return lax.broadcasted_iota(jnp.int32, (rows, HEAD), 1)


def put_thirds(lane, first, values, base):
    high = values.astype(BF16).astype(F32)
    rest = values - high
    middle = rest.astype(BF16).astype(F32)
    turn = (lane - first) % 3
    parts = jnp.where(turn == 0, high, jnp.where(turn == 1, middle, rest - middle))
    return jnp.where((lane >= first) & (lane < first + 3 * HEADS), parts, base).astype(BF16)


def own_lanes(lane, first, head):
    return (lane >= first + 3 * head) & (lane < first + 3 * head + 3)


def head_picker(first, width):
    head = lax.broadcasted_iota(jnp.int32, (width, HEAD), 0) // HEAD
    lane = lax.broadcasted_iota(jnp.int32, (width, HEAD), 1)
    hit = (lane >= first) & (lane < first + 3 * HEADS) & ((lane - first) // 3 == head)
    return jnp.where(hit, 1.0, 0.0).astype(BF16)


def head_dots(left, right, picker):
    product = left.astype(F32) * right.astype(F32)
    high = product.astype(BF16)
    low = (product - high.astype(F32)).astype(BF16)
    return dot_nn(high, picker) + dot_nn(low, picker)


def beside(left, right):
    return jnp.concatenate([left, right], 1)


def split_kernel(group, plan, me_ref, whole_ref, *rest):
    outs, sems = rest[:-1], rest[-1]
    copies = []
    for index, (piece, first, size) in enumerate(plan):
        source = whole_ref.at[pl.ds((me_ref[0] ^ piece) * group + first, size)]
        copies.append(pltpu.make_async_copy(source, outs[index], sems.at[index]))
        copies[-1].start()
    for copy in copies:
        copy.wait()


def split(me, whole, group, plan, waits=()):
    _, rows, width = whole.shape
    return call(
        functools.partial(split_kernel, group, plan),
        (me, whole),
        waits,
        in_specs=[smem_spec(), any_spec()],
        out_specs=[vmem_spec()] * len(plan),
        out_shape=[shape_of((size, rows, width)) for _, _, size in plan],
        scratch_shapes=[pltpu.SemaphoreType.DMA((len(plan),))],
        cost_estimate=cost_of(2),
        name="split",
    )


def query_mask(size):
    row = lax.broadcasted_iota(jnp.int32, (size, HEAD), 0) % GROUP
    lane = lane_of(size)
    return jnp.where((lane < GROUP) & (lane != row), NEGATIVE, 0.0)


def key_mask(size, head):
    row = lax.broadcasted_iota(jnp.int32, (size, HEAD), 0) % GROUP
    lane = lane_of(size)
    return jnp.where((lane == row) | own_lanes(lane, GROUP, head), 1.0, 0.0).astype(BF16)


def gather_cells(group, me_ref, cells_ref):
    feats, rows, _ = cells_ref.shape
    return jnp.concatenate(
        [
            cells_ref[(me_ref[0] ^ (index // group)) * group + index % group, part : part + GROUP, :]
            for part in range(0, rows, GROUP)
            for index in range(feats)
        ],
        0,
    )


def feat_forward_kernel(
    group, plan, me_ref, cells_ref, cot_ref, gain, shift, w_query, w_key, w_value, w_out, bias, *rest
):
    feats, rows, width = cells_ref.shape
    outs = rest[:feats]
    q_ref, k_ref, v_ref, mixed_ref, extra_ref = rest[feats : feats + 5]
    for (piece, first, count), out in zip(plan, rest[feats + 5 :]):
        out[...] = cot_ref[pl.ds((me_ref[0] ^ piece) * group + first, count)]
    size, parts = feats * GROUP, rows // GROUP
    cells = gather_cells(group, me_ref, cells_ref)
    unit, _ = unit_of(cells.astype(F32))
    normed = (unit * gain[...] + shift[...]).astype(BF16)
    q_ref[...] = dot_nn(normed, w_query[...]).astype(BF16)
    k_ref[...] = dot_nn(normed, w_key[...]).astype(BF16)
    v_ref[...] = dot_nn(normed, w_value[...]).astype(BF16)
    mask = query_mask(size)
    mask_low = mask.astype(BF16)
    keys = [key_mask(size, head) for head in range(HEADS)]
    lane = lane_of(size)
    ones = jnp.ones((size, HEAD), BF16)
    pairs = [
        (slice(part * size, (part + 1) * size), head_lanes(head), head)
        for part in range(parts)
        for head in range(HEADS)
    ]
    scores = [
        dot_nt(beside(q_ref[span, lanes], mask_low), beside(k_ref[span, lanes], keys[head]))
        for span, lanes, head in pairs
    ]
    tops = [jnp.max(score, -1, keepdims=True) for score in scores]
    grown = [jnp.exp2((score - top) * SCALE).astype(BF16) for score, top in zip(scores, tops)]
    both = [dot_nn(grow, beside(v_ref[span, lanes], ones)) for (span, lanes, _), grow in zip(pairs, grown)]
    for (span, lanes, _), found in zip(pairs, both):
        mixed_ref[span, lanes] = (found[:, :HEAD] / found[:, HEAD:]).astype(BF16)
    for part in range(parts):
        top, total = jnp.zeros((size, HEAD), F32), jnp.ones((size, HEAD), F32)
        for head in range(HEADS):
            own = own_lanes(lane, GROUP, head)
            top = jnp.where(own, tops[part * HEADS + head], top)
            total = jnp.where(own, both[part * HEADS + head][:, HEAD:], total)
        minus = -(top + jnp.log2(total) * (1.0 / SCALE))
        extra_ref[part * size : (part + 1) * size, :] = put_thirds(lane, GROUP, minus, mask)
    after = cells.astype(F32) + dot_nn(mixed_ref[...], w_out[...]) + bias[...]
    after = after.astype(BF16)
    for part in range(parts):
        for index in range(feats):
            start = part * size + index * GROUP
            outs[index][part * GROUP : (part + 1) * GROUP, :] = after[start : start + GROUP]


def feat_forward(me, cells, cot, weights, group, plan, block=64, waits=()):
    feats, rows, width = cells.shape
    tokens = block * feats
    vector, whole = fixed((1, width)), fixed((width, width))
    return call(
        functools.partial(feat_forward_kernel, group, plan),
        (me, cells, cot, *weights),
        waits,
        grid=(rows // block,),
        in_specs=[smem_spec()]
        + [pl.BlockSpec((feats, block, width), lambda i: (0, i, 0))] * 2
        + [vector, vector, whole, whole, whole, whole, vector],
        out_specs=[pl.BlockSpec((block, width), lambda i: (i, 0))] * feats
        + [pl.BlockSpec((tokens, width), lambda i: (i, 0))] * 4
        + [pl.BlockSpec((tokens, HEAD), lambda i: (i, 0))]
        + [pl.BlockSpec((size, block, width), lambda i: (0, i, 0)) for _, _, size in plan],
        out_shape=[shape_of((rows, width))] * feats
        + [shape_of((rows * feats, width))] * 4
        + [shape_of((rows * feats, HEAD))]
        + [shape_of((size, rows, width)) for _, _, size in plan],
        cost_estimate=cost_of(15),
        name="feat_forward",
    )


def feat_backward_kernel(
    group,
    place_ref,
    cells_ref,
    q_ref,
    k_ref,
    v_ref,
    mixed_ref,
    extra_ref,
    gain,
    shift,
    w_query,
    w_key,
    w_value,
    w_out,
    *rest,
):
    feats, rows, width = cells_ref.shape
    grads, rest = rest[:feats], rest[feats:]
    keep_ref, send_ref, d_query, d_key, d_value, sum_query, sum_key, sum_value, sum_out, vec_ref = rest
    parts, size = rows // GROUP, feats * GROUP

    @pl.when(pl.program_id(0) == 0)
    def _():
        for ref in (sum_query, sum_key, sum_value, sum_out, vec_ref):
            ref[...] = jnp.zeros_like(ref)

    grad_low = jnp.concatenate(
        [ref[part * GROUP : (part + 1) * GROUP, :] for part in range(parts) for ref in grads], 0
    )
    sum_out[...] += dot_tn(mixed_ref[...], grad_low)
    mixed_grad = dot_nt(grad_low, w_out[...]).astype(BF16)
    dots = head_dots(mixed_grad, mixed_ref[...], head_picker(GROUP, width))
    dots = put_thirds(lane_of(dots.shape[0]), GROUP, -dots, jnp.zeros((), F32))
    keys = [key_mask(size, head) for head in range(HEADS)]
    pairs = [
        (slice(part * size, (part + 1) * size), head_lanes(head), head)
        for part in range(parts)
        for head in range(HEADS)
    ]
    scores = [dot_nt(beside(k_ref[s, l], keys[h]), beside(q_ref[s, l], extra_ref[s, :])) for s, l, h in pairs]
    inners = [dot_nt(beside(v_ref[s, l], keys[h]), beside(mixed_grad[s, l], dots[s])) for s, l, h in pairs]
    probs = [jnp.exp2(score * SCALE) for score in scores]
    score_grads = [(prob * inner).astype(BF16) for prob, inner in zip(probs, inners)]
    for (s, l, _), prob in zip(pairs, probs):
        d_value[s, l] = dot_nn(prob.astype(BF16), mixed_grad[s, l]).astype(BF16)
    for (s, l, _), score_grad in zip(pairs, score_grads):
        d_key[s, l] = (dot_nn(score_grad, q_ref[s, l]) * SCORE).astype(BF16)
    for (s, l, _), score_grad in zip(pairs, score_grads):
        d_query[s, l] = (dot_tn(score_grad, k_ref[s, l]) * SCORE).astype(BF16)
    unit, _ = unit_of(gather_cells(group, place_ref, cells_ref).astype(F32))
    normed_t = (unit * gain[...] + shift[...]).astype(BF16).T
    sum_query[...] += dot_nn(normed_t, d_query[...])
    sum_key[...] += dot_nn(normed_t, d_key[...])
    sum_value[...] += dot_nn(normed_t, d_value[...])
    vec_ref[2:3, :] += column_sum(d_query[...].astype(F32))
    vec_ref[3:4, :] += column_sum(d_key[...].astype(F32))
    vec_ref[4:5, :] += column_sum(d_value[...].astype(F32))

    @pl.when(pl.program_id(0) == pl.num_programs(0) - 1)
    def _():
        ones = jnp.ones((8, width), BF16)
        crossed, plain = jnp.zeros((8, width), F32), jnp.zeros((8, width), F32)
        for index, (weight, total) in enumerate(
            ((w_query, sum_query), (w_key, sum_key), (w_value, sum_value))
        ):
            product = weight[...].astype(F32) * total[...]
            column = jnp.broadcast_to(vec_ref[2 + index : 3 + index, :], (8, width))
            for _ in range(3):
                crossed = crossed + dot_nt(ones, product.astype(BF16))
                product = product - product.astype(BF16).astype(F32)
                plain = plain + dot_nt(column.astype(BF16), weight[...])
                column = column - column.astype(BF16).astype(F32)
        vec_ref[0:1, :] = (crossed[:1] - shift[...] * plain[:1]) / gain[...]
        vec_ref[1:2, :] = plain[:1]

        def fill(out, place, quarter, piece):
            start = pl.multiple_of(quarter * HEAD + piece * GROUP, GROUP)
            for index, ref in enumerate((sum_query, sum_key, sum_value, sum_out)):
                out[place, index * GROUP : (index + 1) * GROUP, :] = ref[pl.ds(start, GROUP), :].astype(BF16)
            out[place, 4 * GROUP : 5 * GROUP, :] = padded_vec(vec_ref)

        fill_batch(place_ref, keep_ref, send_ref, fill, x_first)


def feat_backward(place, cells, kept, grads, weights, group, block=64, waits=()):
    feats, rows, width = cells.shape
    tokens = block * feats
    vector, whole = fixed((1, width)), fixed((width, width))
    batch = (BATCH, 5 * GROUP, width)
    row_block = pl.BlockSpec((tokens, width), lambda i: (i, 0))
    return call(
        functools.partial(feat_backward_kernel, group),
        (place, cells, *kept, *weights, *grads,),
        waits,
        grid=(rows // block,),
        in_specs=[smem_spec(), pl.BlockSpec((feats, block, width), lambda i: (0, i, 0))]
        + [row_block] * 4
        + [pl.BlockSpec((tokens, HEAD), lambda i: (i, 0))]
        + [vector, vector, whole, whole, whole, whole]
        + [pl.BlockSpec((block, width), lambda i: (i, 0))] * feats,
        out_specs=[fixed(batch)] * 2 + [row_block] * 3,
        out_shape=[shape_of(batch)] * 2 + [shape_of((rows * feats, width))] * 3,
        scratch_shapes=[pltpu.VMEM((width, width), F32)] * 4 + [pltpu.VMEM((8, width), F32)],
        cost_estimate=cost_of(20),
        name="feat_backward",
    )


def cells_backward_kernel(group, me_ref, cells_ref, d_query, d_key, d_value, gain, w_query, w_key, w_value, *rest):
    grads, (out_ref, mark_ref) = rest[:-2], rest[-2:]
    feats, rows, _ = cells_ref.shape
    mark_ref[...] = jnp.zeros_like(mark_ref)
    parts, size = rows // GROUP, feats * GROUP
    unit, inverse = unit_of(gather_cells(group, me_ref, cells_ref).astype(F32))
    upstream = (
        dot_nt(d_query[...], w_query[...])
        + dot_nt(d_key[...], w_key[...])
        + dot_nt(d_value[...], w_value[...])
    )
    back = norm_back(upstream, unit, inverse, gain[...])
    for index in range(feats):
        true = (me_ref[0] ^ (index // group)) * group + index % group
        for part in range(parts):
            start = part * size + index * GROUP
            span = slice(part * GROUP, (part + 1) * GROUP)
            cells = grads[index][span, :].astype(F32) + back[start : start + GROUP]
            out_ref[true, span, :] = cells.astype(BF16)


def cells_backward(me, cells, d_all, weights, grads, group, block=64, waits=()):
    feats, rows, width = cells.shape
    tokens = block * feats
    vector, whole = fixed((1, width)), fixed((width, width))
    row_block = pl.BlockSpec((tokens, width), lambda i: (i, 0))
    by_rows = pl.BlockSpec((feats, block, width), lambda i: (0, i, 0))
    return call(
        functools.partial(cells_backward_kernel, group),
        (me, cells, *d_all, *weights, *grads,),
        waits,
        grid=(rows // block,),
        in_specs=[smem_spec(), by_rows]
        + [row_block] * 3
        + [vector, whole, whole, whole]
        + [pl.BlockSpec((block, width), lambda i: (i, 0))] * feats,
        out_specs=[by_rows, fixed((8, HEAD))],
        out_shape=[shape_of((feats, rows, width)), shape_of((8, HEAD), F32)],
        cost_estimate=cost_of(12),
        name="cells_backward",
    )


def key_extra(info_ref, piece, rows, head):
    first = (info_ref[0] ^ piece) * rows
    row = lax.broadcasted_iota(jnp.int32, (rows, HEAD), 0) + first
    lane = lane_of(rows)
    bias = jnp.where(row < info_ref[2], 0.0, NEGATIVE)
    return jnp.where(lane == 0, bias, jnp.where(own_lanes(lane, 1, head), 1.0, 0.0)).astype(BF16)


def row_backward_kernel(pieces, info_ref, *rest):
    q_ref, k_ref, v_ref, extra_ref, mixed_grad_ref, dots_ref, rest = *rest[:6], rest[6:]
    afters, rest = rest[:pieces], rest[pieces:]
    grad_hbm, gain, w_query_hbm, w_key_hbm, w_value_hbm = rest[:5]
    outs, rest = rest[5 : 5 + pieces], rest[5 + pieces :]
    d_query, d_key, d_value, vec_ref = rest[:4]
    after, grad, w_query, w_key, w_value, query_all, key_all, value_all, query_sum, sems = rest[4:]
    rows, width = outs[0].shape
    full = rows * pieces
    head = pl.program_id(0)
    copies = [
        pltpu.make_async_copy(afters[piece], after.at[pl.ds(piece * rows, rows), :], sems.at[piece])
        for piece in range(pieces)
    ]
    copies.append(pltpu.make_async_copy(grad_hbm, grad, sems.at[pieces]))
    for index, (source, target) in enumerate(
        ((w_query_hbm, w_query), (w_key_hbm, w_key), (w_value_hbm, w_value))
    ):
        copies.append(pltpu.make_async_copy(source, target, sems.at[pieces + 1 + index]))

    @pl.when(head == 0)
    def _():
        for copy in copies:
            copy.start()

    query = beside(q_ref[...], extra_ref[...])
    upstream = beside(mixed_grad_ref[...], dots_ref[...])
    spans = [slice(index * rows, (index + 1) * rows) for index in range(pieces)]
    keys = [key_extra(info_ref, index, rows, head) for index in range(pieces)]
    scores = [dot_nt(beside(k_ref[span, :], extra), query) for span, extra in zip(spans, keys)]
    inners = [dot_nt(beside(v_ref[span, :], extra), upstream) for span, extra in zip(spans, keys)]
    probs = [jnp.exp2(score * SCALE) for score in scores]
    score_grads = [(prob * inner).astype(BF16) for prob, inner in zip(probs, inners)]
    for span, prob in zip(spans, probs):
        found = dot_nn(prob.astype(BF16), mixed_grad_ref[...]).astype(BF16)
        value_all[head, span, :] = found
        d_value[span, :] = found
    for span, score_grad in zip(spans, score_grads):
        found = (dot_nn(score_grad, q_ref[...]) * SCORE).astype(BF16)
        key_all[head, span, :] = found
        d_key[span, :] = found
    query_sum[...] = dot_nn(k_ref[...].T, jnp.concatenate(score_grads, 0)).T
    found = (query_sum[...] * SCORE).astype(BF16)
    query_all[head] = found
    d_query[...] = found

    @pl.when(head == HEADS - 1)
    def _():
        for copy in copies:
            copy.wait()
        vec_ref[...] = jnp.zeros_like(vec_ref)
        for piece in range(pieces):
            span = slice(piece * rows, (piece + 1) * rows)
            unit, inverse = unit_of(after[span, :].astype(F32))
            upstream = None
            for ref, weight in ((query_all, w_query), (key_all, w_key), (value_all, w_value)):
                flat = jnp.concatenate([ref[index, span, :] for index in range(HEADS)], 1)
                part = dot_nt(flat, weight[...])
                upstream = part if upstream is None else upstream + part
            grad_a = grad[span, :] + norm_back(upstream, unit, inverse, gain[...])
            outs[piece][...] = grad_a.astype(BF16)
            vec_ref[0:1, :] += column_sum(upstream * unit)
            vec_ref[1:2, :] += column_sum(upstream)
            vec_ref[2:3, :] += column_sum(grad_a)


def row_backward(info, kept, back, afters, weights, waits=()):
    rows, width = afters[0].shape
    count = len(afters)
    full = rows * count
    query, key, value, extra = kept
    mixed_grad, grad_b, dots = back
    by_head = pl.BlockSpec((full, HEAD), lambda h: (0, h))
    return call(
        functools.partial(row_backward_kernel, count),
        (info, query, key, value, extra, mixed_grad, dots, *afters, grad_b, *weights,),
        waits,
        grid=(HEADS,),
        in_specs=[smem_spec()]
        + [by_head] * 3
        + [fixed((full, HEAD)), by_head, fixed((full, HEAD))]
        + [any_spec()] * (count + 1)
        + [fixed((1, width))]
        + [any_spec()] * 3,
        out_specs=[fixed((rows, width))] * count + [by_head] * 3 + [fixed((8, width))],
        out_shape=[shape_of((rows, width))] * count + [shape_of((full, width))] * 3 + [shape_of((8, width), F32)],
        scratch_shapes=[
            pltpu.VMEM((full, width), BF16),
            pltpu.VMEM((full, width), F32),
            pltpu.VMEM((width, width), BF16),
            pltpu.VMEM((width, width), BF16),
            pltpu.VMEM((width, width), BF16),
            pltpu.VMEM((HEADS, full, HEAD), BF16),
            pltpu.VMEM((HEADS, full, HEAD), BF16),
            pltpu.VMEM((HEADS, full, HEAD), BF16),
            pltpu.VMEM((full, HEAD), F32),
            pltpu.SemaphoreType.DMA((count + 4,)),
        ],
        cost_estimate=cost_of(15),
        name="row_backward",
    )


def row_weights_kernel(group, place_ref, *rest):
    normeds, rest = rest[:group], rest[group:]
    grads, rest = rest[: 3 * group], rest[3 * group :]
    vecs, rest = rest[:group], rest[group:]
    keep_ref, send_ref, normed, grad, totals, sems = rest
    copies = []
    for j in range(group):
        mine = [pltpu.make_async_copy(normeds[j], normed.at[j], sems.at[4 * j])]
        for index in range(3):
            mine.append(pltpu.make_async_copy(grads[3 * j + index], grad.at[j, index], sems.at[4 * j + 1 + index]))
        for copy in mine:
            copy.start()
        copies.append(mine)
    for j in range(group):
        for copy in copies[j]:
            copy.wait()
        turned = normed[j].T
        for index in range(3):
            part = dot_nn(turned, grad[j, index])
            if j == 0:
                totals[index] = part
            else:
                totals[index] += part
    vec = sum((ref[...] for ref in vecs[1:]), vecs[0][...])

    def fill(out, place, quarter, piece):
        start = pl.multiple_of(quarter * HEAD + piece * GROUP, GROUP)
        for index in range(3):
            out[place, index * GROUP : (index + 1) * GROUP, :] = totals[index, pl.ds(start, GROUP), :].astype(BF16)
        out[place, 3 * GROUP : 4 * GROUP, :] = padded_vec(vec)

    fill_batch(place_ref, keep_ref, send_ref, fill, x_first)


def row_weights(place, normeds, grads, vecs, waits=()):
    group = len(normeds)
    full, width = normeds[0].shape
    batch = (BATCH, 4 * GROUP, width)
    return call(
        functools.partial(row_weights_kernel, group),
        (place, *normeds, *grads, *vecs,),
        waits,
        in_specs=[smem_spec()] + [any_spec()] * (4 * group) + [vmem_spec()] * group,
        out_specs=[vmem_spec()] * 2,
        out_shape=[shape_of(batch)] * 2,
        scratch_shapes=[
            pltpu.VMEM((group, full, width), BF16),
            pltpu.VMEM((group, 3, full, width), BF16),
            pltpu.VMEM((3, width, width), F32),
            pltpu.SemaphoreType.DMA((4 * group,)),
        ],
        cost_estimate=cost_of(8),
        name="row_weights",
    )


CHUNK = 512
UP_ROWS, DOWN_ROWS = GROUP * 4, 4 * GROUP


def units_of(parts):
    centred = [part - jnp.mean(part, -1, keepdims=True) for part in parts]
    inverses = [lax.rsqrt(jnp.mean(part * part, -1, keepdims=True) + EPSILON) for part in centred]
    return [part * inverse for part, inverse in zip(centred, inverses)], inverses


def norms_back(upstreams, units, inverses, gain):
    scaled = [upstream * gain for upstream in upstreams]
    means = [jnp.mean(part, -1, keepdims=True) for part in scaled]
    along = [jnp.mean(part * unit, -1, keepdims=True) for part, unit in zip(scaled, units)]
    return [
        inverse * (part - mean - unit * cross)
        for part, mean, cross, unit, inverse in zip(scaled, means, along, units, inverses)
    ]


def row_and_mlp_kernel(pieces, first, last, with_old, cot_at, info_ref, place_ref, *rest):
    afters, cots, rest = rest[:pieces], rest[pieces : 2 * pieces], rest[2 * pieces :]
    row_gain, row_shift, w_query_hbm, w_key_hbm, w_value_hbm = rest[:5]
    rest = rest[5:]
    w_row_hbm, row_bias, gain, shift, w_up_hbm, up_bias, w_down_hbm, down_bias = rest[:8]
    rest = rest[8:]
    if not first:
        (old_up, old_down, old_row, old_vec), rest = rest[:4], rest[4:]
    if with_old:
        old_layers, rest = rest[: pieces - 1], rest[pieces - 1 :]
    kept, rest = rest[:5], rest[5:]
    outs, (mixed_grad_ref, grad_ref, dots_ref), rest = rest[:pieces], rest[pieces : pieces + 3], rest[pieces + 3 :]
    if last:
        (keep_ref, send_ref), rest = rest[:2], rest[2:]
    else:
        (new_up, new_down, new_row, vec_ref), rest = rest[:4], rest[4:]
    q_ref, k_ref, v_ref, extra_ref, normed_ref, w_query, w_key, w_value = rest[:8]
    rest = rest[8:]
    after, cot, mixed, w_row, w_up, w_down, active_all, hidden_grad_all, up_sum, down_sum, row_sum, sems = rest[:12]
    if last:
        vec_ref = rest[12]
    _, rows, width = outs[0].shape
    full = rows * pieces
    wide = w_up.shape[1]
    spans = [slice(piece * rows, (piece + 1) * rows) for piece in range(pieces)]
    count = iter(range(32))

    def start(source, target):
        copy = pltpu.make_async_copy(source, target, sems.at[next(count)])
        copy.start()
        return copy

    get_after = [start(ref, after.at[pl.ds(piece * rows, rows), :]) for piece, ref in enumerate(afters)]
    get_row = [start(w_query_hbm, w_query), start(w_key_hbm, w_key), start(w_value_hbm, w_value)]
    get_out = [start(w_row_hbm, w_row)]
    get_up = [start(w_up_hbm, w_up)]
    get_down = [
        start(ref.at[cot_at[piece]], cot.at[pl.ds(piece * rows, rows), :]) for piece, ref in enumerate(cots)
    ]
    get_down.append(start(w_down_hbm, w_down))
    get_old = [] if first else [start(old_down, down_sum), start(old_up, up_sum), start(old_row, row_sum)]

    for copy in get_after:
        copy.wait()
    units, _ = units_of([after[span, :].astype(F32) for span in spans])
    normed = [(unit * row_gain[...] + row_shift[...]).astype(BF16) for unit in units]
    for copy in get_row:
        copy.wait()
    for weight, ref in ((w_query, q_ref), (w_key, k_ref), (w_value, v_ref)):
        for span, part in zip(spans, normed):
            ref[span, :] = dot_nn(part, weight[...]).astype(BF16)
    for span, part in zip(spans, normed):
        normed_ref[span, :] = part
    puts = [start(source, target) for source, target in zip((q_ref, k_ref, v_ref, normed_ref), kept)]
    lane = lane_of(rows)
    one_lane = jnp.where(lane == 0, 1.0, 0.0)
    query_low = one_lane.astype(BF16)
    biases = jnp.concatenate([key_extra(info_ref, piece, rows, 0) for piece in range(pieces)], 0)
    ones = jnp.ones((full, HEAD), BF16)
    tops = [jnp.zeros((rows, HEAD), F32) for _ in spans]
    totals = [jnp.ones((rows, HEAD), F32) for _ in spans]
    for head in range(HEADS):
        lanes = head_lanes(head)
        own = own_lanes(lane, 1, head)
        key, value = beside(k_ref[:, lanes], biases), beside(v_ref[:, lanes], ones)
        scores = [dot_nt(beside(q_ref[span, lanes], query_low), key) for span in spans]
        highest = [jnp.max(score, -1, keepdims=True) for score in scores]
        grown = [jnp.exp2((score - top) * SCALE).astype(BF16) for score, top in zip(scores, highest)]
        both = [dot_nn(grow, value) for grow in grown]
        for span, found in zip(spans, both):
            mixed[span, lanes] = (found[:, :HEAD] / found[:, HEAD:]).astype(BF16)
        tops = [jnp.where(own, top, old) for top, old in zip(highest, tops)]
        totals = [jnp.where(own, found[:, HEAD:], old) for found, old in zip(both, totals)]
    for span, top, total in zip(spans, tops, totals):
        extra_ref[span, :] = put_thirds(lane, 1, -(top + jnp.log2(total) * (1.0 / SCALE)), one_lane)
    puts.append(start(extra_ref, kept[4]))
    for copy in get_out:
        copy.wait()
    after_b = [
        after[span, :].astype(F32) + dot_nn(mixed[span, :], w_row[...]) + row_bias[...] for span in spans
    ]
    units, inverses = units_of(after_b)
    normed = [(unit * gain[...] + shift[...]).astype(BF16) for unit in units]
    normed_t = jnp.concatenate([part.T for part in normed], 1)
    for copy in get_up + get_down:
        copy.wait()
    keeps = [
        lax.broadcasted_iota(jnp.int32, (rows, 1), 0) + (info_ref[0] ^ piece) * rows < info_ref[1]
        for piece in range(pieces)
    ]
    grad_c = [jnp.where(keep, cot[span, :], jnp.zeros((), BF16)) for keep, span in zip(keeps, spans)]
    grad_t = jnp.concatenate([part.T for part in grad_c], 1)
    ones = jnp.ones((8, full), BF16)
    parts = [slice(at, at + CHUNK) for at in range(0, wide, CHUNK)]

    def widen(lanes):
        hiddens = [dot_nn(part, w_up[:, lanes]) + up_bias[:, lanes] for part in normed]
        return hiddens, [dot_nt(part, w_down[lanes, :]) for part in grad_c]

    c_one, c_three = math.sqrt(2.0 / math.pi), math.sqrt(2.0 / math.pi) * 0.044715
    ahead = widen(parts[0])
    bias_sums = []
    for index, lanes in enumerate(parts):
        hiddens, active_grads = ahead
        if index + 1 < len(parts):
            ahead = widen(parts[index + 1])
        for span, hidden, active_grad in zip(spans, hiddens, active_grads):
            square = hidden * hidden
            half = 0.5 + 0.5 * jnp.tanh(hidden * (c_one + c_three * square))
            active = hidden * half
            slope = half + active * (1.0 - half) * (2.0 * c_one + 6.0 * c_three * square)
            active_all[span, lanes] = active.astype(BF16)
            hidden_grad_all[span, lanes] = (active_grad * slope).astype(BF16)
        if index == 0:
            for copy in get_old:
                copy.wait()
        to_down = dot_nn(grad_t, active_all[:, lanes])
        to_up = dot_nn(normed_t, hidden_grad_all[:, lanes])
        down_sum[:, lanes] = to_down if first else down_sum[:, lanes] + to_down
        up_sum[:, lanes] = to_up if first else up_sum[:, lanes] + to_up
        bias_sums.append(dot_nn(ones, hidden_grad_all[:, lanes])[:1])
    if not last:
        puts += [start(down_sum, new_down), start(up_sum, new_up)]
    upstreams = [dot_nt(hidden_grad_all[span, :], w_up[...]) for span in spans]
    totals = [dot_nn(active_all[span, :], w_down[...]) for span in spans]
    backs = norms_back(upstreams, units, inverses, gain[...])
    grad_b = [part.astype(F32) + back for part, back in zip(grad_c, backs)]
    grad_low = [part.astype(BF16) for part in grad_b]
    if with_old:
        for out, ref in zip(outs[1:], old_layers):
            out[0] = ref[0]
    for out, total, base, keep in zip(outs, totals, after_b, keeps):
        out[out.shape[0] - 1] = jnp.where(keep, total + base + down_bias[...], 0.0).astype(BF16)
    mixed_grads = [dot_nt(part, w_row[...]).astype(BF16) for part in grad_low]
    to_row = dot_tn(mixed[...], jnp.concatenate(grad_low, 0))
    row_sum[...] = to_row if first else row_sum[...] + to_row
    if not last:
        puts.append(start(row_sum, new_row))
    picker = head_picker(1, width)
    for span, part, mixed_grad in zip(spans, grad_b, mixed_grads):
        grad_ref[span, :] = part
        mixed_grad_ref[span, :] = mixed_grad
    dots = [head_dots(part, mixed[span, :], picker) for part, span in zip(mixed_grads, spans)]
    for span, dot in zip(spans, dots):
        dots_ref[span, :] = put_thirds(lane, 1, -dot, jnp.zeros((), F32))
    sums = bias_sums + [
        dot_nn(ones, jnp.concatenate(grad_c, 0))[:1],
        sum(column_sum(upstream * unit) for upstream, unit in zip(upstreams, units)),
        sum(column_sum(upstream) for upstream in upstreams),
        sum(column_sum(part) for part in grad_b),
    ]
    sums = jnp.concatenate(sums, 0)
    vec_ref[...] = sums if first else old_vec[...] + sums
    if last:

        def fill(out, place, quarter, tab):
            start_row = pl.multiple_of(quarter * HEAD + tab * GROUP, GROUP)
            for index, lanes in enumerate(parts):
                out[place, index * GROUP : (index + 1) * GROUP, :] = up_sum[
                    pl.ds(start_row, GROUP), lanes
                ].astype(BF16)
            rows_of = pl.ds(pl.multiple_of(tab * DOWN_ROWS, GROUP), DOWN_ROWS)
            lanes = pl.ds(pl.multiple_of(quarter * CHUNK, CHUNK), CHUNK)
            out[place, UP_ROWS : UP_ROWS + DOWN_ROWS, :] = down_sum[rows_of, lanes].astype(BF16)
            at = UP_ROWS + DOWN_ROWS
            out[place, at : at + GROUP, :] = row_sum[pl.ds(start_row, GROUP), :].astype(BF16)
            out[place, at + GROUP : at + 2 * GROUP, :] = padded_vec(vec_ref)

        fill_batch(place_ref, keep_ref, send_ref, fill, y_first)
    for copy in puts:
        copy.wait()


def row_and_mlp(info, place, afters, cots, cot_at, row_weights, weights, last, old, old_layers, waits=()):
    rows, width = afters[0].shape
    pieces = len(afters)
    full = rows * pieces
    wide = weights[4].shape[1]
    first = old is None
    batch = (BATCH, UP_ROWS + DOWN_ROWS + 2 * GROUP, width)
    sums = [shape_of((width, wide), F32)] * 2 + [shape_of((width, width), F32), shape_of((8, width), F32)]
    weights = (*row_weights, *weights)
    weight_specs = [any_spec() if weight.shape[0] > 1 else vmem_spec() for weight in weights]
    return call(
        functools.partial(row_and_mlp_kernel, pieces, first, last, bool(old_layers), cot_at),
        (info, place, *afters, *cots, *weights, *([] if first else old), *old_layers,),
        waits,
        in_specs=[smem_spec()] * 2
        + [any_spec()] * (2 * pieces)
        + weight_specs
        + ([] if first else [any_spec()] * 3 + [vmem_spec()])
        + [vmem_spec()] * len(old_layers),
        out_specs=[any_spec()] * 5
        + [vmem_spec()] * (pieces + 3)
        + ([vmem_spec()] * 2 if last else [any_spec()] * 3 + [vmem_spec()]),
        out_shape=[shape_of((full, width))] * 4
        + [shape_of((full, HEAD))]
        + [shape_of((1 + (k > 0 and bool(old_layers)), rows, width)) for k in range(pieces)]
        + [shape_of((full, width)), shape_of((full, width), F32), shape_of((full, HEAD))]
        + ([shape_of(batch)] * 2 if last else sums),
        scratch_shapes=[pltpu.VMEM((full, width), BF16)] * 3
        + [pltpu.VMEM((full, HEAD), BF16), pltpu.VMEM((full, width), BF16)]
        + [pltpu.VMEM((width, width), BF16)] * 3
        + [
            pltpu.VMEM((full, width), BF16),
            pltpu.VMEM((full, width), BF16),
            pltpu.VMEM((full, width), BF16),
            pltpu.VMEM((width, width), BF16),
            pltpu.VMEM((width, wide), BF16),
            pltpu.VMEM((wide, width), BF16),
            pltpu.VMEM((full, wide), BF16),
            pltpu.VMEM((full, wide), BF16),
            pltpu.VMEM((width, wide), F32),
            pltpu.VMEM((width, wide), F32),
            pltpu.VMEM((width, width), F32),
            pltpu.SemaphoreType.DMA((32,)),
        ]
        + ([pltpu.VMEM((8, width), F32)] if last else []),
        cost_estimate=cost_of(28),
        name="row_and_mlp",
    )


BATCH = 16


def padded_vec(vec_ref):
    values = vec_ref[...]
    return jnp.concatenate([values, jnp.zeros_like(values)], 0).astype(BF16)


def y_first(x, y, z):
    return (y * 4 + z) * 2 + x


def x_first(x, y, z):
    return (x * 2 + y) * 4 + z


def fill_batch(place_ref, keep_ref, send_ref, fill, order):
    for core, out in ((0, keep_ref), (1, send_ref)):
        for y in range(2):
            for z in range(4):
                for x in range(2):
                    fill(out, order(x, y, z), place_ref[0] ^ (core + 2 * x), place_ref[1] ^ (y + 2 * z))


def row_swap(values, step):
    if step == 0:
        return values
    return lax.ppermute(values, "row", [(index, index ^ step) for index in range(4)])


def tab_swap(values, step):
    return lax.ppermute(values, "tab", [(index, index ^ step) for index in range(8)])


def add(*parts):
    total = parts[0].astype(F32)
    for part in parts[1:]:
        total = total + part.astype(F32)
    return total.astype(BF16)


def gather_near(own):
    return [own] + [tab_swap(own, 2 * z) for z in range(1, 4)]


def tie(first, second):
    return lax.optimization_barrier((first, second))


def finish_kernel(sizes, sources, place_ref, *rest):
    count = 1 + max(array for array, _ in sources)
    refs, outs = rest[:count], rest[count:]
    at = 0
    for (rows, columns, turned), out in zip(sizes, outs):
        parts = columns // 512
        for index, (array, place) in enumerate(sources):
            tab = place_ref[1] ^ (index // 4 + 2 * (index % 4))
            for part in range(parts):
                block = refs[array][place, at + part * rows : at + (part + 1) * rows, :].astype(F32)
                span = pl.ds(pl.multiple_of(tab * rows, GROUP), rows)
                out[span, part * 512 : (part + 1) * 512] = block
        at += rows * parts


def finish(place, arrays, sizes, waits=()):
    sources = tuple((index, at) for index, block in enumerate(arrays) for at in range(block.shape[0]))
    return call(
        functools.partial(finish_kernel, sizes, sources),
        (place, *arrays),
        waits,
        in_specs=[smem_spec()] + [vmem_spec()] * len(arrays),
        out_specs=[vmem_spec()] * len(sizes),
        out_shape=[shape_of((rows * 8, columns), F32) for rows, columns, _ in sizes],
        cost_estimate=cost_of(2),
        name="finish",
    )


def join_pieces_kernel(group, starts, me_ref, *rest):
    ins, out_ref = rest[:-1], rest[-1]
    for (piece, start), ref in zip(starts, ins):
        out_ref[pl.ds((me_ref[0] ^ piece) * group + start, ref.shape[0])] = ref[...]


def join_pieces(me, blocks, group, waits=()):
    _, rows, width = blocks[0][2].shape
    starts = tuple(block[:2] for block in blocks)
    return call(
        functools.partial(join_pieces_kernel, group, starts),
        (me, *(block[2] for block in blocks)),
        waits,
        in_specs=[smem_spec()] + [vmem_spec()] * len(blocks),
        out_specs=vmem_spec(),
        out_shape=shape_of((4 * group, rows, width)),
        cost_estimate=cost_of(2),
        name="join_pieces",
    )


def by_feature(
    table_cells,
    cotangent,
    row_counts,
    context_counts,
    feat_gain,
    feat_shift,
    feat_query,
    feat_key,
    feat_value,
    feat_out,
    feat_bias,
    row_gain,
    row_shift,
    row_query,
    row_key,
    row_value,
    row_out,
    row_bias,
    mlp_gain,
    mlp_shift,
    up_weight,
    up_bias,
    down_weight,
    down_bias,
):
    count = lax.axis_size("row")
    feats = table_cells.shape[2]
    group = feats // count
    me = lax.axis_index("row").astype(jnp.int32)
    own = me.reshape(1)
    place = jnp.stack([me, lax.axis_index("tab").astype(jnp.int32)])
    info = jnp.stack([me, row_counts[0], context_counts[0]])

    def flat(vector):
        return vector.reshape(1, -1)

    cells = table_cells[0].transpose(1, 0, 2)
    upstream = cotangent[0].transpose(1, 0, 2)
    feat_weights = (flat(feat_gain), flat(feat_shift), feat_query, feat_key, feat_value, feat_out)
    row_weight = (row_query, row_key, row_value)
    mlp_weights = (
        row_out,
        flat(row_bias),
        flat(mlp_gain),
        flat(mlp_shift),
        up_weight,
        flat(up_bias),
        down_weight,
        flat(down_bias),
    )
    far = split(own, upstream, group, ((2, 0, 1), (3, 0, 1)))
    cot_first = [row_swap(far[0], 2), row_swap(far[1], 3)]
    plan = ((0, 0, group), (1, 0, group)) + tuple((k, j, 1) for j in range(1, group) for k in (2, 3))
    forward = feat_forward(own, cells, upstream, (*feat_weights, flat(feat_bias)), group, plan, waits=(far[0],))
    after_out, kept_a = list(forward[:feats]), forward[feats : feats + 5]
    cot_own, cot_near, *cot_far = forward[feats + 5 :]
    leaving = [after_out[k * group] for k in range(1, count)]
    (leaving, cot_near), cot_first = tie((leaving, cot_near), cot_first)
    after_out[group :: group] = leaving
    cot_near = row_swap(cot_near, 1)
    first = [row_swap(after_out[k * group], k) for k in range(count)]
    leaving = [after_out[k * group + 1] for k in range(1, count)]
    leaving, first = tie(leaving, first)
    after_out[group + 1 :: group] = leaving
    afters, own_layers, kept_b, backs, mlp_sums, old_layers, late = [], [], [], [], None, [], []
    for j in range(group):
        afters.append(first if j == 0 else [row_swap(after_out[k * group + j], k) for k in range(count)])
        cot = cot_first if j == 0 else [row_swap(cot_far[2 * j - 2], 2), row_swap(cot_far[2 * j - 1], 3)]
        found = row_and_mlp(
            info,
            place,
            afters[j],
            [cot_own, cot_near, *cot],
            (j, j, 0, 0),
            (flat(row_gain), flat(row_shift), *row_weight),
            mlp_weights,
            j == group - 1,
            mlp_sums,
            old_layers,
        )
        kept_b.append(found[:5])
        layer = found[5 : 5 + count]
        own_layers.append(layer[0])
        old_layers = layer[1:] if j == 0 else []
        if j > 0:
            early, late = late, [row_swap(layer[k], k) for k in range(1, count)]
        backs.append(found[5 + count : 8 + count])
        mlp_sums = found[8 + count :]
    mlp_keep, send = mlp_sums
    send, early = tie(send, early)
    mlp_came = row_swap(send, 1)
    mlp_line = tab_swap(add(mlp_keep[8:], mlp_came[8:]), 1)
    grads, d_rows, vecs = [], [], []
    for j in range(group):
        query, key, value, _, extra = kept_b[j]
        if j == 0:
            waits = [backs[-1][2]]
        elif j == 1:
            waits = [vecs[-1], *late]
        else:
            parts = [
                add(*(ref[2 * z : 2 * z + 2] for ref in (mlp_keep, mlp_came, mlp_line))) for z in range(4)
            ]
            waits = [vecs[-1], *grads[0][2:], parts[0]]
        found = row_backward(
            info, (query, key, value, extra), backs[j], afters[j], (flat(row_gain), *row_weight), waits
        )
        d_rows += found[count : count + 3]
        vecs.append(found[count + 3])
        grads.append([row_swap(found[k], k) for k in range(count)])
    parts[1:] = [tab_swap(parts[z], 2 * z) for z in range(1, 4)]
    row_keep, send = row_weights(place, [kept[3] for kept in kept_b], d_rows, vecs, grads[1][2:])
    away = add(*(part[1] for part in parts))
    (away, send), grads[2][1:] = tie((away, send), grads[2][1:])
    row_came = row_swap(send, 1)
    mlp_line = row_swap(away, 2)
    row_away = add(row_keep[8:], row_came[8:])
    row_line = row_swap(row_away, 2)
    mlp_parts = parts
    grad_back = [grads[j][k] for k in range(count) for j in range(group)]

    keep, send, *d_all = feat_backward(place, cells, kept_a, grad_back, feat_weights, group, waits=(row_away,))
    send, (row_line, mlp_line) = tie(send, (row_line, mlp_line))
    came = row_swap(send, 1)
    mlp_own = add(*(part[0] for part in mlp_parts), mlp_line)
    mlp_near = gather_near(mlp_own[:-GROUP])
    row_turned = tab_swap(add(row_keep[4:8], row_came[4:8], row_line[4:8]), 1)
    away = add(keep[8:], came[8:])
    cells_grad, mark = cells_backward(
        own, cells, d_all, (flat(feat_gain), feat_query, feat_key, feat_value), grad_back, group, waits=(away,)
    )
    line, mark = tie(row_swap(away, 2), mark)
    away = add(keep[4:8], came[4:8], line[4:8])
    away, (row_turned, mlp_near) = tie(away, (row_turned, mlp_near))
    turned = tab_swap(away, 1)
    parts = [add(*(ref[z] for ref in (row_keep, row_came, row_line, row_turned))) for z in range(4)]
    row_parts = [parts[0]] + [tab_swap(parts[z], 2 * z) for z in range(1, 4)]
    parts = [add(*(ref[z] for ref in (keep, came, line, turned))) for z in range(4)]
    parts, mlp_near = tie(parts, mlp_near)
    mlp_near = jnp.stack(mlp_near)
    mlp_far = tab_swap(mlp_near, 1)
    parts[1:] = [tab_swap(parts[z], 2 * z) for z in range(1, 4)]
    parts, row_parts = tie(parts, row_parts)
    row_own, feat_own = add(*row_parts), add(*parts)
    own_piece, *others = gather_near(jnp.concatenate([row_own[:-GROUP], feat_own[:-GROUP]], 0))
    far_own = tab_swap(own_piece, 1)
    others = jnp.stack(others)
    back = (own_piece[None], others, far_own[None], tab_swap(others, 1))
    mlp_vec, row_vec, feat_vec = mlp_own[-GROUP:], row_own[-GROUP:], feat_own[-GROUP:]
    blocks = [(0, j, part) for j, part in enumerate(own_layers)]
    blocks += [(k, 0, part) for k, part in enumerate(early, 1)]
    blocks += [(k, group - 1, part) for k, part in enumerate(late, 1)]
    layer_out = join_pieces(own, blocks, group, (feat_own,))

    up_sum, down_sum, row_out_sum = finish(
        place,
        (mlp_near, mlp_far),
        ((GROUP, 2048, False), (4 * GROUP, 512, True), (GROUP, 512, False)),
        (feat_own,),
    )
    small = ((GROUP, 512, False),) * 7
    sum_rq, sum_rk, sum_rv, sum_fq, sum_fk, sum_fv, sum_fo = finish(place, back, small, (mark, row_out_sum))

    mlp_vec, row_vec, feat_vec = (part.astype(F32) for part in (mlp_vec, row_vec, feat_vec))
    rows = sum_fq.shape[0]

    def quarter(vector):
        return lax.dynamic_slice_in_dim(vector, me * rows, rows, 0)

    return (
        layer_out.transpose(1, 0, 2)[None],
        cells_grad.transpose(1, 0, 2)[None],
        quarter(feat_vec[0]),
        quarter(feat_vec[1]),
        sum_fq,
        sum_fk,
        sum_fv,
        sum_fo,
        quarter(row_vec[2]),
        quarter(row_vec[0]),
        quarter(row_vec[1]),
        sum_rq,
        sum_rk,
        sum_rv,
        row_out_sum,
        quarter(mlp_vec[7]),
        quarter(mlp_vec[5]),
        quarter(mlp_vec[6]),
        up_sum,
        lax.dynamic_index_in_dim(mlp_vec[:4], me, 0, keepdims=False),
        down_sum.T,
        quarter(mlp_vec[4]),
    )


def solution(mesh):
    in_specs = (
        P("tab", "row", None, None),
        P("tab", "row", None, None),
        P("tab"),
        P("tab"),
        P(),
        P(),
        P(),
        P(),
        P(),
        P(),
        P(),
        P(),
        P(),
        P(),
        P(),
        P(),
        P(),
        P(),
        P(),
        P(),
        P(),
        P(),
        P(),
        P(),
    )
    out_specs = (
        P("tab", "row", None, None),
        P("tab", "row", None, None),
        P("row"),
        P("row"),
        P("row", None),
        P("row", None),
        P("row", None),
        P("row", None),
        P("row"),
        P("row"),
        P("row"),
        P("row", None),
        P("row", None),
        P("row", None),
        P("row", None),
        P("row"),
        P("row"),
        P("row"),
        P("row", None),
        P("row"),
        P("row", None),
        P("row"),
    )

    near = (mesh.shape["tab"], mesh.shape["row"]) == (8, 4)
    body = by_feature if near else shards
    return jax.shard_map(body, mesh=mesh, in_specs=in_specs, out_specs=out_specs, check_vma=False)
```
